32 devices in a mesh: ctx: 8 (over y, x, core), fsdp: 4 (over z).
Axes of the slice: x: 2, y: 2, z: 4, core: 2. Of those that a mesh axis runs over, the one named last changes fastest.
Arguments:
- inputs: bfloat16 [8, 1024, 1536], P('fsdp', 'ctx'), may hold values from -6 to 6
- gain_attn: bfloat16 [1536], P('fsdp'), may hold values from 0.5 to 1.5
- w_query: bfloat16 [1536, 1536], P('fsdp'), may hold values from -0.15625 to 0.15625
- w_key: bfloat16 [1536, 1536], P('fsdp'), may hold values from -0.15625 to 0.15625
- w_value: bfloat16 [1536, 1536], P('fsdp'), may hold values from -0.15625 to 0.15625
- w_forget: bfloat16 [1536, 24], P('fsdp'), may hold values from -0.15625 to 0.15625
- forget_bias: bfloat16 [24], P('fsdp'), may hold values from 3 to 8
- w_out: bfloat16 [1536, 1536], P('fsdp'), may hold values from -1.25 to 1.25
- gain_mlp: bfloat16 [1536], P('fsdp'), may hold values from 0.5 to 1.5
- w_gate: bfloat16 [1536, 4096], P('fsdp'), may hold values from -0.15625 to 0.15625
- w_up: bfloat16 [1536, 4096], P('fsdp'), may hold values from -0.15625 to 0.15625
- w_down: bfloat16 [4096, 1536], P('fsdp'), may hold values from -0.09375 to 0.09375
- cotangent: bfloat16 [8, 1024, 1536], P('fsdp', 'ctx'), may hold values from -6 to 6
Outputs:
- output: bfloat16 [8, 1024, 1536], P('fsdp', 'ctx')
- input_grad: float32 [8, 1024, 1536], P('fsdp', 'ctx')
- grad_gain_attn: float32 [1536], P('fsdp')
- grad_query: float32 [1536, 1536], P('fsdp')
- grad_key: float32 [1536, 1536], P('fsdp')
- grad_value: float32 [1536, 1536], P('fsdp')
- grad_forget: float32 [1536, 24], P('fsdp')
- grad_forget_bias: float32 [24], P('fsdp')
- grad_out: float32 [1536, 1536], P('fsdp')
- grad_gain_mlp: float32 [1536], P('fsdp')
- grad_gate: float32 [1536, 4096], P('fsdp')
- grad_up: float32 [1536, 4096], P('fsdp')
- grad_down: float32 [4096, 1536], P('fsdp')
The draws below stay inside these ranges and needn't reach their ends.
All inputs are finite; a program needn't handle non-finite values.
Results may differ from the reference program's by a relative error of at most 0.01615.
The reference program's roundings to bfloat16 on the way count: a program that leaves them out, or rounds other values in their place, can miss the bound.
Values may be sent and summed in bfloat16 or wider, within the bound.
No kernel may reach another device: no remote copies, remote signals or barrier semaphores. Data moves between devices by JAX's collectives and lax.ppermute only.
A program may use at most 256 MiB of HBM per device.

```python
import math
import jax
import jax.numpy as jnp
from jax import lax

D = 1536
HEADS = 24
HEAD_DIM = 64
FF = 4096
BLK = 256
LENGTH = 1024
SEQS = 8


def steps_of(stream_key, shape, shards, least, largest):
    factor_of = 1.0
    for axis_at, parts in shards:
        draws = jax.random.uniform(jax.random.fold_in(jax.random.fold_in(stream_key, 6), axis_at), (parts,), jnp.float32, least / len(shards), largest / len(shards))
        factor_of = factor_of * jnp.repeat(jnp.exp(draws), shape[axis_at] // parts).reshape((-1,) + (1,) * (len(shape) - 1 - axis_at))
    return factor_of


def normal_values(own_key, extent, scale, bound, split=(), held_as=jnp.bfloat16):
    entries = scale * jax.random.normal(own_key, extent, jnp.float32)
    if split:
        entries = entries * steps_of(own_key, extent, split, -0.22, 0.18)
    return jnp.clip(entries, -bound, bound).astype(held_as)


def setup_inputs(seed: int = 0) -> dict:
    seeds = jax.random.split(jax.random.key(seed), 14)
    inputs = normal_values(seeds[0], (SEQS, LENGTH, D), 1.0, 6.0, ((0, 4), (1, 8)))
    gain_attn = jnp.clip(1.0 + 0.1 * jax.random.normal(seeds[1], (D,), jnp.float32), 0.5, 1.5).astype(jnp.bfloat16)
    w_query = normal_values(seeds[2], (D, D), D ** -0.5, 0.15625, ((0, 4),))
    w_key = normal_values(seeds[3], (D, D), D ** -0.5, 0.15625, ((0, 4),))
    w_value = normal_values(seeds[4], (D, D), D ** -0.5, 0.15625, ((0, 4),))
    w_forget = normal_values(seeds[5], (D, HEADS), D ** -0.5, 0.15625, ((0, 4),))
    forget_bias = jnp.clip(3.0 + 5.0 * jax.random.uniform(seeds[6], (HEADS,), jnp.float32) ** steps_of(seeds[6], (HEADS,), ((0, 4),), -0.2, 0.2), 3.0, 8.0).astype(jnp.bfloat16)
    w_out = normal_values(seeds[7], (D, D), (D // 64) ** -0.5, 1.25, ((0, 4),))
    gain_mlp = jnp.clip(1.0 + 0.1 * jax.random.normal(seeds[8], (D,), jnp.float32), 0.5, 1.5).astype(jnp.bfloat16)
    w_gate = normal_values(seeds[9], (D, FF), D ** -0.5, 0.15625, ((0, 4),))
    w_up = normal_values(seeds[10], (D, FF), D ** -0.5, 0.15625, ((0, 4),))
    w_down = normal_values(seeds[11], (FF, D), FF ** -0.5, 0.09375, ((0, 4),))
    cotangent = normal_values(seeds[12], (SEQS, LENGTH, D), 1.0, 6.0, ((0, 4), (1, 8)))
    return dict(inputs=inputs, gain_attn=gain_attn, w_query=w_query, w_key=w_key, w_value=w_value, w_forget=w_forget, forget_bias=forget_bias, w_out=w_out, gain_mlp=gain_mlp, w_gate=w_gate, w_up=w_up, w_down=w_down, cotangent=cotangent)


@jax.custom_vjp
def low(v):
    return lax.optimization_barrier(v.astype(jnp.bfloat16)).astype(jnp.float32)

@jax.custom_vjp
def low_back(v):
    return v

def low_keep(v):
    return (low(v), None)

def low_pass(kept, grad):
    return (grad,)

def back_keep(v):
    return (v, None)

def back_low(kept, grad):
    return (low(grad),)
low.defvjp(low_keep, low_pass)
low_back.defvjp(back_keep, back_low)
norm_eps = 1e-06
highest = lax.Precision.HIGHEST

def rms_norm(values, gain):
    return values * lax.rsqrt(lax.optimization_barrier(jnp.mean(values * values, axis=-1, keepdims=True)) + norm_eps) * gain

def matmul(left, right):
    return jnp.dot(left, right, precision=highest)

def attend_rows(pos_query, queries, decay_query, keys_all, values_all, decay_all):
    key_pos = jnp.arange(LENGTH, dtype=jnp.int32)
    raw_dots = jnp.einsum('qhd,khd->hqk', queries, keys_all, precision=highest)
    visible = key_pos[None, :] // BLK <= pos_query[:, None] // BLK
    signed = jnp.where(key_pos[None, :] <= pos_query[:, None], 1.0, -1.0)
    offsets = signed[None] * (decay_query.T[:, :, None] - decay_all.T[:, None, :])
    scores = low_back(raw_dots * (1.0 / math.sqrt(HEAD_DIM)) + offsets)
    exp_terms = jnp.where(visible[None], jnp.exp(scores), 0.0)
    summed = low_back(jnp.einsum('hqk,khd->qhd', low(exp_terms), values_all, precision=highest))
    totals = lax.optimization_barrier(jnp.sum(exp_terms, axis=2))
    return summed / totals.T[:, :, None]

def attend_sequence(operands):
    queries, keys_all, values_all, decay_all = operands
    block_rows = math.gcd(LENGTH, 512)
    number = LENGTH // block_rows
    positions = jnp.arange(LENGTH, dtype=jnp.int32).reshape(number, block_rows)
    checked = jax.checkpoint(attend_rows)

    def one_block(block_in):
        pos_query, query_blk, decay_blk = block_in
        return checked(pos_query, query_blk, decay_blk, keys_all, values_all, decay_all)
    result = lax.map(one_block, (positions, queries.reshape(number, block_rows, HEADS, HEAD_DIM), decay_all.reshape(number, block_rows, HEADS)))
    return result.reshape(LENGTH, HEADS, HEAD_DIM)

def layer(inputs, gain_attn, w_query, w_key, w_value, w_forget, forget_bias, w_out, gain_mlp, w_gate, w_up, w_down):
    flat_in = inputs.reshape(SEQS * LENGTH, D)
    normed = low(rms_norm(flat_in, gain_attn))
    queries = low_back(low(matmul(normed, w_query)))
    keys = low_back(low(matmul(normed, w_key)))
    values = low_back(low(matmul(normed, w_value)))
    gate_raw = low_back(matmul(normed, w_forget) + forget_bias)
    decay = jnp.cumsum(jax.nn.log_sigmoid(gate_raw).reshape(SEQS, LENGTH, HEADS), axis=1)
    head_shape = (SEQS, LENGTH, HEADS, HEAD_DIM)
    attn = lax.map(attend_sequence, (queries.reshape(head_shape), keys.reshape(head_shape), values.reshape(head_shape), decay))
    mixed = low(attn.reshape(SEQS * LENGTH, D))
    hidden_state = flat_in + low_back(matmul(mixed, w_out))
    normed_two = low(rms_norm(hidden_state, gain_mlp))
    gate_val = low_back(matmul(normed_two, w_gate))
    up_val = low_back(matmul(normed_two, w_up))
    inner = low(jax.nn.silu(gate_val) * up_val)
    result = hidden_state + low_back(matmul(inner, w_down))
    return result.reshape(SEQS, LENGTH, D)

def reference(inputs, gain_attn, w_query, w_key, w_value, w_forget, forget_bias, w_out, gain_mlp, w_gate, w_up, w_down, cotangent):
    floats = tuple((argument.astype(jnp.float32) for argument in (inputs, gain_attn, w_query, w_key, w_value, w_forget, forget_bias, w_out, gain_mlp, w_gate, w_up, w_down)))
    result, pullback = jax.vjp(layer, *floats)
    grads = pullback(cotangent.astype(jnp.float32))
    return (result.astype(jnp.bfloat16), grads[0], grads[1], grads[2], grads[3], grads[4], grads[5], grads[6], grads[7], grads[8], grads[9], grads[10], grads[11])
```

```python
import jax
import jax.numpy as jnp
from jax import lax
from jax.experimental import pallas as pl
from jax.experimental.pallas import tpu as pltpu
from jax.sharding import PartitionSpec as P

HEADS = 24
HEAD_DIM = 64
BLK = 256
EXTRA = 64
norm_eps = 1e-06
bf16 = jnp.bfloat16
f32 = jnp.float32


def exchange(x, axis, mask):
    return lax.ppermute(x, axis, [(i, i ^ mask) for i in range(lax.axis_size(axis))])


def after(x, done):
    return lax.optimization_barrier((x, done))[0]


def first_half(rows):
    return -(-rows // 32) * 16


def gather_start(x, axis):
    return x, exchange(x, axis, 2), exchange(x, axis, 4)


def gather_far(state, axis):
    x, side, above = state
    half = first_half(x.shape[0])
    return x, side, above, exchange(side[:half], axis, 4), exchange(above[half:], axis, 2)


def gather_core(state, axis):
    size = state[0].shape[0]
    half = first_half(size)
    places = ((0, 0, size), (2, 0, size), (4, 0, size), (6, 0, half), (6, half, size - half))
    pieces = [place + (array,) for place, array in zip(places, state)]
    return pieces + [(mask ^ 1, start, rows, exchange(a, axis, 1)) for mask, start, rows, a in pieces]


def arrays_of(pieces):
    return [piece[3] for piece in pieces]


ANY = pl.BlockSpec(memory_space=pl.ANY)
LIMIT = pltpu.CompilerParams(vmem_limit_bytes=48 * 2**20)


def takes(us):
    return pl.CostEstimate(flops=int(us * 1.15e9), bytes_accessed=int(us * 1e5), transcendentals=0)


LARGE = pltpu.CompilerParams(vmem_limit_bytes=60 * 2**20)
SMALL = pltpu.CompilerParams(vmem_limit_bytes=24 * 2**20)


def copy_all(copies, sems):
    started = [pltpu.make_async_copy(source, target, sems.at[i]) for i, (source, target) in enumerate(copies)]
    for copy in started:
        copy.start()
    for copy in started:
        copy.wait()


def rows_at(ref, start, size):
    return ref.at[pl.ds(start if isinstance(start, int) else pl.multiple_of(start, 16), size)]


def slices_of(pieces, me, slots):
    copies = []
    for k, (mask, first, size, _) in enumerate(pieces):
        for start, rows, target in slots(me ^ mask):
            low, high = max(start, first), min(start + rows, first + size)
            if low < high:
                copies.append((k, low - first, high - low, target + (low - start)))
    return copies


def place(pieces, axis, total, slots):
    arrays = [p[3] for p in pieces]
    width, dtype = arrays[0].shape[1], arrays[0].dtype
    me = lax.axis_index(axis).reshape(1)

    def kernel(me, *refs):
        out, sems = refs[-2:]
        copies = slices_of(pieces, me[0], slots)
        copy_all([(refs[k].at[pl.ds(s, size)], rows_at(out, t, size)) for k, s, size, t in copies], sems)

    return pl.pallas_call(
        kernel,
        in_specs=[pl.BlockSpec(memory_space=pltpu.SMEM)] + [ANY] * len(arrays),
        out_specs=pl.BlockSpec(memory_space=pltpu.VMEM),
        out_shape=jax.ShapeDtypeStruct((total, width), dtype),
        scratch_shapes=[pltpu.SemaphoreType.DMA((len(slices_of(pieces, 0, slots)),))],
        compiler_params=LIMIT,
        cost_estimate=takes(5.0),
    )(me, *arrays)


def add_first(keep, moved, half):
    rows, width = keep.shape[1:]

    def kernel(keep_one, moved_one, keep_two, moved_two, kept, sent):
        kept[...] = keep_one[...].astype(f32) + moved_one[...].astype(f32)
        sent[...] = (keep_two[...].astype(f32) + moved_two[...].astype(f32)).astype(bf16)

    def block(at):
        return pl.BlockSpec((1, rows, width), lambda g: (at(g), 0, 0))

    one, two = (block(lambda g: g), block(lambda g: g + 2)) if half % 2 else (block(lambda g: 2 * g), block(lambda g: 2 * g + 1))
    return pl.pallas_call(
        kernel,
        grid=(2,),
        in_specs=[one, one, two, two],
        out_specs=[block(lambda g: g)] * 2,
        out_shape=[jax.ShapeDtypeStruct((2, rows, width), f32), jax.ShapeDtypeStruct((2, rows, width), bf16)],
        compiler_params=SMALL,
        cost_estimate=takes(2.0),
    )(keep, moved, keep, moved)


def add_second(kept, moved):
    rows, width = kept.shape[1:]
    part = rows // 4

    def kernel(kept, moved, own, sent):
        own[...] = kept[0] + moved[0].astype(f32)
        sent[...] = (kept[1] + moved[1].astype(f32)).astype(bf16)

    both = pl.BlockSpec((2, part, width), lambda g: (0, g, 0))
    one = pl.BlockSpec((part, width), lambda g: (g, 0))
    return pl.pallas_call(
        kernel,
        grid=(rows // part,),
        in_specs=[both, both],
        out_specs=[one, one],
        out_shape=[jax.ShapeDtypeStruct((rows, width), f32), jax.ShapeDtypeStruct((rows, width), bf16)],
        compiler_params=SMALL,
        cost_estimate=takes(2.0),
    )(kept, moved)


class Sums:
    def __init__(self, pairs, axis):
        self.axis = axis
        self.kept = [keep for keep, _ in pairs]
        self.moving = [exchange(send, axis, 1) for _, send in pairs]

    def hold(self, others):
        self.moving, others = lax.optimization_barrier((self.moving, others))
        return others

    def first(self):
        added = [add_first(k, m, h) for h, (k, m) in enumerate(zip(self.kept, self.moving))]
        self.kept, self.moving = [a[0] for a in added], [a[1] for a in added]

    def send_first(self):
        self.moving = [exchange(m, self.axis, (2, 4)[h % 2]) for h, m in enumerate(self.moving)]

    def second(self):
        added = [add_second(k, m) for k, m in zip(self.kept, self.moving)]
        self.kept, self.moving = [a[0] for a in added], [a[1] for a in added]

    def send_second(self):
        self.moving = [exchange(m, self.axis, (4, 2)[h % 2]) for h, m in enumerate(self.moving)]

    def result(self):
        return jnp.concatenate([k + m.astype(f32) for k, m in zip(self.kept, self.moving)], axis=0)


def each(count, body, carry):
    if count <= 3:
        for j in range(count):
            carry = body(j, carry)
        return carry
    return lax.fori_loop(0, count, body, carry)


def span(j):
    return pl.ds(j * BLK if isinstance(j, int) else pl.multiple_of(j * BLK, BLK), BLK)


def dot(a, b):
    return jnp.dot(a, b, preferred_element_type=f32)


def dot_t(a, b):
    return lax.dot_general(a, b, (((1,), (1,)), ((), ())), preferred_element_type=f32)


def running_sum(rows, backward):
    length = rows.shape[1]
    lane = lax.broadcasted_iota(jnp.int32, rows.shape, 1)
    step = 1
    while step < length:
        moved = pltpu.roll(rows, length - step if backward else step, 1)
        inside = lane < length - step if backward else lane >= step
        rows = rows + jnp.where(inside, moved, 0.0)
        step *= 2
    return rows


def log_sigmoid(x):
    return jnp.minimum(x, 0.0) - jnp.log1p(jnp.exp(-jnp.abs(x)))


def head_rows(h, part=0):
    return slice(part + h * HEAD_DIM, part + (h + 1) * HEAD_DIM)


def attend(qkv, gate_raw, seqs, heads):
    length, cols = qkv.shape[1] // seqs, heads * HEAD_DIM
    lines = gate_raw.shape[0]

    def kernel(qkv_ref, raw_ref, attn_ref, mixed_ref, total_ref, decay_ref, k_rows, decay_cols):
        decay = running_sum(log_sigmoid(raw_ref[...]), False)
        decay_ref[...] = decay
        decay_cols[...] = decay.T
        total_ref[...] = jnp.ones_like(total_ref)
        for h in range(heads):
            k_rows[h] = qkv_ref[head_rows(h, cols), :].T

        for i in range(length // BLK):
            for h in range(heads):
                at = span(i)
                query = qkv_ref[head_rows(h), at] * 0.125
                decay_q = decay_ref[h : h + 1, at]

                def visit(j, carry):
                    summed, total = carry
                    offset = decay_q - decay_cols[span(j), h : h + 1]
                    if isinstance(j, int) and j == i:
                        offset = -jnp.abs(offset)
                    terms = jnp.exp(dot(k_rows[h, span(j), :], query) + offset)
                    total = total + jnp.sum(terms, axis=0, keepdims=True)
                    return summed + dot(qkv_ref[head_rows(h, 2 * cols), span(j)], terms.astype(bf16)), total

                start = (jnp.zeros((HEAD_DIM, BLK), f32), jnp.zeros((1, BLK), f32))
                summed, total = visit(i, each(i, visit, start))
                attn = summed / total
                attn_ref[head_rows(h), at] = attn
                mixed_ref[head_rows(h), at] = attn.astype(bf16)
                total_ref[h : h + 1, at] = total

    def block(rows):
        return pl.BlockSpec((rows, length), lambda s: (0, s))

    tokens = seqs * length
    return pl.pallas_call(
        kernel,
        grid=(seqs,),
        in_specs=[block(3 * cols), block(lines)],
        out_specs=[block(cols), block(cols), block(lines), block(lines)],
        out_shape=[
            jax.ShapeDtypeStruct((cols, tokens), f32),
            jax.ShapeDtypeStruct((cols, tokens), bf16),
            jax.ShapeDtypeStruct((lines, tokens), f32),
            jax.ShapeDtypeStruct((lines, tokens), f32),
        ],
        scratch_shapes=[pltpu.VMEM((heads, length, HEAD_DIM), bf16), pltpu.VMEM((length, lines), f32)],
        compiler_params=SMALL,
        cost_estimate=takes(9.0),
    )(qkv, gate_raw)


def attend_pull(qkv, decay, grad_mixed, attn, totals, gate_raw, seqs, heads):
    length, cols = qkv.shape[1] // seqs, heads * HEAD_DIM
    lines = gate_raw.shape[0]
    pieces = grad_mixed.shape[0]
    piece = length // pieces
    deep = HEAD_DIM + 16

    def kernel(
        qkv_ref, decay_ref, gm_ref, attn_ref, total_ref, raw_ref, gq_ref, gk_ref, gv_ref, graw_ref,
        k_rows, v_rows, decay_cols, q_more, k_more, gs_all, delta_all, gk_sum, gv_sum, gd_all,
    ):
        decay_cols[...] = decay_ref[...].T
        gd_all[...] = jnp.zeros_like(gd_all)
        gk_sum[...] = jnp.zeros_like(gk_sum)
        gv_sum[...] = jnp.zeros_like(gv_sum)
        more = (lax.broadcasted_iota(jnp.int32, (16, length), 0) == 0).astype(bf16)
        for h in range(heads):
            k_rows[h] = qkv_ref[head_rows(h, cols), :].T
            v_rows[h] = qkv_ref[head_rows(h, 2 * cols), :].T
            k_more[h, :HEAD_DIM, :] = qkv_ref[head_rows(h, cols), :]
            k_more[h, HEAD_DIM:, :] = more
            q_more[h, :HEAD_DIM, :] = qkv_ref[head_rows(h), :] * 0.125
            q_more[h, HEAD_DIM:, :] = more
            for p in range(pieces):
                at = slice(p * piece, (p + 1) * piece)
                grad = gm_ref[p, head_rows(h), :].astype(f32)
                total = total_ref[h : h + 1, at]
                gs_all[head_rows(h), at] = (grad / total).astype(bf16)
                delta_all[h : h + 1, at] = jnp.sum(grad * attn_ref[head_rows(h), at], axis=0, keepdims=True) / total

        key_first = lax.broadcasted_iota(jnp.int32, (BLK, BLK), 0) <= lax.broadcasted_iota(
            jnp.int32, (BLK, BLK), 1
        )
        ones = (lax.broadcasted_iota(jnp.int32, (16, BLK), 0) == 0).astype(bf16)

        for i in range(length // BLK):
            for h in range(heads):
                at = span(i)
                query = q_more[h, :HEAD_DIM, at]
                decay_q = decay_ref[h : h + 1, at]
                gs = gs_all[head_rows(h), at]
                delta = delta_all[h : h + 1, at]

                def terms_of(j, last):
                    offset = decay_q - decay_cols[span(j), h : h + 1]
                    if last:
                        offset = -jnp.abs(offset)
                    terms = jnp.exp(dot(k_rows[h, span(j), :], query) + offset)
                    grads = (terms * (dot(v_rows[h, span(j), :], gs) - delta)).astype(bf16)
                    gv_sum[head_rows(h), span(j)] += dot_t(gs, terms.astype(bf16))
                    return grads

                def visit(j, carry):
                    grads = terms_of(j, False)
                    gk_sum[h, :, span(j)] += dot_t(q_more[h, :, at], grads)
                    return carry + dot(k_more[h, :, span(j)], grads)

                gq = each(i, visit, jnp.zeros((deep, BLK), f32))
                grads = terms_of(i, True)
                gk_sum[h, :HEAD_DIM, at] += dot_t(query, grads)
                gq_own = gq[:HEAD_DIM] + dot(k_more[h, :HEAD_DIM, at], grads)
                signed = jnp.where(key_first, grads, -grads)
                gk_sum[h, HEAD_DIM:, at] += dot_t(ones, signed)
                gd_all[h : h + 1, at] = (gq[HEAD_DIM:] + dot(ones, signed))[:1]
                gq_ref[head_rows(h), at] = (gq_own * 0.125).astype(bf16)

        for h in range(heads):
            gk_ref[head_rows(h), :] = gk_sum[h, :HEAD_DIM, :].astype(bf16)
            gd_all[h : h + 1, :] = gd_all[h : h + 1, :] - gk_sum[h, HEAD_DIM : HEAD_DIM + 1, :]
        gv_ref[...] = gv_sum[...].astype(bf16)
        grad_log = running_sum(gd_all[...], True)
        graw_ref[...] = (grad_log * jax.nn.sigmoid(-raw_ref[...])).astype(bf16).astype(f32)

    def block(rows):
        return pl.BlockSpec((rows, length), lambda s: (0, s))

    tokens = seqs * length
    shape = jax.ShapeDtypeStruct((cols, tokens), bf16)
    return pl.pallas_call(
        kernel,
        grid=(seqs,),
        in_specs=[
            block(3 * cols),
            block(lines),
            pl.BlockSpec((pieces, cols, piece), lambda s: (0, 0, s)),
            block(cols),
            block(lines),
            block(lines),
        ],
        out_specs=[block(cols), block(cols), block(cols), block(lines)],
        out_shape=[shape, shape, shape, jax.ShapeDtypeStruct((lines, tokens), f32)],
        scratch_shapes=[
            pltpu.VMEM((heads, length, HEAD_DIM), bf16),
            pltpu.VMEM((heads, length, HEAD_DIM), bf16),
            pltpu.VMEM((length, lines), f32),
            pltpu.VMEM((heads, deep, length), bf16),
            pltpu.VMEM((heads, deep, length), bf16),
            pltpu.VMEM((cols, length), bf16),
            pltpu.VMEM((lines, length), f32),
            pltpu.VMEM((heads, deep, length), f32),
            pltpu.VMEM((cols, length), f32),
            pltpu.VMEM((lines, length), f32),
        ],
        compiler_params=SMALL,
        cost_estimate=takes(19.0),
    )(qkv, decay, grad_mixed, attn, totals, gate_raw)


def inverse_rms(rows):
    return lax.rsqrt(jnp.mean(rows * rows, axis=-1, keepdims=True) + norm_eps)


def norm_pull(rows, gain, grad):
    scale = inverse_rms(rows)
    weighted = grad * gain
    inner = jnp.mean(rows * weighted, axis=-1, keepdims=True)
    return scale * weighted - rows * (scale * scale * scale * inner), jnp.sum(grad * rows * scale, axis=0)


def place_columns(pieces, axis, parts, both):
    arrays = [p[3] for p in pieces]
    rows, width = arrays[0].shape
    count = 8
    me = lax.axis_index(axis).reshape(1)

    def slots(dev):
        return [(0, rows, dev * rows)]

    def kernel(me, *refs):
        outs, (held, sems) = refs[len(arrays) : -2], refs[-2:]

        @pl.when(pl.program_id(0) == 0)
        def _():
            copies = slices_of(pieces, me[0], slots)
            copy_all([(refs[k].at[pl.ds(s, size)], rows_at(held, t, size)) for k, s, size, t in copies], sems)

        for b, out in enumerate(outs):
            at = pl.multiple_of((b * parts + pl.program_id(0)) * 128, 128)
            for dev in range(count):
                out[:, dev * 128 : (dev + 1) * 128] = held[dev * rows : (dev + 1) * rows, pl.ds(at, 128)].astype(f32)

    return pl.pallas_call(
        kernel,
        grid_spec=pltpu.PrefetchScalarGridSpec(
            num_scalar_prefetch=1,
            grid=(parts,),
            in_specs=[ANY] * len(arrays),
            out_specs=[pl.BlockSpec((rows, count * 128), lambda p, me: (0, p))] * both,
            scratch_shapes=[pltpu.VMEM((count * rows, width), bf16), pltpu.SemaphoreType.DMA((len(arrays),))],
        ),
        out_shape=[jax.ShapeDtypeStruct((rows, parts * count * 128), f32)] * both,
        compiler_params=LIMIT,
        cost_estimate=takes(7.0),
    )(me, *arrays)


def place_wide(pieces, axis):
    arrays = [p[3] for p in pieces]
    rows, width = arrays[0].shape
    count = 8
    me = lax.axis_index(axis).reshape(1)

    def kernel(me, *refs):
        out, held, sems = refs[-3:]

        @pl.when(pl.program_id(0) == 0)
        def _():
            copies = slices_of(pieces, me[0], lambda dev: [(0, rows, dev * rows)])
            copy_all([(refs[k].at[pl.ds(s, size)], rows_at(held, t, size)) for k, s, size, t in copies], sems)

        out[...] = held[pl.ds(pl.multiple_of(pl.program_id(0) * rows, rows), rows), :].astype(f32)

    return pl.pallas_call(
        kernel,
        grid_spec=pltpu.PrefetchScalarGridSpec(
            num_scalar_prefetch=1,
            grid=(count,),
            in_specs=[ANY] * len(arrays),
            out_specs=pl.BlockSpec((rows, width), lambda p, me: (p, 0)),
            scratch_shapes=[pltpu.VMEM((count * rows, width), bf16), pltpu.SemaphoreType.DMA((len(arrays),))],
        ),
        out_shape=jax.ShapeDtypeStruct((count * rows, width), f32),
        compiler_params=LIMIT,
        cost_estimate=takes(6.0),
    )(me, *arrays)


def place_heads(pieces, axis, shard, cols):
    arrays = arrays_of(pieces)
    rows, wide = arrays[0].shape
    count, parts = 8, wide // cols
    me = lax.axis_index(axis).reshape(1)

    def slots(dev):
        return [(0, rows, dev * rows)]

    def kernel(me, *refs):
        refs, outs, tail, (held, sems) = refs[: len(arrays)], refs[len(arrays) : -3], refs[-3], refs[-2:]

        @pl.when(pl.program_id(0) == 0)
        def _():
            copies = slices_of(pieces, me[0], slots)
            copy_all([(refs[k].at[pl.ds(s, size)], rows_at(held, t, size)) for k, s, size, t in copies], sems)
            for dev in range(count):
                tail[dev] = held[dev * rows + shard : dev * rows + shard + 16, :]

        strip = outs[0].shape[0]
        for dev in range(count):
            block = held[pl.ds(pl.multiple_of(dev * rows + pl.program_id(0) * strip, 16), strip), :].astype(f32)
            for part, out in enumerate(outs):
                out[:, dev * cols : (dev + 1) * cols] = block[:, part * cols : (part + 1) * cols]

    steps = 4
    return pl.pallas_call(
        kernel,
        grid_spec=pltpu.PrefetchScalarGridSpec(
            num_scalar_prefetch=1,
            grid=(steps,),
            in_specs=[ANY] * len(arrays),
            out_specs=[pl.BlockSpec((shard // steps, count * cols), lambda g, me: (g, 0))] * parts
            + [pl.BlockSpec((count, 16, wide), lambda g, me: (0, 0, 0))],
            scratch_shapes=[pltpu.VMEM((count * rows, wide), bf16), pltpu.SemaphoreType.DMA((len(arrays),))],
        ),
        out_shape=[jax.ShapeDtypeStruct((shard, count * cols), f32)] * parts
        + [jax.ShapeDtypeStruct((count, 16, wide), bf16)],
        compiler_params=LIMIT,
        cost_estimate=takes(6.0),
    )(me, *arrays)


def own_attention(w_query, w_key, w_value, w_forget, forget_bias, w_out, gains, heads, me, level):
    shard = w_query.shape[0]
    cols = heads * HEAD_DIM
    each_level = forget_bias.shape[0]

    def kernel(at, wq, wk, wv, wo, wf, gain_one, gain_two, bias, out):
        for odd in range(2):

            @pl.when(at[0] % 2 == odd)
            def _():
                for i, w in enumerate((wq, wk, wv, wo)):
                    out[:shard, i * cols : (i + 1) * cols] = w[:, odd * cols : (odd + 1) * cols]

        row = lax.broadcasted_iota(jnp.int32, (16, shard), 0)
        gain_one, gain_two = (jnp.broadcast_to(g[...].astype(f32)[None], (16, shard)) for g in (gain_one, gain_two))
        rows = jnp.where(row == 0, gain_one, jnp.where(row == 1, gain_two, 0.0))
        head = lax.broadcasted_iota(jnp.int32, (16, HEADS), 1)
        slot = lax.broadcasted_iota(jnp.int32, (16, HEADS), 0)
        chosen = ((head == at[0] * heads + slot - 2) & (slot >= 2) & (slot < heads + 2)).astype(bf16)
        out[shard:, :shard] = (rows + dot(chosen, wf[...])).astype(bf16)
        row = lax.broadcasted_iota(jnp.int32, (16, each_level), 0)
        lane = lax.broadcasted_iota(jnp.int32, (16, each_level), 1)
        mine = (at[1] * each_level + lane == at[0] * heads + row) & (row < heads)
        column = jnp.sum(jnp.where(mine, bias[...].astype(f32), 0.0), axis=1, keepdims=True)
        out[shard:, shard:] = jnp.broadcast_to(column, (16, 4 * cols - shard)).astype(bf16)

    pair = pl.BlockSpec((shard, 2 * cols), lambda i, at: (0, at[0] // 2))
    line = pl.BlockSpec((shard,), lambda i, at: (0,))

    def whole(*shape):
        return pl.BlockSpec(shape, lambda i, at: (0, 0))

    return pl.pallas_call(
        kernel,
        grid_spec=pltpu.PrefetchScalarGridSpec(
            num_scalar_prefetch=1,
            grid=(1,),
            in_specs=[pair] * 4 + [whole(HEADS, shard), line, line, whole(1, each_level)],
            out_specs=whole(shard + 16, 4 * cols),
        ),
        out_shape=jax.ShapeDtypeStruct((shard + 16, 4 * cols), bf16),
        compiler_params=LARGE,
        cost_estimate=takes(3.0),
    )(
        jnp.stack([me, level]), w_query, w_key, w_value, w_out, w_forget.T, *gains, forget_bias.reshape(1, -1)
    )


def norm_project(pieces, pack, axis, seqs, cols):
    arrays = [p[3] for p in pieces]
    rows, width = arrays[0].shape[0] // seqs, arrays[0].shape[1]
    count, depth, wide = 8, pack.shape[0], pack.shape[2]
    shard = width // depth
    tokens = seqs * count * rows
    tile, heads = 2 * rows, cols // HEAD_DIM
    me = lax.axis_index(axis).reshape(1)

    def slots(dev):
        return [(s * rows, rows, (s * count + dev) * rows) for s in range(seqs)]

    number = len(slices_of(pieces, 0, slots))

    def kernel(me, pack_ref, *refs):
        x_out, out, qkv_out, raw_out, held, weights, turned, small, gain, sems = refs[-10:]
        step = pl.program_id(0)

        @pl.when(step == 0)
        def _():
            copies = []
            for z in range(depth):
                copies.append((pack_ref.at[z, pl.ds(0, shard)], rows_at(weights, z * shard, shard)))
                copies.append((pack_ref.at[z, pl.ds(pack.shape[1] - 16, 16)], small.at[z]))
            for k, s, size, t in slices_of(pieces, me[0], slots):
                copies.append((refs[k].at[pl.ds(s, size)], rows_at(held, t, size)))
            copy_all(copies, sems)
            turned[: 3 * cols, :] = weights[:, : 3 * cols].T
            row = lax.broadcasted_iota(jnp.int32, (16, shard), 0)
            for z in range(depth):
                at = slice(z * shard, (z + 1) * shard)
                rows = small[z, :, :shard].astype(f32)
                gain[:, at] = rows
                moved = jnp.concatenate([rows[2:], rows[:2]], axis=0)
                turned[3 * cols :, at] = jnp.where(row < heads, moved, 0.0).astype(bf16)

        bias = sum(small[z, :, shard:].astype(f32) for z in range(depth))[:, :1]
        block = held[pl.ds(pl.multiple_of(step * tile, tile), tile), :]
        x_out[...] = block
        x = block.astype(f32)
        normed = (x * inverse_rms(x) * gain[:1, :]).astype(bf16)
        out[...] = normed
        projected = dot_t(turned[...], normed)
        qkv_out[...] = projected[: 3 * cols].astype(bf16)
        raw_out[...] = projected[3 * cols :] + bias

    spec = pl.BlockSpec((tile, width), lambda p, me: (p, 0))
    shape = jax.ShapeDtypeStruct((tokens, width), bf16)
    return pl.pallas_call(
        kernel,
        grid_spec=pltpu.PrefetchScalarGridSpec(
            num_scalar_prefetch=1,
            grid=(tokens // tile,),
            in_specs=[ANY] * (1 + len(arrays)),
            out_specs=[
                spec,
                spec,
                pl.BlockSpec((3 * cols, tile), lambda p, me: (0, p)),
                pl.BlockSpec((16, tile), lambda p, me: (0, p)),
            ],
            scratch_shapes=[
                pltpu.VMEM((tokens, width), bf16),
                pltpu.VMEM((width, wide), bf16),
                pltpu.VMEM((3 * cols + 16, width), bf16),
                pltpu.VMEM((depth, 16, wide), bf16),
                pltpu.VMEM((16, width), f32),
                pltpu.SemaphoreType.DMA((number + 2 * depth,)),
            ],
        ),
        out_shape=[
            shape,
            shape,
            jax.ShapeDtypeStruct((3 * cols, tokens), bf16),
            jax.ShapeDtypeStruct((16, tokens), f32),
        ],
        compiler_params=LIMIT,
        cost_estimate=takes(12.0),
    )(me, pack, *arrays)


def hidden_norm(x_all, mixed_all, w_out, gain, seqs, rows, axis, turned):
    tokens, width = x_all.shape
    tile = 2 * rows
    tiles = tokens // seqs // tile
    me = lax.axis_index(axis).reshape(1)

    def kernel(me, x_ref, mixed_ref, w_ref, gain_ref, out_ref, own_ref, hidden_ref):
        hidden = x_ref[...].astype(f32) + (dot_t if turned else dot)(mixed_ref[...].T, w_ref[...])
        out_ref[...] = (hidden * inverse_rms(hidden) * gain_ref[...]).astype(bf16)

        @pl.when(pl.program_id(1) == me[0] // 2)
        def _():
            hidden_ref[...] = hidden
            own_ref[...] = hidden_ref[pl.ds(pl.multiple_of(me[0] % 2 * rows, rows), rows), :]

    return pl.pallas_call(
        kernel,
        grid_spec=pltpu.PrefetchScalarGridSpec(
            num_scalar_prefetch=1,
            grid=(seqs, tiles),
            in_specs=[
                pl.BlockSpec((tile, width), lambda s, t, me: (s * tiles + t, 0)),
                pl.BlockSpec((width, tile), lambda s, t, me: (0, s * tiles + t)),
                pl.BlockSpec((width, width), lambda s, t, me: (0, 0)),
                pl.BlockSpec((1, width), lambda s, t, me: (0, 0)),
            ],
            out_specs=[
                pl.BlockSpec((tile, width), lambda s, t, me: (s * tiles + t, 0)),
                pl.BlockSpec((rows, width), lambda s, t, me: (s, 0)),
            ],
            scratch_shapes=[pltpu.VMEM((tile, width), f32)],
        ),
        out_shape=[jax.ShapeDtypeStruct((tokens, width), bf16), jax.ShapeDtypeStruct((seqs * rows, width), f32)],
        compiler_params=LIMIT,
        cost_estimate=takes(17.0),
    )(me, x_all, mixed_all, w_out, gain.reshape(1, width))


def split_pair(value, keep_ref, send_ref, me):
    rows = value.shape[0] // 4
    blocks = [value[i * rows : (i + 1) * rows] for i in range(4)]
    core, side = me % 2 == 0, me // 2 % 2 == 0
    for t in range(2):
        first, second = (jnp.where(side, blocks[2 * t + c], blocks[2 - 2 * t + c]) for c in range(2))
        keep_ref[t] = jnp.where(core, first, second).astype(bf16)
        send_ref[t] = jnp.where(core, second, first).astype(bf16)


def pair_specs(paired, tile, tiles, width):
    if paired:
        block = pl.BlockSpec((2, tile // 4, width), lambda t, me: (t, 0, 0))
        shape = jax.ShapeDtypeStruct((2 * tiles, tile // 4, width), bf16)
        return (lambda t, me: me[0] // 4 ^ t), [block] * 2, [shape] * 2
    block = pl.BlockSpec((tile, width), lambda t, me: (t, 0))
    return (lambda t, me: t), [block], [jax.ShapeDtypeStruct((tiles * tile, width), bf16)]


def feed_forward(normed, cot, mlp, axis, seq, seqs, own):
    tokens, width = normed.shape
    depth, packed, ff_cols = mlp.shape
    shard = width // depth
    paired = lax.axis_size(axis) == 8
    tile = 512
    tiles = tokens // seqs // tile
    at, specs, shapes = pair_specs(paired, tile, tiles, width)
    blocks = width // ff_cols
    me = lax.axis_index(axis).reshape(1)

    def kernel(me, normed_ref, cot_ref, mlp_ref, inner_ref, grads_ref, *refs):
        outs, (gate_up, down, sems) = refs[:-3], refs[-3:]

        @pl.when(pl.program_id(0) == 0)
        def _():
            copies = []
            for z in range(depth):
                for part in range(2):
                    copies.append(
                        (
                            mlp_ref.at[z, pl.ds(part * shard, shard)],
                            gate_up.at[pl.ds(z * shard, shard), pl.ds(part * ff_cols, ff_cols)],
                        )
                    )
                for k in range(blocks):
                    copies.append(
                        (
                            mlp_ref.at[z, pl.ds(2 * shard + k * own, own)],
                            down.at[pl.ds(z * own, own), pl.ds(k * ff_cols, ff_cols)],
                        )
                    )
            copy_all(copies, sems)

        both = dot(normed_ref[...], gate_up[...])
        grad_inner = dot_t(cot_ref[...], down[...])
        gate, up = both[:, :ff_cols], both[:, ff_cols:]
        sig = jax.nn.sigmoid(gate)
        silu = gate * sig
        inner = (silu * up).astype(bf16)
        inner_ref[...] = inner
        grads_ref[:, :ff_cols] = (grad_inner * up * sig * (1.0 + gate * (1.0 - sig))).astype(bf16)
        grads_ref[:, ff_cols:] = (grad_inner * silu).astype(bf16)
        back = dot_t(grads_ref[...], gate_up[...])
        result = dot(inner, down[...])
        if paired:
            split_pair(back, outs[0], outs[1], me[0])
            split_pair(result, outs[2], outs[3], me[0])
        else:
            outs[0][...] = back.astype(bf16)
            outs[1][...] = result.astype(bf16)

    rows = pl.BlockSpec((tile, width), lambda t, me: (seq * tiles + at(t, me), 0))
    length = tokens // seqs

    def own_rows(cols):
        return pl.BlockSpec((tile, cols), lambda t, me: (at(t, me), 0))

    return pl.pallas_call(
        kernel,
        grid_spec=pltpu.PrefetchScalarGridSpec(
            num_scalar_prefetch=1,
            grid=(tiles,),
            in_specs=[rows, rows, ANY],
            out_specs=[own_rows(ff_cols), own_rows(2 * ff_cols)] + specs * 2,
            scratch_shapes=[
                pltpu.VMEM((width, 2 * ff_cols), bf16),
                pltpu.VMEM((ff_cols, width), bf16),
                pltpu.SemaphoreType.DMA((depth * (2 + blocks),)),
            ],
        ),
        out_shape=[
            jax.ShapeDtypeStruct((length, ff_cols), bf16),
            jax.ShapeDtypeStruct((length, 2 * ff_cols), bf16),
        ]
        + shapes * 2,
        compiler_params=LIMIT,
        cost_estimate=takes(17.0),
    )(me, normed, cot, mlp)


def project_back(grads, raw, pack, width, axis, seqs):
    cols, tokens = grads[0].shape
    depth, wide = pack.shape[0], pack.shape[2]
    shard, heads = width // depth, cols // HEAD_DIM
    tile = 512
    tiles = tokens // seqs // tile
    at, specs, shapes = pair_specs(True, tile, tiles, width)
    me = lax.axis_index(axis).reshape(1)

    def kernel(me, gq, gk, gv, raw, pack_ref, *refs):
        outs, (weights, small, turned, sems) = refs[:-4], refs[-4:]

        @pl.when((pl.program_id(0) == 0) & (pl.program_id(1) == 0))
        def _():
            copies = []
            for z in range(depth):
                copies.append((pack_ref.at[z, pl.ds(0, shard), pl.ds(0, 5 * 128)], rows_at(weights, z * shard, shard)))
                copies.append((pack_ref.at[z, pl.ds(shard, 16)], small.at[z]))
            copy_all(copies, sems)
            for z in range(depth):
                forget = jnp.concatenate(
                    [small[z, 2 : 2 + heads, :shard].astype(f32), jnp.zeros((EXTRA - heads, shard), f32)], axis=0
                )
                weights[z * shard : (z + 1) * shard, 3 * cols :] = forget.T.astype(bf16)

        for i, part in enumerate((gq, gk, gv)):
            turned[i * cols : (i + 1) * cols, :] = part[...]
        turned[3 * cols : 3 * cols + 16, :] = raw[...].astype(bf16)
        turned[3 * cols + 16 :, :] = jnp.zeros((EXTRA - 16, tile), bf16)
        back = dot_t(turned[...].T, weights[...])
        for s in range(seqs):

            @pl.when(pl.program_id(0) == s)
            def _():
                split_pair(back, outs[2 * s], outs[2 * s + 1], me[0])

    def seq_block(s):
        return pl.BlockSpec(
            (2, tile // 4, width), lambda q, t, me: (jnp.where(q == s, t, jnp.where(q < s, 0, tiles - 1)), 0, 0)
        )

    def columns(rows):
        return pl.BlockSpec((rows, tile), lambda s, t, me: (0, s * tiles + at(t, me)))

    return pl.pallas_call(
        kernel,
        grid_spec=pltpu.PrefetchScalarGridSpec(
            num_scalar_prefetch=1,
            grid=(seqs, tiles),
            in_specs=[columns(cols)] * 3 + [columns(16), ANY],
            out_specs=[seq_block(s) for s in range(seqs) for _ in range(2)],
            scratch_shapes=[
                pltpu.VMEM((width, 3 * cols + EXTRA), bf16),
                pltpu.VMEM((depth, 16, wide), bf16),
                pltpu.VMEM((3 * cols + EXTRA, tile), bf16),
                pltpu.SemaphoreType.DMA((2 * depth,)),
            ],
        ),
        out_shape=shapes * seqs,
        compiler_params=LIMIT,
        cost_estimate=takes(11.0),
    )(me, *grads, raw, pack)


def attention_grads(grads, raw, normed, branch, mixed, gain_row, pack, axis, seqs, depth, heads, each_level):
    cols, tokens = grads[0].shape
    width = normed.shape[1]
    shard = width // depth
    count, own_out, piece = branch.shape
    wide = pack.shape[2]
    me = lax.axis_index(axis).reshape(1)
    part = piece // seqs

    def kernel(me, gq, gk, gv, raw, normed_ref, branch_ref, mixed_ref, gain_ref, pack_ref, small_ref, out, turned, branches):
        z = pl.program_id(0)

        @pl.when(z == 0)
        def _():
            for i, g in enumerate((gq, gk, gv)):
                turned[i * cols : (i + 1) * cols, :] = g[...]
            turned[3 * cols :, :] = raw[...].astype(bf16)
            for dev in range(count):
                for s in range(seqs):
                    to = (s * count + dev) * part
                    branches[:, to : to + part] = branch_ref[dev, :, s * part : (s + 1) * part]

        grad = dot(turned[...], normed_ref[...])
        forget = grad[3 * cols :]
        columns = grad[: 3 * cols].T
        out[0, :shard, : 3 * cols] = columns.astype(bf16)
        out[0, :shard, 3 * cols :] = dot_t(mixed_ref[...], branches[...]).astype(bf16)
        by_row = jnp.sum(columns * pack_ref[0, :, : 3 * cols].astype(f32), axis=1, keepdims=True)
        by_row = jnp.broadcast_to(by_row, (shard, 8)).T[:1]
        small = small_ref[0, :, :shard].astype(f32)
        by_row = by_row + jnp.sum(forget[:heads] * small[2 : 2 + heads], axis=0, keepdims=True)
        row = lax.broadcasted_iota(jnp.int32, (16, shard), 0)
        lane = lax.broadcasted_iota(jnp.int32, (16, shard), 1)
        more = jnp.where(row == heads, gain_ref[...], jnp.where(row == heads + 2, by_row / small[:1], 0.0))
        sums = jnp.sum(raw[...], axis=1, keepdims=True)
        for h in range(heads):
            head = me[0] * heads + h
            at = head // each_level * shard + head % each_level - z * shard
            more = more + jnp.where((row == heads + 1) & (lane == at), sums[h : h + 1, :], 0.0)
        out[0, shard : shard + 16, :shard] = jnp.where(row < heads, forget, more).astype(bf16)
        out[0, shard : shard + 16, shard:] = jnp.zeros((16, wide - shard), bf16)
        out[0, shard + 16 :, :] = jnp.zeros((16, wide), bf16)

    def whole(*shape):
        return pl.BlockSpec(shape, lambda z, me: (0,) * len(shape))

    return pl.pallas_call(
        kernel,
        grid_spec=pltpu.PrefetchScalarGridSpec(
            num_scalar_prefetch=1,
            grid=(depth,),
            in_specs=[whole(cols, tokens)] * 3
            + [
                whole(16, tokens),
                pl.BlockSpec((tokens, shard), lambda z, me: (0, z)),
                whole(count, own_out, piece),
                pl.BlockSpec((shard, tokens), lambda z, me: (z, 0)),
                pl.BlockSpec((1, shard), lambda z, me: (0, z)),
                pl.BlockSpec((1, shard, wide), lambda z, me: (z, 0, 0)),
                pl.BlockSpec((1, 16, wide), lambda z, me: (z, shard // 16, 0)),
            ],
            out_specs=pl.BlockSpec((1, shard + 32, wide), lambda z, me: (z, 0, 0)),
            scratch_shapes=[pltpu.VMEM((3 * cols + 16, tokens), bf16), pltpu.VMEM((own_out, tokens), bf16)],
        ),
        out_shape=jax.ShapeDtypeStruct((depth, shard + 32, wide), bf16),
        compiler_params=LIMIT,
        cost_estimate=takes(12.0),
    )(me, *grads, raw, normed, branch, mixed, gain_row, pack, pack)


def own_kernel(me, gate, up, down, out):
    rows, own = gate.shape[0], down.shape[0]
    out[:rows, :] = gate[...]
    out[rows : 2 * rows, :] = up[...]
    for k in range(down.shape[1] // (128 * pl.num_programs(0))):
        at = (k * pl.num_programs(0) + pl.program_id(0)) * 128
        out[2 * rows + k * own : 2 * rows + (k + 1) * own, :] = down[:, pl.ds(pl.multiple_of(at, 128), 128)]


def own_mlp(w_gate, w_up, w_down, depth, count, me):
    shard, ff = w_gate.shape
    own = w_down.shape[0] // count
    width = w_down.shape[1]
    ff_cols = depth * own
    if own == 128:
        strip = pl.BlockSpec((shard, 128), lambda z, me: (0, z * count + me[0]))
        total = 2 * shard + own * width // ff_cols
        return pl.pallas_call(
            own_kernel,
            grid_spec=pltpu.PrefetchScalarGridSpec(
                num_scalar_prefetch=1,
                grid=(depth,),
                in_specs=[strip, strip, pl.BlockSpec((own, width), lambda z, me: (me[0], 0))],
                out_specs=pl.BlockSpec((total, 128), lambda z, me: (0, z)),
            ),
            out_shape=jax.ShapeDtypeStruct((total, ff_cols), bf16),
            cost_estimate=takes(4.0),
        )(me.reshape(1), w_gate, w_up, w_down)

    def ff_columns(w):
        w = w.reshape(shard, depth, count, own)
        return lax.dynamic_index_in_dim(w, me, 2, keepdims=False).reshape(shard, ff_cols)

    down = lax.dynamic_slice_in_dim(w_down, me * own, own, 0)
    return jnp.concatenate([ff_columns(w_gate), ff_columns(w_up), stack_columns(down, ff_cols)], axis=0)


def contract(a, b, da, db):
    return lax.dot_general(a, b, (((da,), (db,)), ((), ())), preferred_element_type=f32)


def stack_columns(a, width):
    return jnp.concatenate([a[:, i : i + width] for i in range(0, a.shape[1], width)], axis=0)


def to_shards(grad):
    return lax.psum_scatter(grad, "fsdp", scatter_dimension=0, tiled=True)


def local_eight(
    inputs,
    gain_attn,
    w_query,
    w_key,
    w_value,
    w_forget,
    forget_bias,
    w_out,
    gain_mlp,
    w_gate,
    w_up,
    w_down,
    cotangent,
):
    axis = "ctx"
    count, me = lax.axis_size(axis), lax.axis_index(axis)
    depth, level = lax.axis_size("fsdp"), lax.axis_index("fsdp")
    seqs, rows, width = inputs.shape
    tokens = seqs * count * rows
    shard = width // depth
    heads = HEADS // count
    cols = heads * HEAD_DIM
    ff_own = w_down.shape[0] // count
    ff_cols = depth * ff_own
    own_out = width // count
    flat_in, flat_cot = inputs.reshape(seqs * rows, width), cotangent.reshape(seqs * rows, width)

    def token_slots(dev):
        return [(s * rows, rows, (s * count + dev) * rows) for s in range(seqs)]

    x_state = gather_start(flat_in, axis)
    own = own_attention(
        w_query, w_key, w_value, w_forget, forget_bias, w_out, (gain_attn, gain_mlp), heads, me, level
    )
    pack = lax.all_gather(own, "fsdp", axis=0)
    mlp = lax.all_gather(own_mlp(after(w_gate, x_state[1:]), w_up, w_down, depth, count, me), "fsdp", axis=0)
    x_state = gather_far(x_state, axis)
    g_state = gather_start(after(flat_cot, x_state[3:]), axis)
    x_pieces = gather_core(x_state, axis)
    pack = after(pack, g_state[1:])
    out_own = pack[:, :shard, 3 * cols :].transpose(2, 0, 1).reshape(own_out, width)
    out_state = gather_start(out_own, axis)
    gains = pack[:, shard : shard + 2, :shard].astype(f32)
    gain_one, gain_two = gains[:, 0].reshape(width), gains[:, 1].reshape(width)

    x_all, normed, qkv, gate_raw = norm_project(x_pieces, pack, axis, seqs, cols)
    gate_raw, out_state = lax.optimization_barrier((gate_raw, out_state))
    out_state = gather_far(out_state, axis)
    attn, mixed, totals, decay = attend(qkv, gate_raw, seqs, heads)
    mixed, out_state = lax.optimization_barrier((mixed, out_state))
    mixed_state = gather_start(mixed, axis)
    out_full = place(gather_core(out_state, axis), axis, width, lambda dev: [(0, own_out, dev * own_out)])
    mixed_state = gather_far(after(mixed_state, out_full), axis)
    g_state = gather_far(after(g_state, mixed_state[3:]), axis)
    mixed_pieces = gather_core(mixed_state, axis)
    mixed_all = place(mixed_pieces, axis, width, lambda dev: [(0, cols, dev * cols)])
    normed_two, hidden_own = hidden_norm(x_all, mixed_all, out_full, gain_two, seqs, rows, axis, True)

    g_all = place(gather_core(after(g_state, normed_two), axis), axis, tokens, token_slots)
    sides = [feed_forward(normed_two, g_all, mlp, axis, s, seqs, ff_own) for s in range(seqs)]
    inner = jnp.concatenate([side[0] for side in sides], axis=0)
    gate_up_grads = jnp.concatenate([side[1] for side in sides], axis=0)
    back = Sums([side[2:4] for side in sides], axis)
    grad_down = back.hold(contract(inner, g_all, 0, 0).astype(bf16))
    back.first()
    normed_two = back.hold(normed_two)
    back.send_first()
    grad_gate_up = back.hold(contract(normed_two, gate_up_grads, 0, 0).astype(bf16))
    back.second()
    back.send_second()
    back = back.result()
    grad_down, grad_gate_up = to_shards(grad_down), to_shards(grad_gate_up)

    grad_from_norm, grad_gain_two = norm_pull(hidden_own, gain_two, back)
    grad_hidden = flat_cot.astype(f32) + grad_from_norm
    branch = grad_hidden.astype(bf16)
    grad_mixed = contract(out_full, branch, 0, 1).astype(bf16).reshape(count, cols, seqs * rows)
    result = Sums(after([side[4:6] for side in sides], grad_mixed), axis)
    branch = after(branch, grad_mixed).T.reshape(count, own_out, seqs * rows)
    grad_mixed = lax.all_to_all(grad_mixed, axis, 0, 0, tiled=True)
    result.first()
    grad_mixed, grad_down, branch = result.hold((grad_mixed, grad_down, branch))
    branch = lax.all_to_all(branch, axis, 0, 0, tiled=True)
    result.send_first()
    down_state = gather_start(grad_down, axis)
    gq, gk, gv, grad_raw = attend_pull(qkv, decay, grad_mixed, attn, totals, gate_raw, seqs, heads)

    down_state, branch, grad_gate_up, grad_raw = result.hold((down_state, branch, grad_gate_up, grad_raw))
    gate_up_state = gather_start(grad_gate_up, axis)
    down_state = gather_far(down_state, axis)
    result.second()
    grad_raw = result.hold(grad_raw)
    result.send_second()
    grads = (gq, gk, gv)
    grad_pack = attention_grads(
        grads, grad_raw, normed, branch, mixed_all, grad_gain_two[None], pack, axis, seqs, depth, heads, HEADS // depth
    )
    pairs = project_back(grads, after(grad_raw, grad_pack), pack, width, axis, seqs)
    grad_pack = to_shards(grad_pack.reshape(-1, 4 * cols))
    pairs, down_state, gate_up_state = result.hold((pairs, down_state, gate_up_state))
    grad_normed = Sums([pairs[2 * s : 2 * s + 2] for s in range(seqs)], axis)
    gate_up_state = gather_far(gate_up_state, axis)
    down_pieces = gather_core(down_state, axis)
    grad_normed.first()
    gate_up_state = grad_normed.hold(gate_up_state)
    grad_normed.send_first()
    gate_up_pieces = gather_core(gate_up_state, axis)
    output = (hidden_own + result.result()).astype(bf16).reshape(seqs, rows, width)
    grad_pack, gate_up_arrays, _ = grad_normed.hold((grad_pack, arrays_of(gate_up_pieces), output))
    gate_up_pieces = [piece[:3] + (array,) for piece, array in zip(gate_up_pieces, gate_up_arrays)]
    grad_normed.second()
    grad_normed.send_second()
    pack_state = gather_start(grad_pack, axis)
    grad_down = place_wide(down_pieces, axis)
    grad_gate, grad_up = place_columns(gate_up_pieces, axis, depth, 2)
    pack_state, _ = grad_normed.hold((pack_state, (grad_down, grad_gate)))
    pack_state = gather_far(pack_state, axis)
    grad_in, _ = norm_pull(flat_in.astype(f32), gain_one, grad_normed.result())
    input_grad = (grad_hidden + grad_in).reshape(seqs, rows, width)
    pack_pieces = gather_core(after(pack_state, input_grad), axis)
    grad_query, grad_key, grad_value, grad_out, tail = place_heads(pack_pieces, axis, shard, cols)
    tail = tail[:, :, :shard].astype(f32)
    tail_sum = jnp.sum(tail[:, heads : heads + 3], axis=0)
    return (
        output,
        input_grad,
        tail_sum[2],
        grad_query,
        grad_key,
        grad_value,
        tail[:, :heads].reshape(HEADS, shard).T,
        tail_sum[1, : forget_bias.shape[0]],
        grad_out,
        tail_sum[0],
        grad_gate,
        grad_up,
        grad_down,
    )


def local_any(
    inputs,
    gain_attn,
    w_query,
    w_key,
    w_value,
    w_forget,
    forget_bias,
    w_out,
    gain_mlp,
    w_gate,
    w_up,
    w_down,
    cotangent,
):
    axis = "ctx"
    count, me = lax.axis_size(axis), lax.axis_index(axis)
    depth, level = lax.axis_size("fsdp"), lax.axis_index("fsdp")
    seqs, rows, width = inputs.shape
    tokens = seqs * count * rows
    shard = width // depth
    heads = -(-HEADS // count)
    cols = heads * HEAD_DIM
    ff_own = w_down.shape[0] // count
    ff_cols = depth * ff_own
    out_rows, own_out = shard // count, width // count
    flat_in, flat_cot = inputs.reshape(seqs * rows, width), cotangent.reshape(seqs * rows, width)

    def own_columns(w, each_head):
        w = jnp.pad(w, ((0, 0), (0, count * heads * each_head - w.shape[1])))
        return lax.dynamic_slice_in_dim(w, me * heads * each_head, heads * each_head, 1)

    extra = [own_columns(w_forget, 1), gain_attn[:, None], gain_mlp[:, None]]
    extra += [jnp.pad(forget_bias, (0, shard - forget_bias.shape[0]))[:, None]]
    extra += [jnp.zeros((shard, EXTRA - heads - 3), bf16)]
    pack = [own_columns(w, HEAD_DIM) for w in (w_query, w_key, w_value)] + extra
    pack = lax.all_gather(jnp.concatenate(pack, axis=1), "fsdp", axis=0, tiled=True)
    extra = pack[:, 3 * cols :]
    gain_one = extra[:, heads].astype(f32)
    gain_two = extra[:, heads + 1].astype(f32)
    biases = extra[:, heads + 2].reshape(depth, shard)[:, : forget_bias.shape[0]].reshape(-1)
    biases = jnp.pad(biases, (0, count * heads - HEADS))
    bias = lax.dynamic_slice_in_dim(biases, me * heads, heads).astype(f32)
    out_own = lax.all_gather(lax.dynamic_slice_in_dim(w_out, me * out_rows, out_rows, 0), "fsdp", axis=0)
    out_full = lax.all_gather(out_own, axis, axis=1).reshape(width, width)
    mlp = lax.all_gather(own_mlp(w_gate, w_up, w_down, depth, count, me), "fsdp", axis=0)

    x_all = lax.all_gather(inputs, axis, axis=1, tiled=True).reshape(tokens, width)
    x_wide = x_all.astype(f32)
    normed = (x_wide * inverse_rms(x_wide) * gain_one).astype(bf16)
    g_all = lax.all_gather(after(cotangent, normed), axis, axis=1, tiled=True).reshape(tokens, width)
    qkv = contract(pack[:, : 3 * cols], normed, 0, 1).astype(bf16)
    gate_raw = contract(extra, normed, 0, 1)[:heads] + bias[:, None]
    gate_raw = jnp.pad(gate_raw, ((0, -heads % 16), (0, 0)))
    attn, mixed, totals, decay = attend(qkv, gate_raw, seqs, heads)
    mixed_all = lax.all_gather(mixed, axis, axis=0, tiled=True)[:width]
    normed_two, hidden_own = hidden_norm(x_all, mixed_all, out_full, gain_two, seqs, rows, axis, False)

    def summed(part):
        return lax.psum_scatter(part.reshape(count, rows, width), axis, scatter_dimension=0).astype(f32)

    sides, sums = [], []
    for s in range(seqs):
        side = feed_forward(normed_two, g_all, mlp, axis, s, seqs, ff_own)
        sides.append(side[:2])
        sums.append([summed(side[2]), summed(side[3])])
        normed_two = after(normed_two, sums[s])
    back, result = (jnp.concatenate(parts, axis=0) for parts in zip(*sums))
    inner = jnp.concatenate([side[0] for side in sides], axis=0)
    gate_up_grads = jnp.concatenate([side[1] for side in sides], axis=0)
    grad_down = to_shards(contract(inner, g_all, 0, 0).astype(bf16))
    grad_gate_up = to_shards(contract(normed_two, gate_up_grads, 0, 0).astype(bf16))
    output = (hidden_own + result).astype(bf16)

    grad_from_norm, grad_gain_two = norm_pull(hidden_own, gain_two, back)
    grad_hidden = flat_cot.astype(f32) + grad_from_norm
    branch = grad_hidden.astype(bf16)
    grad_mixed = contract(out_full, branch, 1, 1).astype(bf16)
    grad_mixed = jnp.pad(grad_mixed, ((0, count * cols - width), (0, 0)))
    grad_mixed = lax.all_to_all(grad_mixed.reshape(count, cols, seqs * rows), axis, 0, 0, tiled=True)
    branch = lax.all_to_all(branch.T.reshape(count, own_out, seqs * rows), axis, 0, 0, tiled=True)
    branch = branch.reshape(count, own_out, seqs, rows).transpose(1, 2, 0, 3).reshape(own_out, tokens)
    grad_out = contract(branch, mixed_all, 1, 1)
    gq, gk, gv, grad_raw = attend_pull(qkv, decay, grad_mixed, attn, totals, gate_raw, seqs, heads)
    grad_raw = jnp.pad(grad_raw[:heads].astype(bf16), ((0, EXTRA - heads), (0, 0)))
    grads = jnp.concatenate([gq, gk, gv, grad_raw], axis=0)
    grad_normed = contract(grads, pack, 0, 1).astype(bf16).reshape(seqs, count * rows, width)
    grad_normed = jnp.concatenate([summed(part) for part in grad_normed], axis=0)

    grad_pack = contract(grads, normed, 1, 0)
    head_at = me * heads + jnp.arange(heads)
    bias_col = head_at // (HEADS // depth) * shard + head_at % (HEADS // depth)
    bias_sum = jnp.where(head_at < HEADS, jnp.sum(grad_raw[:heads].astype(f32), axis=1), 0.0)
    at_col = jnp.arange(width)[None, :] == bias_col[:, None]
    bias_row = jnp.sum(jnp.where(at_col, bias_sum[:, None], 0.0), axis=0, keepdims=True)
    tail = [grad_pack[3 * cols : 3 * cols + heads], grad_gain_two[None], bias_row]
    tail += [jnp.zeros((EXTRA - heads - 2, width), f32)]
    grad_pack = jnp.concatenate([grad_pack[: 3 * cols]] + tail + [grad_out], axis=0).astype(bf16)
    grad_pack = to_shards(grad_pack.reshape(-1, depth, shard).transpose(1, 0, 2).reshape(-1, shard))
    grad_pack = lax.all_gather(grad_pack, axis)
    out_at = 3 * cols + EXTRA

    def turned(start, size):
        return grad_pack[:, start : start + size].reshape(-1, shard)[:width].T.astype(f32)

    tail = grad_pack[:, 3 * cols : out_at].astype(f32)
    tail_sum = jnp.sum(tail[:, heads : heads + 2], axis=0)
    grad_down = lax.all_gather(grad_down, axis, axis=0, tiled=True).astype(f32)
    grad_gate_up = lax.all_gather(grad_gate_up.reshape(shard, 2, depth, ff_own), axis)
    grad_gate_up = grad_gate_up.transpose(2, 1, 3, 0, 4).reshape((2,) + w_gate.shape).astype(f32)
    grad_in, grad_gain_one = norm_pull(flat_in.astype(f32), gain_one, grad_normed)
    grad_gain_one = lax.psum(grad_gain_one, (axis, "fsdp"))
    return (
        output.reshape(seqs, rows, width),
        (grad_hidden + grad_in).reshape(seqs, rows, width),
        lax.dynamic_slice_in_dim(grad_gain_one, level * shard, shard),
        turned(0, cols),
        turned(cols, cols),
        turned(2 * cols, cols),
        tail[:, :heads].reshape(count * heads, shard)[:HEADS].T,
        tail_sum[1, : forget_bias.shape[0]],
        turned(out_at, own_out),
        tail_sum[0],
        grad_gate_up[0],
        grad_gate_up[1],
        grad_down,
    )


def solution(mesh):
    split, first, rest = P("fsdp", "ctx", None), P("fsdp"), P("fsdp", None)
    return jax.shard_map(
        local_eight if mesh.shape["ctx"] == 8 else local_any,
        mesh=mesh,
        in_specs=(split, first, rest, rest, rest, rest, first, rest, first, rest, rest, rest, split),
        out_specs=(split, split, first, rest, rest, rest, rest, first, rest, first, rest, rest, rest),
        check_vma=False,
    )
```

```python
import jax
import jax.numpy as jnp
from jax import lax
from jax.experimental import pallas as pl
from jax.experimental.pallas import tpu as pltpu
from jax.sharding import PartitionSpec as P

HEADS = 24
HEAD_DIM = 64
BLK = 256
EXTRA = 64
norm_eps = 1e-06
bf16 = jnp.bfloat16
f32 = jnp.float32


def exchange(x, axis, mask):
    return lax.ppermute(x, axis, [(i, i ^ mask) for i in range(lax.axis_size(axis))])


def after(x, done):
    return lax.optimization_barrier((x, done))[0]


def first_half(rows):
    return -(-rows // 32) * 16


def gather_start(x, axis):
    return x, exchange(x, axis, 2), exchange(x, axis, 4)


def gather_far(state, axis):
    x, side, above = state
    half = first_half(x.shape[0])
    return x, side, above, exchange(side[:half], axis, 4), exchange(above[half:], axis, 2)


def gather_core_once(state, axis):
    size = state[0].shape[0]
    half = first_half(size)
    all_rows = jnp.concatenate(state, axis=0)
    other = exchange(all_rows, axis, 1)
    places = ((0, 0, size), (2, 0, size), (4, 0, size), (6, 0, half), (6, half, size - half))
    pieces = [place + (array,) for place, array in zip(places, state)]
    return pieces + [(mask ^ 1, 0, size, other, i * size) for i, mask in enumerate((0, 2, 4, 6))]


def gather_core(state, axis):
    size = state[0].shape[0]
    half = first_half(size)
    places = ((0, 0, size), (2, 0, size), (4, 0, size), (6, 0, half), (6, half, size - half))
    pieces = [place + (array,) for place, array in zip(places, state)]
    return pieces + [(mask ^ 1, start, rows, exchange(a, axis, 1)) for mask, start, rows, a in pieces]


def held(first, second, pieces):
    first, second, arrays = lax.optimization_barrier((first, second, arrays_of(pieces)))
    return first, second, [piece[:3] + (array,) for piece, array in zip(pieces, arrays)]


def arrays_of(pieces):
    return [piece[3] for piece in pieces]


ANY = pl.BlockSpec(memory_space=pl.ANY)
LIMIT = pltpu.CompilerParams(vmem_limit_bytes=48 * 2**20)


def takes(us):
    return pl.CostEstimate(flops=int(us * 1.15e9), bytes_accessed=int(us * 1e5), transcendentals=0)


LARGE = pltpu.CompilerParams(vmem_limit_bytes=60 * 2**20)
SMALL = pltpu.CompilerParams(vmem_limit_bytes=24 * 2**20)


def copy_all(copies, sems):
    started = [pltpu.make_async_copy(source, target, sems.at[i]) for i, (source, target) in enumerate(copies)]
    for copy in started:
        copy.start()
    for copy in started:
        copy.wait()


def rows_at(ref, start, size):
    return ref.at[pl.ds(start if isinstance(start, int) else pl.multiple_of(start, 16), size)]


def slices_of(pieces, me, slots):
    copies = []
    for k, (mask, first, size, _, *at) in enumerate(pieces):
        for start, rows, target in slots(me ^ mask):
            low, high = max(start, first), min(start + rows, first + size)
            if low < high:
                copies.append((k, low - first + sum(at), high - low, target + (low - start)))
    return copies


def place(pieces, axis, total, slots):
    arrays = [p[3] for p in pieces]
    width, dtype = arrays[0].shape[1], arrays[0].dtype
    me = lax.axis_index(axis).reshape(1)

    def kernel(me, *refs):
        out, sems = refs[-2:]
        copies = slices_of(pieces, me[0], slots)
        copy_all([(refs[k].at[pl.ds(s, size)], rows_at(out, t, size)) for k, s, size, t in copies], sems)

    return pl.pallas_call(
        kernel,
        in_specs=[pl.BlockSpec(memory_space=pltpu.SMEM)] + [ANY] * len(arrays),
        out_specs=pl.BlockSpec(memory_space=pltpu.VMEM),
        out_shape=jax.ShapeDtypeStruct((total, width), dtype),
        scratch_shapes=[pltpu.SemaphoreType.DMA((len(slices_of(pieces, 0, slots)),))],
        compiler_params=LIMIT,
        cost_estimate=takes(5.0),
    )(me, *arrays)


def add_first(keep, core, half):
    rows, width = keep.shape[1:]

    def kernel(keep, core, sent):
        sent[...] = (keep[...].astype(f32) + core[...].astype(f32)).astype(bf16)

    block = pl.BlockSpec((1, rows, width), (lambda g: (g + 2, 0, 0)) if half % 2 else (lambda g: (2 * g + 1, 0, 0)))
    return pl.pallas_call(
        kernel,
        grid=(2,),
        in_specs=[block, block],
        out_specs=pl.BlockSpec((1, rows, width), lambda g: (g, 0, 0)),
        out_shape=jax.ShapeDtypeStruct((2, rows, width), bf16),
        compiler_params=SMALL,
        cost_estimate=takes(2),
    )(keep, core)


def add_second(keep, core, moved, half):
    rows, width = keep.shape[1:]
    part = rows // 2

    def kernel(keep, core, moved, sent):
        total = keep[0].astype(f32) + core[0].astype(f32) + moved[0].astype(f32)
        sent[...] = total.astype(bf16)

    def block(at):
        return pl.BlockSpec((1, part, width), lambda g: (at, g, 0))

    other = 1 if half % 2 else 2
    return pl.pallas_call(
        kernel,
        grid=(rows // part,),
        in_specs=[block(other), block(other), block(1)],
        out_specs=pl.BlockSpec((part, width), lambda g: (g, 0)),
        out_shape=jax.ShapeDtypeStruct((rows, width), bf16),
        compiler_params=SMALL,
        cost_estimate=takes(2),
    )(keep, core, moved)


class Sums:
    def __init__(self, pairs, axis):
        self.axis = axis
        self.parts = [[keep] for keep, _ in pairs]
        self.moving = [exchange(send, axis, 1) for _, send in pairs]

    def hold(self, others):
        self.moving, others = lax.optimization_barrier((self.moving, others))
        return others

    def arrived(self):
        for part, moved in zip(self.parts, self.moving):
            part.append(moved)

    def first(self):
        self.arrived()
        self.moving = [add_first(*part, h) for h, part in enumerate(self.parts)]

    def send_first(self):
        self.moving = [exchange(m, self.axis, (2, 4)[h % 2]) for h, m in enumerate(self.moving)]

    def second(self):
        self.arrived()
        self.moving = [add_second(*part, h) for h, part in enumerate(self.parts)]

    def send_second(self):
        self.moving = [exchange(m, self.axis, (4, 2)[h % 2]) for h, m in enumerate(self.moving)]

    def result(self):
        sums = [sum(p[0].astype(f32) for p in part) for part in self.parts]
        return jnp.concatenate([s + m.astype(f32) for s, m in zip(sums, self.moving)], axis=0)


def each(count, body, carry):
    if count <= 3:
        for j in range(count):
            carry = body(j, carry)
        return carry
    return lax.fori_loop(0, count, body, carry)


def span(j):
    return pl.ds(j * BLK if isinstance(j, int) else pl.multiple_of(j * BLK, BLK), BLK)


def dot(a, b):
    return jnp.dot(a, b, preferred_element_type=f32)


def dot_t(a, b):
    return lax.dot_general(a, b, (((1,), (1,)), ((), ())), preferred_element_type=f32)


def running_sum(rows, backward):
    length = rows.shape[1]
    lane = lax.broadcasted_iota(jnp.int32, rows.shape, 1)
    step = 1
    while step < length:
        moved = pltpu.roll(rows, length - step if backward else step, 1)
        inside = lane < length - step if backward else lane >= step
        rows = rows + jnp.where(inside, moved, 0.0)
        step *= 2
    return rows


def log_sigmoid(x):
    return jnp.minimum(x, 0.0) - jnp.log1p(jnp.exp(-jnp.abs(x)))


def head_rows(h, part=0):
    return slice(part + h * HEAD_DIM, part + (h + 1) * HEAD_DIM)


def attend(qkv, gate_raw, seqs, heads):
    length, cols = qkv.shape[1] // seqs, heads * HEAD_DIM
    lines = gate_raw.shape[0]

    def kernel(qkv_ref, raw_ref, attn_ref, mixed_ref, total_ref, decay_ref, k_rows, decay_cols):
        decay = running_sum(log_sigmoid(raw_ref[...]), False)
        decay_ref[...] = decay
        decay_cols[...] = decay.T
        total_ref[...] = jnp.ones_like(total_ref)
        for h in range(heads):
            k_rows[h] = qkv_ref[head_rows(h, cols), :].T

        for i in range(length // BLK):
            for h in range(heads):
                at = span(i)
                query = qkv_ref[head_rows(h), at] * 0.125
                decay_q = decay_ref[h : h + 1, at]

                def visit(j, carry):
                    summed, total = carry
                    offset = decay_q - decay_cols[span(j), h : h + 1]
                    if isinstance(j, int) and j == i:
                        offset = -jnp.abs(offset)
                    terms = jnp.exp(dot(k_rows[h, span(j), :], query) + offset)
                    total = total + jnp.sum(terms, axis=0, keepdims=True)
                    return summed + dot(qkv_ref[head_rows(h, 2 * cols), span(j)], terms.astype(bf16)), total

                start = (jnp.zeros((HEAD_DIM, BLK), f32), jnp.zeros((1, BLK), f32))
                summed, total = visit(i, each(i, visit, start))
                attn = summed / total
                attn_ref[head_rows(h), at] = attn
                mixed_ref[head_rows(h), at] = attn.astype(bf16)
                total_ref[h : h + 1, at] = total

    def block(rows):
        return pl.BlockSpec((rows, length), lambda s: (0, s))

    tokens = seqs * length
    return pl.pallas_call(
        kernel,
        grid=(seqs,),
        in_specs=[block(3 * cols), block(lines)],
        out_specs=[block(cols), block(cols), block(lines), block(lines)],
        out_shape=[
            jax.ShapeDtypeStruct((cols, tokens), f32),
            jax.ShapeDtypeStruct((cols, tokens), bf16),
            jax.ShapeDtypeStruct((lines, tokens), f32),
            jax.ShapeDtypeStruct((lines, tokens), f32),
        ],
        scratch_shapes=[pltpu.VMEM((heads, length, HEAD_DIM), bf16), pltpu.VMEM((length, lines), f32)],
        compiler_params=SMALL,
        cost_estimate=takes(9.0),
    )(qkv, gate_raw)


def attend_pull(qkv, decay, grad_mixed, attn, totals, gate_raw, seqs, heads):
    length, cols = qkv.shape[1] // seqs, heads * HEAD_DIM
    lines = gate_raw.shape[0]
    pieces = grad_mixed.shape[0]
    piece = length // pieces
    deep = HEAD_DIM + 16

    def kernel(
        qkv_ref, decay_ref, gm_ref, attn_ref, total_ref, raw_ref, gq_ref, gk_ref, gv_ref, graw_ref,
        k_rows, v_rows, decay_cols, q_more, k_more, gs_all, delta_all, gk_sum, gv_sum, gd_all,
    ):
        decay_cols[...] = decay_ref[...].T
        gd_all[...] = jnp.zeros_like(gd_all)
        gk_sum[...] = jnp.zeros_like(gk_sum)
        gv_sum[...] = jnp.zeros_like(gv_sum)
        more = (lax.broadcasted_iota(jnp.int32, (16, length), 0) == 0).astype(bf16)
        for h in range(heads):
            k_rows[h] = qkv_ref[head_rows(h, cols), :].T
            v_rows[h] = qkv_ref[head_rows(h, 2 * cols), :].T
            k_more[h, :HEAD_DIM, :] = qkv_ref[head_rows(h, cols), :]
            k_more[h, HEAD_DIM:, :] = more
            q_more[h, :HEAD_DIM, :] = qkv_ref[head_rows(h), :] * 0.125
            q_more[h, HEAD_DIM:, :] = more
            for p in range(pieces):
                at = slice(p * piece, (p + 1) * piece)
                grad = gm_ref[p, head_rows(h), :].astype(f32)
                total = total_ref[h : h + 1, at]
                gs_all[head_rows(h), at] = (grad / total).astype(bf16)
                delta_all[h : h + 1, at] = jnp.sum(grad * attn_ref[head_rows(h), at], axis=0, keepdims=True) / total

        key_first = lax.broadcasted_iota(jnp.int32, (BLK, BLK), 0) <= lax.broadcasted_iota(
            jnp.int32, (BLK, BLK), 1
        )
        ones = (lax.broadcasted_iota(jnp.int32, (16, BLK), 0) == 0).astype(bf16)

        for i in range(length // BLK):
            for h in range(heads):
                at = span(i)
                query = q_more[h, :HEAD_DIM, at]
                decay_q = decay_ref[h : h + 1, at]
                gs = gs_all[head_rows(h), at]
                delta = delta_all[h : h + 1, at]

                def terms_of(j, last):
                    offset = decay_q - decay_cols[span(j), h : h + 1]
                    if last:
                        offset = -jnp.abs(offset)
                    terms = jnp.exp(dot(k_rows[h, span(j), :], query) + offset)
                    grads = (terms * (dot(v_rows[h, span(j), :], gs) - delta)).astype(bf16)
                    gv_sum[head_rows(h), span(j)] += dot_t(gs, terms.astype(bf16))
                    return grads

                def visit(j, carry):
                    grads = terms_of(j, False)
                    gk_sum[h, :, span(j)] += dot_t(q_more[h, :, at], grads)
                    return carry + dot(k_more[h, :, span(j)], grads)

                gq = each(i, visit, jnp.zeros((deep, BLK), f32))
                grads = terms_of(i, True)
                gk_sum[h, :HEAD_DIM, at] += dot_t(query, grads)
                gq_own = gq[:HEAD_DIM] + dot(k_more[h, :HEAD_DIM, at], grads)
                signed = jnp.where(key_first, grads, -grads)
                gk_sum[h, HEAD_DIM:, at] += dot_t(ones, signed)
                gd_all[h : h + 1, at] = (gq[HEAD_DIM:] + dot(ones, signed))[:1]
                gq_ref[head_rows(h), at] = (gq_own * 0.125).astype(bf16)

        for h in range(heads):
            gk_ref[head_rows(h), :] = gk_sum[h, :HEAD_DIM, :].astype(bf16)
            gd_all[h : h + 1, :] = gd_all[h : h + 1, :] - gk_sum[h, HEAD_DIM : HEAD_DIM + 1, :]
        gv_ref[...] = gv_sum[...].astype(bf16)
        grad_log = running_sum(gd_all[...], True)
        graw_ref[...] = (grad_log * jax.nn.sigmoid(-raw_ref[...])).astype(bf16).astype(f32)

    def block(rows):
        return pl.BlockSpec((rows, length), lambda s: (0, s))

    tokens = seqs * length
    shape = jax.ShapeDtypeStruct((cols, tokens), bf16)
    return pl.pallas_call(
        kernel,
        grid=(seqs,),
        in_specs=[
            block(3 * cols),
            block(lines),
            pl.BlockSpec((pieces, cols, piece), lambda s: (0, 0, s)),
            block(cols),
            block(lines),
            block(lines),
        ],
        out_specs=[block(cols), block(cols), block(cols), block(lines)],
        out_shape=[shape, shape, shape, jax.ShapeDtypeStruct((lines, tokens), f32)],
        scratch_shapes=[
            pltpu.VMEM((heads, length, HEAD_DIM), bf16),
            pltpu.VMEM((heads, length, HEAD_DIM), bf16),
            pltpu.VMEM((length, lines), f32),
            pltpu.VMEM((heads, deep, length), bf16),
            pltpu.VMEM((heads, deep, length), bf16),
            pltpu.VMEM((cols, length), bf16),
            pltpu.VMEM((lines, length), f32),
            pltpu.VMEM((heads, deep, length), f32),
            pltpu.VMEM((cols, length), f32),
            pltpu.VMEM((lines, length), f32),
        ],
        compiler_params=SMALL,
        cost_estimate=takes(19.0),
    )(qkv, decay, grad_mixed, attn, totals, gate_raw)


def inverse_rms(rows):
    return lax.rsqrt(jnp.mean(rows * rows, axis=-1, keepdims=True) + norm_eps)


def norm_pull(rows, gain, grad):
    scale = inverse_rms(rows)
    weighted = grad * gain
    inner = jnp.mean(rows * weighted, axis=-1, keepdims=True)
    return scale * weighted - rows * (scale * scale * scale * inner), jnp.sum(grad * rows * scale, axis=0)


def place_columns(pieces, axis, parts, both):
    arrays = [p[3] for p in pieces]
    rows, width = arrays[0].shape
    count = 8
    me = lax.axis_index(axis).reshape(1)

    def slots(dev):
        return [(0, rows, dev * rows)]

    def kernel(me, *refs):
        outs, (held, sems) = refs[len(arrays) : -2], refs[-2:]

        @pl.when(pl.program_id(0) == 0)
        def _():
            copies = slices_of(pieces, me[0], slots)
            copy_all([(refs[k].at[pl.ds(s, size)], rows_at(held, t, size)) for k, s, size, t in copies], sems)

        for b, out in enumerate(outs):
            at = pl.multiple_of((b * parts + pl.program_id(0)) * 128, 128)
            for dev in range(count):
                out[:, dev * 128 : (dev + 1) * 128] = held[dev * rows : (dev + 1) * rows, pl.ds(at, 128)].astype(f32)

    return pl.pallas_call(
        kernel,
        grid_spec=pltpu.PrefetchScalarGridSpec(
            num_scalar_prefetch=1,
            grid=(parts,),
            in_specs=[ANY] * len(arrays),
            out_specs=[pl.BlockSpec((rows, count * 128), lambda p, me: (0, p))] * both,
            scratch_shapes=[pltpu.VMEM((count * rows, width), bf16), pltpu.SemaphoreType.DMA((len(arrays),))],
        ),
        out_shape=[jax.ShapeDtypeStruct((rows, parts * count * 128), f32)] * both,
        compiler_params=LIMIT,
        cost_estimate=takes(7.0),
    )(me, *arrays)


def place_wide(pieces, axis):
    arrays = [p[3] for p in pieces]
    rows, width = arrays[0].shape
    count = 8
    me = lax.axis_index(axis).reshape(1)

    def kernel(me, *refs):
        out, held, sems = refs[-3:]

        @pl.when(pl.program_id(0) == 0)
        def _():
            copies = slices_of(pieces, me[0], lambda dev: [(0, rows, dev * rows)])
            copy_all([(refs[k].at[pl.ds(s, size)], rows_at(held, t, size)) for k, s, size, t in copies], sems)

        out[...] = held[pl.ds(pl.multiple_of(pl.program_id(0) * rows, rows), rows), :].astype(f32)

    return pl.pallas_call(
        kernel,
        grid_spec=pltpu.PrefetchScalarGridSpec(
            num_scalar_prefetch=1,
            grid=(count,),
            in_specs=[ANY] * len(arrays),
            out_specs=pl.BlockSpec((rows, width), lambda p, me: (p, 0)),
            scratch_shapes=[pltpu.VMEM((count * rows, width), bf16), pltpu.SemaphoreType.DMA((len(arrays),))],
        ),
        out_shape=jax.ShapeDtypeStruct((count * rows, width), f32),
        compiler_params=LIMIT,
        cost_estimate=takes(6.0),
    )(me, *arrays)


def place_heads(pieces, axis, shard, cols):
    arrays = arrays_of(pieces)
    rows, wide = arrays[0].shape
    count, parts = 8, wide // cols
    me = lax.axis_index(axis).reshape(1)

    def slots(dev):
        return [(0, rows, dev * rows)]

    def kernel(me, *refs):
        refs, outs, tail, (held, sems) = refs[: len(arrays)], refs[len(arrays) : -3], refs[-3], refs[-2:]

        @pl.when(pl.program_id(0) == 0)
        def _():
            copies = slices_of(pieces, me[0], slots)
            copy_all([(refs[k].at[pl.ds(s, size)], rows_at(held, t, size)) for k, s, size, t in copies], sems)
            for dev in range(count):
                tail[dev] = held[dev * rows + shard : dev * rows + shard + 16, :]

        strip = outs[0].shape[0]
        for dev in range(count):
            block = held[pl.ds(pl.multiple_of(dev * rows + pl.program_id(0) * strip, 16), strip), :].astype(f32)
            for part, out in enumerate(outs):
                out[:, dev * cols : (dev + 1) * cols] = block[:, part * cols : (part + 1) * cols]

    steps = 4
    return pl.pallas_call(
        kernel,
        grid_spec=pltpu.PrefetchScalarGridSpec(
            num_scalar_prefetch=1,
            grid=(steps,),
            in_specs=[ANY] * len(arrays),
            out_specs=[pl.BlockSpec((shard // steps, count * cols), lambda g, me: (g, 0))] * parts
            + [pl.BlockSpec((count, 16, wide), lambda g, me: (0, 0, 0))],
            scratch_shapes=[pltpu.VMEM((count * rows, wide), bf16), pltpu.SemaphoreType.DMA((len(arrays),))],
        ),
        out_shape=[jax.ShapeDtypeStruct((shard, count * cols), f32)] * parts
        + [jax.ShapeDtypeStruct((count, 16, wide), bf16)],
        compiler_params=LIMIT,
        cost_estimate=takes(6.0),
    )(me, *arrays)


def own_attention(w_query, w_key, w_value, w_forget, forget_bias, w_out, gains, heads, me, level):
    shard = w_query.shape[0]
    cols = heads * HEAD_DIM
    each_level = forget_bias.shape[0]

    def kernel(at, wq, wk, wv, wo, wf, gain_one, gain_two, bias, out):
        for odd in range(2):

            @pl.when(at[0] % 2 == odd)
            def _():
                for i, w in enumerate((wq, wk, wv, wo)):
                    out[:shard, i * cols : (i + 1) * cols] = w[:, odd * cols : (odd + 1) * cols]

        row = lax.broadcasted_iota(jnp.int32, (16, shard), 0)
        gain_one, gain_two = (jnp.broadcast_to(g[...].astype(f32)[None], (16, shard)) for g in (gain_one, gain_two))
        rows = jnp.where(row == 0, gain_one, jnp.where(row == 1, gain_two, 0.0))
        head = lax.broadcasted_iota(jnp.int32, (16, HEADS), 1)
        slot = lax.broadcasted_iota(jnp.int32, (16, HEADS), 0)
        chosen = ((head == at[0] * heads + slot - 2) & (slot >= 2) & (slot < heads + 2)).astype(bf16)
        out[shard:, :shard] = (rows + dot(chosen, wf[...])).astype(bf16)
        row = lax.broadcasted_iota(jnp.int32, (16, each_level), 0)
        lane = lax.broadcasted_iota(jnp.int32, (16, each_level), 1)
        mine = (at[1] * each_level + lane == at[0] * heads + row) & (row < heads)
        column = jnp.sum(jnp.where(mine, bias[...].astype(f32), 0.0), axis=1, keepdims=True)
        out[shard:, shard:] = jnp.broadcast_to(column, (16, 4 * cols - shard)).astype(bf16)

    pair = pl.BlockSpec((shard, 2 * cols), lambda i, at: (0, at[0] // 2))
    line = pl.BlockSpec((shard,), lambda i, at: (0,))

    def whole(*shape):
        return pl.BlockSpec(shape, lambda i, at: (0, 0))

    return pl.pallas_call(
        kernel,
        grid_spec=pltpu.PrefetchScalarGridSpec(
            num_scalar_prefetch=1,
            grid=(1,),
            in_specs=[pair] * 4 + [whole(HEADS, shard), line, line, whole(1, each_level)],
            out_specs=whole(shard + 16, 4 * cols),
        ),
        out_shape=jax.ShapeDtypeStruct((shard + 16, 4 * cols), bf16),
        compiler_params=LARGE,
        cost_estimate=takes(3.0),
    )(
        jnp.stack([me, level]), w_query, w_key, w_value, w_out, w_forget.T, *gains, forget_bias.reshape(1, -1)
    )


def norm_project(pieces, pack, axis, seqs, cols):
    arrays = [p[3] for p in pieces]
    rows, width = arrays[0].shape[0] // seqs, arrays[0].shape[1]
    count, depth, wide = 8, pack.shape[0], pack.shape[2]
    shard = width // depth
    tokens = seqs * count * rows
    tile, heads = 2 * rows, cols // HEAD_DIM
    me = lax.axis_index(axis).reshape(1)

    def slots(dev):
        return [(s * rows, rows, (s * count + dev) * rows) for s in range(seqs)]

    number = len(slices_of(pieces, 0, slots))

    def kernel(me, pack_ref, *refs):
        x_out, out, qkv_out, raw_out, held, weights, turned, small, gain, sems = refs[-10:]
        step = pl.program_id(0)

        @pl.when(step == 0)
        def _():
            copies = []
            for z in range(depth):
                copies.append((pack_ref.at[z, pl.ds(0, shard)], rows_at(weights, z * shard, shard)))
                copies.append((pack_ref.at[z, pl.ds(pack.shape[1] - 16, 16)], small.at[z]))
            for k, s, size, t in slices_of(pieces, me[0], slots):
                copies.append((refs[k].at[pl.ds(s, size)], rows_at(held, t, size)))
            copy_all(copies, sems)
            turned[: 3 * cols, :] = weights[:, : 3 * cols].T
            row = lax.broadcasted_iota(jnp.int32, (16, shard), 0)
            for z in range(depth):
                at = slice(z * shard, (z + 1) * shard)
                rows = small[z, :, :shard].astype(f32)
                gain[:, at] = rows
                moved = jnp.concatenate([rows[2:], rows[:2]], axis=0)
                turned[3 * cols :, at] = jnp.where(row < heads, moved, 0.0).astype(bf16)

        bias = sum(small[z, :, shard:].astype(f32) for z in range(depth))[:, :1]
        block = held[pl.ds(pl.multiple_of(step * tile, tile), tile), :]
        x_out[...] = block
        x = block.astype(f32)
        normed = (x * inverse_rms(x) * gain[:1, :]).astype(bf16)
        out[...] = normed
        projected = dot_t(turned[...], normed)
        qkv_out[...] = projected[: 3 * cols].astype(bf16)
        raw_out[...] = projected[3 * cols :] + bias

    spec = pl.BlockSpec((tile, width), lambda p, me: (p, 0))
    shape = jax.ShapeDtypeStruct((tokens, width), bf16)
    return pl.pallas_call(
        kernel,
        grid_spec=pltpu.PrefetchScalarGridSpec(
            num_scalar_prefetch=1,
            grid=(tokens // tile,),
            in_specs=[ANY] * (1 + len(arrays)),
            out_specs=[
                spec,
                spec,
                pl.BlockSpec((3 * cols, tile), lambda p, me: (0, p)),
                pl.BlockSpec((16, tile), lambda p, me: (0, p)),
            ],
            scratch_shapes=[
                pltpu.VMEM((tokens, width), bf16),
                pltpu.VMEM((width, wide), bf16),
                pltpu.VMEM((3 * cols + 16, width), bf16),
                pltpu.VMEM((depth, 16, wide), bf16),
                pltpu.VMEM((16, width), f32),
                pltpu.SemaphoreType.DMA((number + 2 * depth,)),
            ],
        ),
        out_shape=[
            shape,
            shape,
            jax.ShapeDtypeStruct((3 * cols, tokens), bf16),
            jax.ShapeDtypeStruct((16, tokens), f32),
        ],
        compiler_params=LIMIT,
        cost_estimate=takes(12.0),
    )(me, pack, *arrays)


def hidden_norm(x_all, mixed_all, w_out, gain, seqs, rows, axis, turned):
    tokens, width = x_all.shape
    tile = 2 * rows
    tiles = tokens // seqs // tile
    me = lax.axis_index(axis).reshape(1)

    def kernel(me, x_ref, mixed_ref, w_ref, gain_ref, out_ref, own_ref, hidden_ref):
        hidden = x_ref[...].astype(f32) + (dot_t if turned else dot)(mixed_ref[...].T, w_ref[...])
        out_ref[...] = (hidden * inverse_rms(hidden) * gain_ref[...]).astype(bf16)

        @pl.when(pl.program_id(1) == me[0] // 2)
        def _():
            hidden_ref[...] = hidden
            own_ref[...] = hidden_ref[pl.ds(pl.multiple_of(me[0] % 2 * rows, rows), rows), :]

    return pl.pallas_call(
        kernel,
        grid_spec=pltpu.PrefetchScalarGridSpec(
            num_scalar_prefetch=1,
            grid=(seqs, tiles),
            in_specs=[
                pl.BlockSpec((tile, width), lambda s, t, me: (s * tiles + t, 0)),
                pl.BlockSpec((width, tile), lambda s, t, me: (0, s * tiles + t)),
                pl.BlockSpec((width, width), lambda s, t, me: (0, 0)),
                pl.BlockSpec((1, width), lambda s, t, me: (0, 0)),
            ],
            out_specs=[
                pl.BlockSpec((tile, width), lambda s, t, me: (s * tiles + t, 0)),
                pl.BlockSpec((rows, width), lambda s, t, me: (s, 0)),
            ],
            scratch_shapes=[pltpu.VMEM((tile, width), f32)],
        ),
        out_shape=[jax.ShapeDtypeStruct((tokens, width), bf16), jax.ShapeDtypeStruct((seqs * rows, width), f32)],
        compiler_params=LIMIT,
        cost_estimate=takes(17.0),
    )(me, x_all, mixed_all, w_out, gain.reshape(1, width))


def split_pair(value, keep_ref, send_ref, me):
    rows = value.shape[0] // 4
    blocks = [value[i * rows : (i + 1) * rows] for i in range(4)]
    core, side = me % 2 == 0, me // 2 % 2 == 0
    for t in range(2):
        first, second = (jnp.where(side, blocks[2 * t + c], blocks[2 - 2 * t + c]) for c in range(2))
        keep_ref[t] = jnp.where(core, first, second).astype(bf16)
        send_ref[t] = jnp.where(core, second, first).astype(bf16)


def pair_specs(paired, tile, tiles, width):
    if paired:
        block = pl.BlockSpec((2, tile // 4, width), lambda t, me: (t, 0, 0))
        shape = jax.ShapeDtypeStruct((2 * tiles, tile // 4, width), bf16)
        return (lambda t, me: me[0] // 4 ^ t), [block] * 2, [shape] * 2
    block = pl.BlockSpec((tile, width), lambda t, me: (t, 0))
    return (lambda t, me: t), [block], [jax.ShapeDtypeStruct((tiles * tile, width), bf16)]


def feed_forward(normed, cot, mlp, axis, seq, seqs, own):
    tokens, width = normed.shape
    depth, packed, ff_cols = mlp.shape
    shard = width // depth
    paired = lax.axis_size(axis) == 8
    tile = 512
    tiles = tokens // seqs // tile
    at, specs, shapes = pair_specs(paired, tile, tiles, width)
    blocks = width // ff_cols
    me = lax.axis_index(axis).reshape(1)

    def kernel(me, normed_ref, cot_ref, mlp_ref, inner_ref, grads_ref, *refs):
        outs, (gate_up, down, sems) = refs[:-3], refs[-3:]

        @pl.when(pl.program_id(0) == 0)
        def _():
            copies = []
            for z in range(depth):
                for part in range(2):
                    copies.append(
                        (
                            mlp_ref.at[z, pl.ds(part * shard, shard)],
                            gate_up.at[pl.ds(z * shard, shard), pl.ds(part * ff_cols, ff_cols)],
                        )
                    )
                for k in range(blocks):
                    copies.append(
                        (
                            mlp_ref.at[z, pl.ds(2 * shard + k * own, own)],
                            down.at[pl.ds(z * own, own), pl.ds(k * ff_cols, ff_cols)],
                        )
                    )
            copy_all(copies, sems)

        both = dot(normed_ref[...], gate_up[...])
        grad_inner = dot_t(cot_ref[...], down[...])
        gate, up = both[:, :ff_cols], both[:, ff_cols:]
        sig = jax.nn.sigmoid(gate)
        silu = gate * sig
        inner = (silu * up).astype(bf16)
        inner_ref[...] = inner
        grads_ref[:, :ff_cols] = (grad_inner * up * sig * (1.0 + gate * (1.0 - sig))).astype(bf16)
        grads_ref[:, ff_cols:] = (grad_inner * silu).astype(bf16)
        back = dot_t(grads_ref[...], gate_up[...])
        result = dot(inner, down[...])
        if paired:
            split_pair(back, outs[0], outs[1], me[0])
            split_pair(result, outs[2], outs[3], me[0])
        else:
            outs[0][...] = back.astype(bf16)
            outs[1][...] = result.astype(bf16)

    rows = pl.BlockSpec((tile, width), lambda t, me: (seq * tiles + at(t, me), 0))
    length = tokens // seqs

    def own_rows(cols):
        return pl.BlockSpec((tile, cols), lambda t, me: (at(t, me), 0))

    return pl.pallas_call(
        kernel,
        grid_spec=pltpu.PrefetchScalarGridSpec(
            num_scalar_prefetch=1,
            grid=(tiles,),
            in_specs=[rows, rows, ANY],
            out_specs=[own_rows(ff_cols), own_rows(2 * ff_cols)] + specs * 2,
            scratch_shapes=[
                pltpu.VMEM((width, 2 * ff_cols), bf16),
                pltpu.VMEM((ff_cols, width), bf16),
                pltpu.SemaphoreType.DMA((depth * (2 + blocks),)),
            ],
        ),
        out_shape=[
            jax.ShapeDtypeStruct((length, ff_cols), bf16),
            jax.ShapeDtypeStruct((length, 2 * ff_cols), bf16),
        ]
        + shapes * 2,
        compiler_params=LIMIT,
        cost_estimate=takes(17.0),
    )(me, normed, cot, mlp)


def project_back(grads, raw, pack, width, axis, seqs):
    cols, tokens = grads[0].shape
    depth, wide = pack.shape[0], pack.shape[2]
    shard, heads = width // depth, cols // HEAD_DIM
    tile = 512
    tiles = tokens // seqs // tile
    at, specs, shapes = pair_specs(True, tile, tiles, width)
    me = lax.axis_index(axis).reshape(1)

    def kernel(me, gq, gk, gv, raw, pack_ref, *refs):
        outs, (weights, small, turned, sems) = refs[:-4], refs[-4:]

        @pl.when((pl.program_id(0) == 0) & (pl.program_id(1) == 0))
        def _():
            copies = []
            for z in range(depth):
                copies.append((pack_ref.at[z, pl.ds(0, shard), pl.ds(0, 5 * 128)], rows_at(weights, z * shard, shard)))
                copies.append((pack_ref.at[z, pl.ds(shard, 16)], small.at[z]))
            copy_all(copies, sems)
            for z in range(depth):
                forget = jnp.concatenate(
                    [small[z, 2 : 2 + heads, :shard].astype(f32), jnp.zeros((EXTRA - heads, shard), f32)], axis=0
                )
                weights[z * shard : (z + 1) * shard, 3 * cols :] = forget.T.astype(bf16)

        for i, part in enumerate((gq, gk, gv)):
            turned[i * cols : (i + 1) * cols, :] = part[...]
        turned[3 * cols : 3 * cols + 16, :] = raw[...].astype(bf16)
        turned[3 * cols + 16 :, :] = jnp.zeros((EXTRA - 16, tile), bf16)
        back = dot_t(turned[...].T, weights[...])
        for s in range(seqs):

            @pl.when(pl.program_id(0) == s)
            def _():
                split_pair(back, outs[2 * s], outs[2 * s + 1], me[0])

    def seq_block(s):
        return pl.BlockSpec(
            (2, tile // 4, width), lambda q, t, me: (jnp.where(q == s, t, jnp.where(q < s, 0, tiles - 1)), 0, 0)
        )

    def columns(rows):
        return pl.BlockSpec((rows, tile), lambda s, t, me: (0, s * tiles + at(t, me)))

    return pl.pallas_call(
        kernel,
        grid_spec=pltpu.PrefetchScalarGridSpec(
            num_scalar_prefetch=1,
            grid=(seqs, tiles),
            in_specs=[columns(cols)] * 3 + [columns(16), ANY],
            out_specs=[seq_block(s) for s in range(seqs) for _ in range(2)],
            scratch_shapes=[
                pltpu.VMEM((width, 3 * cols + EXTRA), bf16),
                pltpu.VMEM((depth, 16, wide), bf16),
                pltpu.VMEM((3 * cols + EXTRA, tile), bf16),
                pltpu.SemaphoreType.DMA((2 * depth,)),
            ],
        ),
        out_shape=shapes * seqs,
        compiler_params=LIMIT,
        cost_estimate=takes(11.0),
    )(me, *grads, raw, pack)


def attention_grads(grads, raw, normed, branch, mixed, gain_row, pack, axis, seqs, depth, heads, each_level):
    cols, tokens = grads[0].shape
    width = normed.shape[1]
    shard = width // depth
    count, own_out, piece = branch.shape
    wide = pack.shape[2]
    me = lax.axis_index(axis).reshape(1)
    part = piece // seqs

    def kernel(me, gq, gk, gv, raw, normed_ref, branch_ref, mixed_ref, gain_ref, pack_ref, small_ref, out, turned, branches):
        z = pl.program_id(0)

        @pl.when(z == 0)
        def _():
            for i, g in enumerate((gq, gk, gv)):
                turned[i * cols : (i + 1) * cols, :] = g[...]
            turned[3 * cols :, :] = raw[...].astype(bf16)
            for dev in range(count):
                for s in range(seqs):
                    to = (s * count + dev) * part
                    branches[:, to : to + part] = branch_ref[dev, :, s * part : (s + 1) * part]

        grad = dot(turned[...], normed_ref[...])
        forget = grad[3 * cols :]
        columns = grad[: 3 * cols].T
        out[0, :shard, : 3 * cols] = columns.astype(bf16)
        out[0, :shard, 3 * cols :] = dot_t(mixed_ref[...], branches[...]).astype(bf16)
        by_row = jnp.sum(columns * pack_ref[0, :, : 3 * cols].astype(f32), axis=1, keepdims=True)
        by_row = jnp.broadcast_to(by_row, (shard, 8)).T[:1]
        small = small_ref[0, :, :shard].astype(f32)
        by_row = by_row + jnp.sum(forget[:heads] * small[2 : 2 + heads], axis=0, keepdims=True)
        row = lax.broadcasted_iota(jnp.int32, (16, shard), 0)
        lane = lax.broadcasted_iota(jnp.int32, (16, shard), 1)
        more = jnp.where(row == heads, gain_ref[...], jnp.where(row == heads + 2, by_row / small[:1], 0.0))
        sums = jnp.sum(raw[...], axis=1, keepdims=True)
        for h in range(heads):
            head = me[0] * heads + h
            at = head // each_level * shard + head % each_level - z * shard
            more = more + jnp.where((row == heads + 1) & (lane == at), sums[h : h + 1, :], 0.0)
        out[0, shard : shard + 16, :shard] = jnp.where(row < heads, forget, more).astype(bf16)
        out[0, shard : shard + 16, shard:] = jnp.zeros((16, wide - shard), bf16)
        out[0, shard + 16 :, :] = jnp.zeros((16, wide), bf16)

    def whole(*shape):
        return pl.BlockSpec(shape, lambda z, me: (0,) * len(shape))

    return pl.pallas_call(
        kernel,
        grid_spec=pltpu.PrefetchScalarGridSpec(
            num_scalar_prefetch=1,
            grid=(depth,),
            in_specs=[whole(cols, tokens)] * 3
            + [
                whole(16, tokens),
                pl.BlockSpec((tokens, shard), lambda z, me: (0, z)),
                whole(count, own_out, piece),
                pl.BlockSpec((shard, tokens), lambda z, me: (z, 0)),
                pl.BlockSpec((1, shard), lambda z, me: (0, z)),
                pl.BlockSpec((1, shard, wide), lambda z, me: (z, 0, 0)),
                pl.BlockSpec((1, 16, wide), lambda z, me: (z, shard // 16, 0)),
            ],
            out_specs=pl.BlockSpec((1, shard + 32, wide), lambda z, me: (z, 0, 0)),
            scratch_shapes=[pltpu.VMEM((3 * cols + 16, tokens), bf16), pltpu.VMEM((own_out, tokens), bf16)],
        ),
        out_shape=jax.ShapeDtypeStruct((depth, shard + 32, wide), bf16),
        compiler_params=LIMIT,
        cost_estimate=takes(12.0),
    )(me, *grads, raw, normed, branch, mixed, gain_row, pack, pack)


def out_turned(pack, cols, shard):
    depth, rows, wide = pack.shape

    def kernel(pack_ref, out):
        out[...] = pack_ref[0, :, 3 * cols :].T

    return pl.pallas_call(
        kernel,
        grid=(depth,),
        in_specs=[pl.BlockSpec((1, shard, wide), lambda z: (z, 0, 0))],
        out_specs=pl.BlockSpec((cols, shard), lambda z: (0, z)),
        out_shape=jax.ShapeDtypeStruct((cols, depth * shard), bf16),
        compiler_params=SMALL,
        cost_estimate=takes(2),
    )(pack)


def own_kernel(me, gate, up, down, out):
    rows, own = gate.shape[0], down.shape[0]
    out[:rows, :] = gate[...]
    out[rows : 2 * rows, :] = up[...]
    for k in range(down.shape[1] // (128 * pl.num_programs(0))):
        at = (k * pl.num_programs(0) + pl.program_id(0)) * 128
        out[2 * rows + k * own : 2 * rows + (k + 1) * own, :] = down[:, pl.ds(pl.multiple_of(at, 128), 128)]


def own_mlp(w_gate, w_up, w_down, depth, count, me):
    shard, ff = w_gate.shape
    own = w_down.shape[0] // count
    width = w_down.shape[1]
    ff_cols = depth * own
    if own == 128:
        strip = pl.BlockSpec((shard, 128), lambda z, me: (0, z * count + me[0]))
        total = 2 * shard + own * width // ff_cols
        return pl.pallas_call(
            own_kernel,
            grid_spec=pltpu.PrefetchScalarGridSpec(
                num_scalar_prefetch=1,
                grid=(depth,),
                in_specs=[strip, strip, pl.BlockSpec((own, width), lambda z, me: (me[0], 0))],
                out_specs=pl.BlockSpec((total, 128), lambda z, me: (0, z)),
            ),
            out_shape=jax.ShapeDtypeStruct((total, ff_cols), bf16),
            cost_estimate=takes(4.0),
        )(me.reshape(1), w_gate, w_up, w_down)

    def ff_columns(w):
        w = w.reshape(shard, depth, count, own)
        return lax.dynamic_index_in_dim(w, me, 2, keepdims=False).reshape(shard, ff_cols)

    down = lax.dynamic_slice_in_dim(w_down, me * own, own, 0)
    return jnp.concatenate([ff_columns(w_gate), ff_columns(w_up), stack_columns(down, ff_cols)], axis=0)


def contract(a, b, da, db):
    return lax.dot_general(a, b, (((da,), (db,)), ((), ())), preferred_element_type=f32)


def stack_columns(a, width):
    return jnp.concatenate([a[:, i : i + width] for i in range(0, a.shape[1], width)], axis=0)


def to_shards(grad):
    return lax.psum_scatter(grad, "fsdp", scatter_dimension=0, tiled=True)


def local_eight(
    inputs,
    gain_attn,
    w_query,
    w_key,
    w_value,
    w_forget,
    forget_bias,
    w_out,
    gain_mlp,
    w_gate,
    w_up,
    w_down,
    cotangent,
):
    axis = "ctx"
    count, me = lax.axis_size(axis), lax.axis_index(axis)
    depth, level = lax.axis_size("fsdp"), lax.axis_index("fsdp")
    seqs, rows, width = inputs.shape
    tokens = seqs * count * rows
    shard = width // depth
    heads = HEADS // count
    cols = heads * HEAD_DIM
    ff_own = w_down.shape[0] // count
    ff_cols = depth * ff_own
    own_out = width // count
    flat_in, flat_cot = inputs.reshape(seqs * rows, width), cotangent.reshape(seqs * rows, width)

    def token_slots(dev):
        return [(s * rows, rows, (s * count + dev) * rows) for s in range(seqs)]

    x_state = gather_start(flat_in, axis)
    own = own_attention(
        w_query, w_key, w_value, w_forget, forget_bias, w_out, (gain_attn, gain_mlp), heads, me, level
    )
    pack = lax.all_gather(own, "fsdp", axis=0)
    x_far = gather_far(x_state, axis)
    mlp = lax.all_gather(own_mlp(after(w_gate, x_far[3:]), w_up, w_down, depth, count, me), "fsdp", axis=0)
    g_state = gather_start(after(flat_cot, x_far[3:]), axis)
    x_pieces = gather_core_once(x_far, axis)
    pack = after(pack, g_state[1:])
    g_state = gather_far(g_state, axis)
    out_state = gather_start(out_turned(pack, cols, shard), axis)
    gains = pack[:, shard : shard + 2, :shard].astype(f32)
    gain_one, gain_two = gains[:, 0].reshape(width), gains[:, 1].reshape(width)

    x_all, normed, qkv, gate_raw = norm_project(x_pieces, pack, axis, seqs, cols)
    attn, mixed, totals, decay = attend(qkv, gate_raw, seqs, heads)
    mixed, g_state, out_state = lax.optimization_barrier((mixed, g_state, out_state))
    out_state = gather_far(out_state, axis)
    mixed_state = gather_start(mixed, axis)
    g_pieces = gather_core_once(g_state, axis)
    g_all = place(g_pieces, axis, tokens, token_slots)
    out_full = place(gather_core_once(out_state, axis), axis, width, lambda dev: [(0, own_out, dev * own_out)])
    mixed_state = gather_far(after(mixed_state, (g_all, out_full)), axis)
    mixed_pieces = gather_core(mixed_state, axis)
    mixed_all = place(mixed_pieces, axis, width, lambda dev: [(0, cols, dev * cols)])
    normed_two, hidden_own = hidden_norm(x_all, mixed_all, out_full, gain_two, seqs, rows, axis, True)

    sides = [feed_forward(normed_two, g_all, mlp, axis, s, seqs, ff_own) for s in range(seqs)]
    inner = jnp.concatenate([side[0] for side in sides], axis=0)
    gate_up_grads = jnp.concatenate([side[1] for side in sides], axis=0)
    back = Sums([side[2:4] for side in sides], axis)
    grad_down = back.hold(contract(inner, g_all, 0, 0).astype(bf16))
    back.first()
    normed_two = back.hold(normed_two)
    back.send_first()
    result = Sums([after(side[4:6], normed_two) for side in sides], axis)
    grad_gate_up = result.hold(contract(normed_two, gate_up_grads, 0, 0).astype(bf16))
    result.first()
    grad_gate_up, result.moving = back.hold((grad_gate_up, result.moving))
    back.second()
    back.send_second()
    back = back.result()
    grad_down, grad_gate_up = to_shards(grad_down), to_shards(grad_gate_up)

    grad_from_norm, grad_gain_two = norm_pull(hidden_own, gain_two, back)
    grad_hidden = flat_cot.astype(f32) + grad_from_norm
    branch = grad_hidden.astype(bf16)
    grad_mixed = contract(out_full, branch, 0, 1).astype(bf16).reshape(count, cols, seqs * rows)
    branch = after(branch, grad_mixed).T.reshape(count, own_out, seqs * rows)
    grad_mixed = result.hold(grad_mixed)
    grad_mixed = lax.all_to_all(grad_mixed, axis, 0, 0, tiled=True)
    result.send_first()
    grad_mixed, grad_down, branch = lax.optimization_barrier((grad_mixed, grad_down, branch))
    branch = lax.all_to_all(branch, axis, 0, 0, tiled=True)
    down_state = gather_start(grad_down, axis)
    gq, gk, gv, grad_raw = attend_pull(qkv, decay, grad_mixed, attn, totals, gate_raw, seqs, heads)

    down_state, branch, grad_gate_up, grad_raw = result.hold((down_state, branch, grad_gate_up, grad_raw))
    gate_up_state = gather_start(grad_gate_up, axis)
    down_state = gather_far(down_state, axis)
    grads = (gq, gk, gv)
    grad_pack = attention_grads(
        grads, grad_raw, normed, branch, mixed_all, grad_gain_two[None], pack, axis, seqs, depth, heads, HEADS // depth
    )
    grad_raw, down_state, gate_up_state, _ = lax.optimization_barrier((grad_raw, down_state, gate_up_state, grad_pack))
    gate_up_state = gather_far(gate_up_state, axis)
    result.hold(grad_pack)
    result.second()
    grad_raw = result.hold(grad_raw)
    result.send_second()
    down_pieces = gather_core(down_state, axis)
    pairs = project_back(grads, grad_raw, pack, width, axis, seqs)
    grad_pack = to_shards(grad_pack.reshape(-1, 4 * cols))
    pairs, gate_up_state, down_pieces = held(pairs, gate_up_state, down_pieces)
    grad_normed = Sums([pairs[2 * s : 2 * s + 2] for s in range(seqs)], axis)
    grad_normed.first()
    gate_up_state = result.hold(grad_normed.hold(gate_up_state))
    grad_normed.send_first()
    gate_up_pieces = gather_core(gate_up_state, axis)
    grad_down = place_wide(down_pieces, axis)
    grad_gate, grad_up = place_columns(gate_up_pieces, axis, depth, 2)
    grad_pack, _ = grad_normed.hold((grad_pack, (grad_down, grad_gate)))
    grad_normed.second()
    grad_normed.send_second()
    pack_state = gather_start(grad_pack, axis)
    pack_state = grad_normed.hold(pack_state)
    pack_state = gather_far(pack_state, axis)
    grad_in, _ = norm_pull(flat_in.astype(f32), gain_one, grad_normed.result())
    input_grad = (grad_hidden + grad_in).reshape(seqs, rows, width)
    output = (hidden_own + result.result()).astype(bf16).reshape(seqs, rows, width)
    pack_pieces = gather_core(after(pack_state, (input_grad, output)), axis)
    grad_query, grad_key, grad_value, grad_out, tail = place_heads(pack_pieces, axis, shard, cols)
    tail = tail[:, :, :shard].astype(f32)
    tail_sum = jnp.sum(tail[:, heads : heads + 3], axis=0)
    return (
        output,
        input_grad,
        tail_sum[2],
        grad_query,
        grad_key,
        grad_value,
        tail[:, :heads].reshape(HEADS, shard).T,
        tail_sum[1, : forget_bias.shape[0]],
        grad_out,
        tail_sum[0],
        grad_gate,
        grad_up,
        grad_down,
    )


def local_any(
    inputs,
    gain_attn,
    w_query,
    w_key,
    w_value,
    w_forget,
    forget_bias,
    w_out,
    gain_mlp,
    w_gate,
    w_up,
    w_down,
    cotangent,
):
    axis = "ctx"
    count, me = lax.axis_size(axis), lax.axis_index(axis)
    depth, level = lax.axis_size("fsdp"), lax.axis_index("fsdp")
    seqs, rows, width = inputs.shape
    tokens = seqs * count * rows
    shard = width // depth
    heads = -(-HEADS // count)
    cols = heads * HEAD_DIM
    ff_own = w_down.shape[0] // count
    ff_cols = depth * ff_own
    out_rows, own_out = shard // count, width // count
    flat_in, flat_cot = inputs.reshape(seqs * rows, width), cotangent.reshape(seqs * rows, width)

    def own_columns(w, each_head):
        w = jnp.pad(w, ((0, 0), (0, count * heads * each_head - w.shape[1])))
        return lax.dynamic_slice_in_dim(w, me * heads * each_head, heads * each_head, 1)

    extra = [own_columns(w_forget, 1), gain_attn[:, None], gain_mlp[:, None]]
    extra += [jnp.pad(forget_bias, (0, shard - forget_bias.shape[0]))[:, None]]
    extra += [jnp.zeros((shard, EXTRA - heads - 3), bf16)]
    pack = [own_columns(w, HEAD_DIM) for w in (w_query, w_key, w_value)] + extra
    pack = lax.all_gather(jnp.concatenate(pack, axis=1), "fsdp", axis=0, tiled=True)
    extra = pack[:, 3 * cols :]
    gain_one = extra[:, heads].astype(f32)
    gain_two = extra[:, heads + 1].astype(f32)
    biases = extra[:, heads + 2].reshape(depth, shard)[:, : forget_bias.shape[0]].reshape(-1)
    biases = jnp.pad(biases, (0, count * heads - HEADS))
    bias = lax.dynamic_slice_in_dim(biases, me * heads, heads).astype(f32)
    out_own = lax.all_gather(lax.dynamic_slice_in_dim(w_out, me * out_rows, out_rows, 0), "fsdp", axis=0)
    out_full = lax.all_gather(out_own, axis, axis=1).reshape(width, width)
    mlp = lax.all_gather(own_mlp(w_gate, w_up, w_down, depth, count, me), "fsdp", axis=0)

    x_all = lax.all_gather(inputs, axis, axis=1, tiled=True).reshape(tokens, width)
    x_wide = x_all.astype(f32)
    normed = (x_wide * inverse_rms(x_wide) * gain_one).astype(bf16)
    g_all = lax.all_gather(after(cotangent, normed), axis, axis=1, tiled=True).reshape(tokens, width)
    qkv = contract(pack[:, : 3 * cols], normed, 0, 1).astype(bf16)
    gate_raw = contract(extra, normed, 0, 1)[:heads] + bias[:, None]
    gate_raw = jnp.pad(gate_raw, ((0, -heads % 16), (0, 0)))
    attn, mixed, totals, decay = attend(qkv, gate_raw, seqs, heads)
    mixed_all = lax.all_gather(mixed, axis, axis=0, tiled=True)[:width]
    normed_two, hidden_own = hidden_norm(x_all, mixed_all, out_full, gain_two, seqs, rows, axis, False)

    def summed(part):
        return lax.psum_scatter(part.reshape(count, rows, width), axis, scatter_dimension=0).astype(f32)

    sides, sums = [], []
    for s in range(seqs):
        side = feed_forward(normed_two, g_all, mlp, axis, s, seqs, ff_own)
        sides.append(side[:2])
        sums.append([summed(side[2]), summed(side[3])])
        normed_two = after(normed_two, sums[s])
    back, result = (jnp.concatenate(parts, axis=0) for parts in zip(*sums))
    inner = jnp.concatenate([side[0] for side in sides], axis=0)
    gate_up_grads = jnp.concatenate([side[1] for side in sides], axis=0)
    grad_down = to_shards(contract(inner, g_all, 0, 0).astype(bf16))
    grad_gate_up = to_shards(contract(normed_two, gate_up_grads, 0, 0).astype(bf16))
    output = (hidden_own + result).astype(bf16)

    grad_from_norm, grad_gain_two = norm_pull(hidden_own, gain_two, back)
    grad_hidden = flat_cot.astype(f32) + grad_from_norm
    branch = grad_hidden.astype(bf16)
    grad_mixed = contract(out_full, branch, 1, 1).astype(bf16)
    grad_mixed = jnp.pad(grad_mixed, ((0, count * cols - width), (0, 0)))
    grad_mixed = lax.all_to_all(grad_mixed.reshape(count, cols, seqs * rows), axis, 0, 0, tiled=True)
    branch = lax.all_to_all(branch.T.reshape(count, own_out, seqs * rows), axis, 0, 0, tiled=True)
    branch = branch.reshape(count, own_out, seqs, rows).transpose(1, 2, 0, 3).reshape(own_out, tokens)
    grad_out = contract(branch, mixed_all, 1, 1)
    gq, gk, gv, grad_raw = attend_pull(qkv, decay, grad_mixed, attn, totals, gate_raw, seqs, heads)
    grad_raw = jnp.pad(grad_raw[:heads].astype(bf16), ((0, EXTRA - heads), (0, 0)))
    grads = jnp.concatenate([gq, gk, gv, grad_raw], axis=0)
    grad_normed = contract(grads, pack, 0, 1).astype(bf16).reshape(seqs, count * rows, width)
    grad_normed = jnp.concatenate([summed(part) for part in grad_normed], axis=0)

    grad_pack = contract(grads, normed, 1, 0)
    head_at = me * heads + jnp.arange(heads)
    bias_col = head_at // (HEADS // depth) * shard + head_at % (HEADS // depth)
    bias_sum = jnp.where(head_at < HEADS, jnp.sum(grad_raw[:heads].astype(f32), axis=1), 0.0)
    at_col = jnp.arange(width)[None, :] == bias_col[:, None]
    bias_row = jnp.sum(jnp.where(at_col, bias_sum[:, None], 0.0), axis=0, keepdims=True)
    tail = [grad_pack[3 * cols : 3 * cols + heads], grad_gain_two[None], bias_row]
    tail += [jnp.zeros((EXTRA - heads - 2, width), f32)]
    grad_pack = jnp.concatenate([grad_pack[: 3 * cols]] + tail + [grad_out], axis=0).astype(bf16)
    grad_pack = to_shards(grad_pack.reshape(-1, depth, shard).transpose(1, 0, 2).reshape(-1, shard))
    grad_pack = lax.all_gather(grad_pack, axis)
    out_at = 3 * cols + EXTRA

    def turned(start, size):
        return grad_pack[:, start : start + size].reshape(-1, shard)[:width].T.astype(f32)

    tail = grad_pack[:, 3 * cols : out_at].astype(f32)
    tail_sum = jnp.sum(tail[:, heads : heads + 2], axis=0)
    grad_down = lax.all_gather(grad_down, axis, axis=0, tiled=True).astype(f32)
    grad_gate_up = lax.all_gather(grad_gate_up.reshape(shard, 2, depth, ff_own), axis)
    grad_gate_up = grad_gate_up.transpose(2, 1, 3, 0, 4).reshape((2,) + w_gate.shape).astype(f32)
    grad_in, grad_gain_one = norm_pull(flat_in.astype(f32), gain_one, grad_normed)
    grad_gain_one = lax.psum(grad_gain_one, (axis, "fsdp"))
    return (
        output.reshape(seqs, rows, width),
        (grad_hidden + grad_in).reshape(seqs, rows, width),
        lax.dynamic_slice_in_dim(grad_gain_one, level * shard, shard),
        turned(0, cols),
        turned(cols, cols),
        turned(2 * cols, cols),
        tail[:, :heads].reshape(count * heads, shard)[:HEADS].T,
        tail_sum[1, : forget_bias.shape[0]],
        turned(out_at, own_out),
        tail_sum[0],
        grad_gate_up[0],
        grad_gate_up[1],
        grad_down,
    )


def solution(mesh):
    split, first, rest = P("fsdp", "ctx", None), P("fsdp"), P("fsdp", None)
    return jax.shard_map(
        local_eight if mesh.shape["ctx"] == 8 else local_any,
        mesh=mesh,
        in_specs=(split, first, rest, rest, rest, rest, first, rest, first, rest, rest, rest, split),
        out_specs=(split, split, first, rest, rest, rest, rest, first, rest, first, rest, rest, rest),
        check_vma=False,
    )
```

```python
import jax
import jax.numpy as jnp
from jax import lax
from jax.experimental import pallas as pl
from jax.experimental.pallas import tpu as pltpu
from jax.sharding import PartitionSpec as P

HEADS = 24
HEAD_DIM = 64
BLK = 256
EXTRA = 64
norm_eps = 1e-06
bf16 = jnp.bfloat16
f32 = jnp.float32


def exchange(x, axis, mask):
    return lax.ppermute(x, axis, [(i, i ^ mask) for i in range(lax.axis_size(axis))])


def after(x, done):
    return lax.optimization_barrier((x, done))[0]


def first_half(rows):
    return -(-rows // 32) * 16


def gather_start(x, axis):
    return x, exchange(x, axis, 2), exchange(x, axis, 4)


def gather_far(state, axis):
    x, side, above = state
    half = first_half(x.shape[0])
    return x, side, above, exchange(side[:half], axis, 4), exchange(above[half:], axis, 2)


def gather_core_once(state, axis):
    size = state[0].shape[0]
    half = first_half(size)
    all_rows = jnp.concatenate(state, axis=0)
    other = exchange(all_rows, axis, 1)
    places = ((0, 0, size), (2, 0, size), (4, 0, size), (6, 0, half), (6, half, size - half))
    pieces = [place + (array,) for place, array in zip(places, state)]
    return pieces + [(mask ^ 1, 0, size, other, i * size) for i, mask in enumerate((0, 2, 4, 6))]


def gather_core(state, axis):
    size = state[0].shape[0]
    half = first_half(size)
    places = ((0, 0, size), (2, 0, size), (4, 0, size), (6, 0, half), (6, half, size - half))
    pieces = [place + (array,) for place, array in zip(places, state)]
    return pieces + [(mask ^ 1, start, rows, exchange(a, axis, 1)) for mask, start, rows, a in pieces]


def held(first, second, pieces):
    first, second, arrays = lax.optimization_barrier((first, second, arrays_of(pieces)))
    return first, second, [piece[:3] + (array,) for piece, array in zip(pieces, arrays)]


def arrays_of(pieces):
    return [piece[3] for piece in pieces]


ANY = pl.BlockSpec(memory_space=pl.ANY)
LIMIT = pltpu.CompilerParams(vmem_limit_bytes=48 * 2**20)


def takes(us):
    return pl.CostEstimate(flops=int(us * 1.15e9), bytes_accessed=int(us * 1e5), transcendentals=0)


LARGE = pltpu.CompilerParams(vmem_limit_bytes=60 * 2**20)
SMALL = pltpu.CompilerParams(vmem_limit_bytes=24 * 2**20)


def copy_all(copies, sems):
    started = [pltpu.make_async_copy(source, target, sems.at[i]) for i, (source, target) in enumerate(copies)]
    for copy in started:
        copy.start()
    for copy in started:
        copy.wait()


def rows_at(ref, start, size):
    return ref.at[pl.ds(start if isinstance(start, int) else pl.multiple_of(start, 16), size)]


def slices_of(pieces, me, slots):
    copies = []
    for k, (mask, first, size, _, *at) in enumerate(pieces):
        for start, rows, target in slots(me ^ mask):
            low, high = max(start, first), min(start + rows, first + size)
            if low < high:
                copies.append((k, low - first + sum(at), high - low, target + (low - start)))
    return copies


def place(pieces, axis, total, slots):
    arrays = [p[3] for p in pieces]
    width, dtype = arrays[0].shape[1], arrays[0].dtype
    me = lax.axis_index(axis).reshape(1)

    def kernel(me, *refs):
        out, sems = refs[-2:]
        copies = slices_of(pieces, me[0], slots)
        copy_all([(refs[k].at[pl.ds(s, size)], rows_at(out, t, size)) for k, s, size, t in copies], sems)

    return pl.pallas_call(
        kernel,
        in_specs=[pl.BlockSpec(memory_space=pltpu.SMEM)] + [ANY] * len(arrays),
        out_specs=pl.BlockSpec(memory_space=pltpu.VMEM),
        out_shape=jax.ShapeDtypeStruct((total, width), dtype),
        scratch_shapes=[pltpu.SemaphoreType.DMA((len(slices_of(pieces, 0, slots)),))],
        compiler_params=LIMIT,
        cost_estimate=takes(5.0),
    )(me, *arrays)


def add_first(parts):
    rows, width = parts[0][0].shape[1:]

    def kernel(*refs):
        for h in range(2):
            refs[4 + h][...] = (refs[2 * h][...].astype(f32) + refs[2 * h + 1][...].astype(f32)).astype(bf16)

    blocks = [pl.BlockSpec((1, rows, width), at) for at in (lambda g: (2 * g + 1, 0, 0), lambda g: (g + 2, 0, 0))]
    return pl.pallas_call(
        kernel,
        grid=(2,),
        in_specs=[blocks[0]] * 2 + [blocks[1]] * 2,
        out_specs=[pl.BlockSpec((1, rows, width), lambda g: (g, 0, 0))] * 2,
        out_shape=[jax.ShapeDtypeStruct((2, rows, width), bf16)] * 2,
        compiler_params=SMALL,
        cost_estimate=takes(3),
    )(*parts[0], *parts[1])


def add_second(parts):
    rows, width = parts[0][0].shape[1:]
    part = rows // 2

    def kernel(*refs):
        for h in range(2):
            keep, core, moved = (ref[0].astype(f32) for ref in refs[3 * h : 3 * h + 3])
            refs[6 + h][...] = (keep + core + moved).astype(bf16)

    def block(at):
        return pl.BlockSpec((1, part, width), lambda g: (at, g, 0))

    return pl.pallas_call(
        kernel,
        grid=(rows // part,),
        in_specs=[block(2), block(2), block(1), block(1), block(1), block(1)],
        out_specs=[pl.BlockSpec((part, width), lambda g: (g, 0))] * 2,
        out_shape=[jax.ShapeDtypeStruct((rows, width), bf16)] * 2,
        compiler_params=SMALL,
        cost_estimate=takes(3),
    )(*parts[0], *parts[1])


class Sums:
    def __init__(self, pairs, axis):
        self.axis = axis
        self.parts = [[keep] for keep, _ in pairs]
        self.moving = [exchange(send, axis, 1) for _, send in pairs]

    def hold(self, others):
        self.moving, others = lax.optimization_barrier((self.moving, others))
        return others

    def arrived(self):
        for part, moved in zip(self.parts, self.moving):
            part.append(moved)

    def first(self):
        self.arrived()
        self.moving = list(add_first(self.parts))

    def send_first(self):
        self.moving = [exchange(m, self.axis, (2, 4)[h % 2]) for h, m in enumerate(self.moving)]

    def second(self):
        self.arrived()
        self.moving = list(add_second(self.parts))

    def send_second(self):
        self.moving = [exchange(m, self.axis, (4, 2)[h % 2]) for h, m in enumerate(self.moving)]

    def result(self):
        sums = [sum(p[0].astype(f32) for p in part) for part in self.parts]
        return jnp.concatenate([s + m.astype(f32) for s, m in zip(sums, self.moving)], axis=0)


def each(count, body, carry):
    if count <= 3:
        for j in range(count):
            carry = body(j, carry)
        return carry
    return lax.fori_loop(0, count, body, carry)


def span(j):
    return pl.ds(j * BLK if isinstance(j, int) else pl.multiple_of(j * BLK, BLK), BLK)


def dot(a, b):
    return jnp.dot(a, b, preferred_element_type=f32)


def dot_t(a, b):
    return lax.dot_general(a, b, (((1,), (1,)), ((), ())), preferred_element_type=f32)


def running_sum(rows, backward):
    length = rows.shape[1]
    lane = lax.broadcasted_iota(jnp.int32, rows.shape, 1)
    step = 1
    while step < length:
        moved = pltpu.roll(rows, length - step if backward else step, 1)
        inside = lane < length - step if backward else lane >= step
        rows = rows + jnp.where(inside, moved, 0.0)
        step *= 2
    return rows


def log_sigmoid(x):
    return jnp.minimum(x, 0.0) - jnp.log1p(jnp.exp(-jnp.abs(x)))


def head_rows(h, part=0):
    return slice(part + h * HEAD_DIM, part + (h + 1) * HEAD_DIM)


def attend(qkv, gate_raw, seqs, heads):
    length, cols = qkv.shape[1] // seqs, heads * HEAD_DIM
    lines = gate_raw.shape[0]

    def kernel(qkv_ref, raw_ref, attn_ref, mixed_ref, total_ref, decay_ref, k_rows, decay_cols):
        decay = running_sum(log_sigmoid(raw_ref[...]), False)
        decay_ref[...] = decay
        decay_cols[...] = decay.T
        total_ref[...] = jnp.ones_like(total_ref)
        for h in range(heads):
            k_rows[h] = qkv_ref[head_rows(h, cols), :].T

        for i in range(length // BLK):
            for h in range(heads):
                at = span(i)
                query = qkv_ref[head_rows(h), at] * 0.125
                decay_q = decay_ref[h : h + 1, at]

                def visit(j, carry):
                    summed, total = carry
                    offset = decay_q - decay_cols[span(j), h : h + 1]
                    if isinstance(j, int) and j == i:
                        offset = -jnp.abs(offset)
                    terms = jnp.exp(dot(k_rows[h, span(j), :], query) + offset)
                    total = total + jnp.sum(terms, axis=0, keepdims=True)
                    return summed + dot(qkv_ref[head_rows(h, 2 * cols), span(j)], terms.astype(bf16)), total

                start = (jnp.zeros((HEAD_DIM, BLK), f32), jnp.zeros((1, BLK), f32))
                summed, total = visit(i, each(i, visit, start))
                attn = summed / total
                attn_ref[head_rows(h), at] = attn
                mixed_ref[head_rows(h), at] = attn.astype(bf16)
                total_ref[h : h + 1, at] = total

    def block(rows):
        return pl.BlockSpec((rows, length), lambda s: (0, s))

    tokens = seqs * length
    return pl.pallas_call(
        kernel,
        grid=(seqs,),
        in_specs=[block(3 * cols), block(lines)],
        out_specs=[block(cols), block(cols), block(lines), block(lines)],
        out_shape=[
            jax.ShapeDtypeStruct((cols, tokens), f32),
            jax.ShapeDtypeStruct((cols, tokens), bf16),
            jax.ShapeDtypeStruct((lines, tokens), f32),
            jax.ShapeDtypeStruct((lines, tokens), f32),
        ],
        scratch_shapes=[pltpu.VMEM((heads, length, HEAD_DIM), bf16), pltpu.VMEM((length, lines), f32)],
        compiler_params=SMALL,
        cost_estimate=takes(9.0),
    )(qkv, gate_raw)


def attend_pull(qkv, decay, grad_mixed, attn, totals, gate_raw, seqs, heads):
    length, cols = qkv.shape[1] // seqs, heads * HEAD_DIM
    lines = gate_raw.shape[0]
    pieces = grad_mixed.shape[0]
    piece = length // pieces
    deep = HEAD_DIM + 16

    def kernel(
        qkv_ref, decay_ref, gm_ref, attn_ref, total_ref, raw_ref, gq_ref, gk_ref, gv_ref, graw_ref,
        k_rows, v_rows, decay_cols, q_more, k_more, gs_all, delta_all, gk_sum, gv_sum, gd_all,
    ):
        decay_cols[...] = decay_ref[...].T
        gd_all[...] = jnp.zeros_like(gd_all)
        gk_sum[...] = jnp.zeros_like(gk_sum)
        gv_sum[...] = jnp.zeros_like(gv_sum)
        more = (lax.broadcasted_iota(jnp.int32, (16, length), 0) == 0).astype(bf16)
        for h in range(heads):
            k_rows[h] = qkv_ref[head_rows(h, cols), :].T
            v_rows[h] = qkv_ref[head_rows(h, 2 * cols), :].T
            k_more[h, :HEAD_DIM, :] = qkv_ref[head_rows(h, cols), :]
            k_more[h, HEAD_DIM:, :] = more
            q_more[h, :HEAD_DIM, :] = qkv_ref[head_rows(h), :] * 0.125
            q_more[h, HEAD_DIM:, :] = more
            for p in range(pieces):
                at = slice(p * piece, (p + 1) * piece)
                grad = gm_ref[p, head_rows(h), :].astype(f32)
                total = total_ref[h : h + 1, at]
                gs_all[head_rows(h), at] = (grad / total).astype(bf16)
                delta_all[h : h + 1, at] = jnp.sum(grad * attn_ref[head_rows(h), at], axis=0, keepdims=True) / total

        key_first = lax.broadcasted_iota(jnp.int32, (BLK, BLK), 0) <= lax.broadcasted_iota(
            jnp.int32, (BLK, BLK), 1
        )
        ones = (lax.broadcasted_iota(jnp.int32, (16, BLK), 0) == 0).astype(bf16)

        for i in range(length // BLK):
            for h in range(heads):
                at = span(i)
                query = q_more[h, :HEAD_DIM, at]
                decay_q = decay_ref[h : h + 1, at]
                gs = gs_all[head_rows(h), at]
                delta = delta_all[h : h + 1, at]

                def terms_of(j, last):
                    offset = decay_q - decay_cols[span(j), h : h + 1]
                    if last:
                        offset = -jnp.abs(offset)
                    terms = jnp.exp(dot(k_rows[h, span(j), :], query) + offset)
                    grads = (terms * (dot(v_rows[h, span(j), :], gs) - delta)).astype(bf16)
                    gv_sum[head_rows(h), span(j)] += dot_t(gs, terms.astype(bf16))
                    return grads

                def visit(j, carry):
                    grads = terms_of(j, False)
                    gk_sum[h, :, span(j)] += dot_t(q_more[h, :, at], grads)
                    return carry + dot(k_more[h, :, span(j)], grads)

                gq = each(i, visit, jnp.zeros((deep, BLK), f32))
                grads = terms_of(i, True)
                gk_sum[h, :HEAD_DIM, at] += dot_t(query, grads)
                gq_own = gq[:HEAD_DIM] + dot(k_more[h, :HEAD_DIM, at], grads)
                signed = jnp.where(key_first, grads, -grads)
                gk_sum[h, HEAD_DIM:, at] += dot_t(ones, signed)
                gd_all[h : h + 1, at] = (gq[HEAD_DIM:] + dot(ones, signed))[:1]
                gq_ref[head_rows(h), at] = (gq_own * 0.125).astype(bf16)

        for h in range(heads):
            gk_ref[head_rows(h), :] = gk_sum[h, :HEAD_DIM, :].astype(bf16)
            gd_all[h : h + 1, :] = gd_all[h : h + 1, :] - gk_sum[h, HEAD_DIM : HEAD_DIM + 1, :]
        gv_ref[...] = gv_sum[...].astype(bf16)
        grad_log = running_sum(gd_all[...], True)
        graw_ref[...] = (grad_log * jax.nn.sigmoid(-raw_ref[...])).astype(bf16).astype(f32)

    def block(rows):
        return pl.BlockSpec((rows, length), lambda s: (0, s))

    tokens = seqs * length
    shape = jax.ShapeDtypeStruct((cols, tokens), bf16)
    return pl.pallas_call(
        kernel,
        grid=(seqs,),
        in_specs=[
            block(3 * cols),
            block(lines),
            pl.BlockSpec((pieces, cols, piece), lambda s: (0, 0, s)),
            block(cols),
            block(lines),
            block(lines),
        ],
        out_specs=[block(cols), block(cols), block(cols), block(lines)],
        out_shape=[shape, shape, shape, jax.ShapeDtypeStruct((lines, tokens), f32)],
        scratch_shapes=[
            pltpu.VMEM((heads, length, HEAD_DIM), bf16),
            pltpu.VMEM((heads, length, HEAD_DIM), bf16),
            pltpu.VMEM((length, lines), f32),
            pltpu.VMEM((heads, deep, length), bf16),
            pltpu.VMEM((heads, deep, length), bf16),
            pltpu.VMEM((cols, length), bf16),
            pltpu.VMEM((lines, length), f32),
            pltpu.VMEM((heads, deep, length), f32),
            pltpu.VMEM((cols, length), f32),
            pltpu.VMEM((lines, length), f32),
        ],
        compiler_params=LARGE,
        cost_estimate=takes(19.0),
    )(qkv, decay, grad_mixed, attn, totals, gate_raw)


def inverse_rms(rows):
    return lax.rsqrt(jnp.mean(rows * rows, axis=-1, keepdims=True) + norm_eps)


def norm_pull(rows, gain, grad):
    scale = inverse_rms(rows)
    weighted = grad * gain
    inner = jnp.mean(rows * weighted, axis=-1, keepdims=True)
    return scale * weighted - rows * (scale * scale * scale * inner), jnp.sum(grad * rows * scale, axis=0)


def place_columns(pieces, axis, parts, both):
    arrays = [p[3] for p in pieces]
    rows, width = arrays[0].shape
    count = 8
    me = lax.axis_index(axis).reshape(1)

    def slots(dev):
        return [(0, rows, dev * rows)]

    def kernel(me, *refs):
        outs, (held, sems) = refs[len(arrays) : -2], refs[-2:]

        @pl.when(pl.program_id(0) == 0)
        def _():
            copies = slices_of(pieces, me[0], slots)
            copy_all([(refs[k].at[pl.ds(s, size)], rows_at(held, t, size)) for k, s, size, t in copies], sems)

        for b, out in enumerate(outs):
            at = pl.multiple_of((b * parts + pl.program_id(0)) * 128, 128)
            for dev in range(count):
                out[:, dev * 128 : (dev + 1) * 128] = held[dev * rows : (dev + 1) * rows, pl.ds(at, 128)].astype(f32)

    return pl.pallas_call(
        kernel,
        grid_spec=pltpu.PrefetchScalarGridSpec(
            num_scalar_prefetch=1,
            grid=(parts,),
            in_specs=[ANY] * len(arrays),
            out_specs=[pl.BlockSpec((rows, count * 128), lambda p, me: (0, p))] * both,
            scratch_shapes=[pltpu.VMEM((count * rows, width), bf16), pltpu.SemaphoreType.DMA((len(arrays),))],
        ),
        out_shape=[jax.ShapeDtypeStruct((rows, parts * count * 128), f32)] * both,
        compiler_params=LIMIT,
        cost_estimate=takes(7.0),
    )(me, *arrays)


def place_wide(pieces, axis):
    arrays = [p[3] for p in pieces]
    rows, width = arrays[0].shape
    count = 8
    me = lax.axis_index(axis).reshape(1)

    def kernel(me, *refs):
        out, held, sems = refs[-3:]

        @pl.when(pl.program_id(0) == 0)
        def _():
            copies = slices_of(pieces, me[0], lambda dev: [(0, rows, dev * rows)])
            copy_all([(refs[k].at[pl.ds(s, size)], rows_at(held, t, size)) for k, s, size, t in copies], sems)

        out[...] = held[pl.ds(pl.multiple_of(pl.program_id(0) * rows, rows), rows), :].astype(f32)

    return pl.pallas_call(
        kernel,
        grid_spec=pltpu.PrefetchScalarGridSpec(
            num_scalar_prefetch=1,
            grid=(count,),
            in_specs=[ANY] * len(arrays),
            out_specs=pl.BlockSpec((rows, width), lambda p, me: (p, 0)),
            scratch_shapes=[pltpu.VMEM((count * rows, width), bf16), pltpu.SemaphoreType.DMA((len(arrays),))],
        ),
        out_shape=jax.ShapeDtypeStruct((count * rows, width), f32),
        compiler_params=LIMIT,
        cost_estimate=takes(6.0),
    )(me, *arrays)


def place_heads(pieces, axis, shard, cols, heads, biases):
    arrays = arrays_of(pieces)
    rows, wide = arrays[0].shape
    count, parts = 8, wide // cols
    me = lax.axis_index(axis).reshape(1)

    def slots(dev):
        return [(0, rows, dev * rows)]

    def kernel(me, *refs):
        forget, gain_one, gain_two, bias, held, turned, sems = refs[-7:]
        refs, outs = refs[: len(arrays)], refs[len(arrays) : -7]

        @pl.when(pl.program_id(0) == 0)
        def _():
            copies = slices_of(pieces, me[0], slots)
            copy_all([(refs[k].at[pl.ds(s, size)], rows_at(held, t, size)) for k, s, size, t in copies], sems)
            tails = [held[dev * rows + shard : dev * rows + shard + 16, :shard].astype(f32) for dev in range(count)]
            for dev in range(count):
                turned[dev * heads : (dev + 1) * heads, :] = tails[dev][:heads]
            forget[...] = turned[...].T
            total = sum(tails)
            gain_two[...] = total[heads]
            bias[...] = total[heads + 1, :biases]
            gain_one[...] = total[heads + 2]

        strip = outs[0].shape[0]
        for dev in range(count):
            block = held[pl.ds(pl.multiple_of(dev * rows + pl.program_id(0) * strip, 16), strip), :].astype(f32)
            for part, out in enumerate(outs):
                out[:, dev * cols : (dev + 1) * cols] = block[:, part * cols : (part + 1) * cols]

    steps = 4
    return pl.pallas_call(
        kernel,
        grid_spec=pltpu.PrefetchScalarGridSpec(
            num_scalar_prefetch=1,
            grid=(steps,),
            in_specs=[ANY] * len(arrays),
            out_specs=[pl.BlockSpec((shard // steps, count * cols), lambda g, me: (g, 0))] * parts
            + [
                pl.BlockSpec((shard, count * heads), lambda g, me: (0, 0)),
                pl.BlockSpec((shard,), lambda g, me: (0,)),
                pl.BlockSpec((shard,), lambda g, me: (0,)),
                pl.BlockSpec((biases,), lambda g, me: (0,)),
            ],
            scratch_shapes=[
                pltpu.VMEM((count * rows, wide), bf16),
                pltpu.VMEM((count * heads, shard), f32),
                pltpu.SemaphoreType.DMA((len(arrays),)),
            ],
        ),
        out_shape=[jax.ShapeDtypeStruct((shard, count * cols), f32)] * parts
        + [jax.ShapeDtypeStruct(s, f32) for s in ((shard, count * heads), (shard,), (shard,), (biases,))],
        compiler_params=LIMIT,
        cost_estimate=takes(6.0),
    )(me, *arrays)


def own_attention(w_query, w_key, w_value, w_forget, forget_bias, w_out, gains, heads, me, level):
    shard = w_query.shape[0]
    cols = heads * HEAD_DIM
    each_level = forget_bias.shape[0]

    def kernel(at, wq, wk, wv, wo, wf, gain_one, gain_two, bias, out):
        for odd in range(2):

            @pl.when(at[0] % 2 == odd)
            def _():
                for i, w in enumerate((wq, wk, wv, wo)):
                    out[:shard, i * cols : (i + 1) * cols] = w[:, odd * cols : (odd + 1) * cols]

        row = lax.broadcasted_iota(jnp.int32, (16, shard), 0)
        gain_one, gain_two = (jnp.broadcast_to(g[...].astype(f32)[None], (16, shard)) for g in (gain_one, gain_two))
        rows = jnp.where(row == 0, gain_one, jnp.where(row == 1, gain_two, 0.0))
        head = lax.broadcasted_iota(jnp.int32, (16, HEADS), 1)
        slot = lax.broadcasted_iota(jnp.int32, (16, HEADS), 0)
        chosen = ((head == at[0] * heads + slot - 2) & (slot >= 2) & (slot < heads + 2)).astype(bf16)
        out[shard:, :shard] = (rows + dot(chosen, wf[...])).astype(bf16)
        row = lax.broadcasted_iota(jnp.int32, (16, each_level), 0)
        lane = lax.broadcasted_iota(jnp.int32, (16, each_level), 1)
        mine = (at[1] * each_level + lane == at[0] * heads + row) & (row < heads)
        column = jnp.sum(jnp.where(mine, bias[...].astype(f32), 0.0), axis=1, keepdims=True)
        out[shard:, shard:] = jnp.broadcast_to(column, (16, 4 * cols - shard)).astype(bf16)

    pair = pl.BlockSpec((shard, 2 * cols), lambda i, at: (0, at[0] // 2))
    line = pl.BlockSpec((shard,), lambda i, at: (0,))

    def whole(*shape):
        return pl.BlockSpec(shape, lambda i, at: (0, 0))

    return pl.pallas_call(
        kernel,
        grid_spec=pltpu.PrefetchScalarGridSpec(
            num_scalar_prefetch=1,
            grid=(1,),
            in_specs=[pair] * 4 + [whole(HEADS, shard), line, line, whole(1, each_level)],
            out_specs=whole(shard + 16, 4 * cols),
        ),
        out_shape=jax.ShapeDtypeStruct((shard + 16, 4 * cols), bf16),
        compiler_params=LARGE,
        cost_estimate=takes(3.0),
    )(
        jnp.stack([me, level]), w_query, w_key, w_value, w_out, w_forget.T, *gains, forget_bias.reshape(1, -1)
    )


def norm_project(pieces, pack, axis, seqs, cols):
    arrays = [p[3] for p in pieces]
    rows, width = arrays[0].shape[0] // seqs, arrays[0].shape[1]
    count, depth, wide = 8, pack.shape[0], pack.shape[2]
    shard = width // depth
    tokens = seqs * count * rows
    tile, heads = 2 * rows, cols // HEAD_DIM
    me = lax.axis_index(axis).reshape(1)

    def slots(dev):
        return [(s * rows, rows, (s * count + dev) * rows) for s in range(seqs)]

    number = len(slices_of(pieces, 0, slots))

    def kernel(me, pack_ref, *refs):
        x_out, out, qkv_out, raw_out, held, weights, turned, small, gain, sems = refs[-10:]
        step = pl.program_id(0)

        @pl.when(step == 0)
        def _():
            copies = []
            for z in range(depth):
                copies.append((pack_ref.at[z, pl.ds(0, shard)], rows_at(weights, z * shard, shard)))
                copies.append((pack_ref.at[z, pl.ds(pack.shape[1] - 16, 16)], small.at[z]))
            for k, s, size, t in slices_of(pieces, me[0], slots):
                copies.append((refs[k].at[pl.ds(s, size)], rows_at(held, t, size)))
            copy_all(copies, sems)
            turned[: 3 * cols, :] = weights[:, : 3 * cols].T
            row = lax.broadcasted_iota(jnp.int32, (16, shard), 0)
            for z in range(depth):
                at = slice(z * shard, (z + 1) * shard)
                rows = small[z, :, :shard].astype(f32)
                gain[:, at] = rows
                moved = jnp.concatenate([rows[2:], rows[:2]], axis=0)
                turned[3 * cols :, at] = jnp.where(row < heads, moved, 0.0).astype(bf16)

        bias = sum(small[z, :, shard:].astype(f32) for z in range(depth))[:, :1]
        block = held[pl.ds(pl.multiple_of(step * tile, tile), tile), :]
        x_out[...] = block
        x = block.astype(f32)
        normed = (x * inverse_rms(x) * gain[:1, :]).astype(bf16)
        out[...] = normed
        projected = dot_t(turned[...], normed)
        qkv_out[...] = projected[: 3 * cols].astype(bf16)
        raw_out[...] = projected[3 * cols :] + bias

    spec = pl.BlockSpec((tile, width), lambda p, me: (p, 0))
    shape = jax.ShapeDtypeStruct((tokens, width), bf16)
    return pl.pallas_call(
        kernel,
        grid_spec=pltpu.PrefetchScalarGridSpec(
            num_scalar_prefetch=1,
            grid=(tokens // tile,),
            in_specs=[ANY] * (1 + len(arrays)),
            out_specs=[
                spec,
                spec,
                pl.BlockSpec((3 * cols, tile), lambda p, me: (0, p)),
                pl.BlockSpec((16, tile), lambda p, me: (0, p)),
            ],
            scratch_shapes=[
                pltpu.VMEM((tokens, width), bf16),
                pltpu.VMEM((width, wide), bf16),
                pltpu.VMEM((3 * cols + 16, width), bf16),
                pltpu.VMEM((depth, 16, wide), bf16),
                pltpu.VMEM((16, width), f32),
                pltpu.SemaphoreType.DMA((number + 2 * depth,)),
            ],
        ),
        out_shape=[
            shape,
            shape,
            jax.ShapeDtypeStruct((3 * cols, tokens), bf16),
            jax.ShapeDtypeStruct((16, tokens), f32),
        ],
        compiler_params=LIMIT,
        cost_estimate=takes(12.0),
    )(me, pack, *arrays)


def hidden_norm(x_all, mixed_all, w_out, gain, seqs, rows, axis, turned):
    tokens, width = x_all.shape
    tile = 4 * rows
    tiles = tokens // seqs // tile
    me = lax.axis_index(axis).reshape(1)

    def kernel(me, x_ref, mixed_ref, w_ref, gain_ref, out_ref, own_ref, hidden_ref):
        parts = [slice(2 * i * rows, 2 * (i + 1) * rows) for i in range(2)]
        for at in parts:
            hidden_ref[at, :] = x_ref[at, :].astype(f32) + (dot_t if turned else dot)(mixed_ref[:, at].T, w_ref[...])
        for at in parts:
            hidden = hidden_ref[at, :]
            out_ref[at, :] = (hidden * inverse_rms(hidden) * gain_ref[...]).astype(bf16)

        @pl.when(pl.program_id(1) == me[0] // 4)
        def _():
            own_ref[...] = hidden_ref[pl.ds(pl.multiple_of(me[0] % 4 * rows, rows), rows), :]

    return pl.pallas_call(
        kernel,
        grid_spec=pltpu.PrefetchScalarGridSpec(
            num_scalar_prefetch=1,
            grid=(seqs, tiles),
            in_specs=[
                pl.BlockSpec((tile, width), lambda s, t, me: (s * tiles + t, 0)),
                pl.BlockSpec((width, tile), lambda s, t, me: (0, s * tiles + t)),
                pl.BlockSpec((width, width), lambda s, t, me: (0, 0)),
                pl.BlockSpec((1, width), lambda s, t, me: (0, 0)),
            ],
            out_specs=[
                pl.BlockSpec((tile, width), lambda s, t, me: (s * tiles + t, 0)),
                pl.BlockSpec((rows, width), lambda s, t, me: (s, 0)),
            ],
            scratch_shapes=[pltpu.VMEM((tile, width), f32)],
        ),
        out_shape=[jax.ShapeDtypeStruct((tokens, width), bf16), jax.ShapeDtypeStruct((seqs * rows, width), f32)],
        compiler_params=LIMIT,
        cost_estimate=takes(17.0),
    )(me, x_all, mixed_all, w_out, gain.reshape(1, width))


def split_pair(value, keep_ref, send_ref, me):
    rows = value.shape[0] // 4
    blocks = [value[i * rows : (i + 1) * rows] for i in range(4)]
    core, side = me % 2 == 0, me // 2 % 2 == 0
    for t in range(2):
        first, second = (jnp.where(side, blocks[2 * t + c], blocks[2 - 2 * t + c]) for c in range(2))
        keep_ref[t] = jnp.where(core, first, second).astype(bf16)
        send_ref[t] = jnp.where(core, second, first).astype(bf16)


def pair_specs(paired, tile, tiles, width):
    if paired:
        block = pl.BlockSpec((2, tile // 4, width), lambda t, me: (t, 0, 0))
        shape = jax.ShapeDtypeStruct((2 * tiles, tile // 4, width), bf16)
        return (lambda t, me: me[0] // 4 ^ t), [block] * 2, [shape] * 2
    block = pl.BlockSpec((tile, width), lambda t, me: (t, 0))
    return (lambda t, me: t), [block], [jax.ShapeDtypeStruct((tiles * tile, width), bf16)]


def feed_forward(normed, cot, mlp, axis, seq, seqs, own):
    tokens, width = normed.shape
    depth, packed, ff_cols = mlp.shape
    shard = width // depth
    paired = lax.axis_size(axis) == 8
    tile = 512
    tiles = tokens // seqs // tile
    at, specs, shapes = pair_specs(paired, tile, tiles, width)
    blocks = width // ff_cols
    me = lax.axis_index(axis).reshape(1)

    def kernel(me, normed_ref, cot_ref, mlp_ref, inner_ref, grads_ref, *refs):
        outs, (gate_up, down, sems) = refs[:-3], refs[-3:]

        @pl.when(pl.program_id(0) == 0)
        def _():
            copies = []
            for z in range(depth):
                for part in range(2):
                    copies.append(
                        (
                            mlp_ref.at[z, pl.ds(part * shard, shard)],
                            gate_up.at[pl.ds(z * shard, shard), pl.ds(part * ff_cols, ff_cols)],
                        )
                    )
                for k in range(blocks):
                    copies.append(
                        (
                            mlp_ref.at[z, pl.ds(2 * shard + k * own, own)],
                            down.at[pl.ds(z * own, own), pl.ds(k * ff_cols, ff_cols)],
                        )
                    )
            copy_all(copies, sems)

        both = dot(normed_ref[...], gate_up[...])
        grad_inner = dot_t(cot_ref[...], down[...])
        gate, up = both[:, :ff_cols], both[:, ff_cols:]
        sig = jax.nn.sigmoid(gate)
        silu = gate * sig
        inner = (silu * up).astype(bf16)
        inner_ref[...] = inner
        grads_ref[:, :ff_cols] = (grad_inner * up * sig * (1.0 + gate * (1.0 - sig))).astype(bf16)
        grads_ref[:, ff_cols:] = (grad_inner * silu).astype(bf16)
        back = dot_t(grads_ref[...], gate_up[...])
        result = dot(inner, down[...])
        if paired:
            split_pair(back, outs[0], outs[1], me[0])
            split_pair(result, outs[2], outs[3], me[0])
        else:
            outs[0][...] = back.astype(bf16)
            outs[1][...] = result.astype(bf16)

    rows = pl.BlockSpec((tile, width), lambda t, me: (seq * tiles + at(t, me), 0))
    length = tokens // seqs

    def own_rows(cols):
        return pl.BlockSpec((tile, cols), lambda t, me: (at(t, me), 0))

    return pl.pallas_call(
        kernel,
        grid_spec=pltpu.PrefetchScalarGridSpec(
            num_scalar_prefetch=1,
            grid=(tiles,),
            in_specs=[rows, rows, ANY],
            out_specs=[own_rows(ff_cols), own_rows(2 * ff_cols)] + specs * 2,
            scratch_shapes=[
                pltpu.VMEM((width, 2 * ff_cols), bf16),
                pltpu.VMEM((ff_cols, width), bf16),
                pltpu.SemaphoreType.DMA((depth * (2 + blocks),)),
            ],
        ),
        out_shape=[
            jax.ShapeDtypeStruct((length, ff_cols), bf16),
            jax.ShapeDtypeStruct((length, 2 * ff_cols), bf16),
        ]
        + shapes * 2,
        compiler_params=LARGE,
        cost_estimate=takes(17.0),
    )(me, normed, cot, mlp)


def project_back(grads, raw, pack, width, axis, seqs):
    cols, tokens = grads[0].shape
    depth, wide = pack.shape[0], pack.shape[2]
    shard, heads = width // depth, cols // HEAD_DIM
    tile = 512
    tiles = tokens // seqs // tile
    at, specs, shapes = pair_specs(True, tile, tiles, width)
    me = lax.axis_index(axis).reshape(1)

    def kernel(me, gq, gk, gv, raw, pack_ref, *refs):
        outs, (weights, small, turned, sems) = refs[:-4], refs[-4:]

        @pl.when((pl.program_id(0) == 0) & (pl.program_id(1) == 0))
        def _():
            copies = []
            for z in range(depth):
                copies.append((pack_ref.at[z, pl.ds(0, shard), pl.ds(0, 5 * 128)], rows_at(weights, z * shard, shard)))
                copies.append((pack_ref.at[z, pl.ds(shard, 16)], small.at[z]))
            copy_all(copies, sems)
            for z in range(depth):
                forget = jnp.concatenate(
                    [small[z, 2 : 2 + heads, :shard].astype(f32), jnp.zeros((EXTRA - heads, shard), f32)], axis=0
                )
                weights[z * shard : (z + 1) * shard, 3 * cols :] = forget.T.astype(bf16)

        for i, part in enumerate((gq, gk, gv)):
            turned[i * cols : (i + 1) * cols, :] = part[...]
        turned[3 * cols : 3 * cols + 16, :] = raw[...].astype(bf16)
        turned[3 * cols + 16 :, :] = jnp.zeros((EXTRA - 16, tile), bf16)
        back = dot_t(turned[...].T, weights[...])
        for s in range(seqs):

            @pl.when(pl.program_id(0) == s)
            def _():
                split_pair(back, outs[2 * s], outs[2 * s + 1], me[0])

    def seq_block(s):
        return pl.BlockSpec(
            (2, tile // 4, width), lambda q, t, me: (jnp.where(q == s, t, jnp.where(q < s, 0, tiles - 1)), 0, 0)
        )

    def columns(rows):
        return pl.BlockSpec((rows, tile), lambda s, t, me: (0, s * tiles + at(t, me)))

    return pl.pallas_call(
        kernel,
        grid_spec=pltpu.PrefetchScalarGridSpec(
            num_scalar_prefetch=1,
            grid=(seqs, tiles),
            in_specs=[columns(cols)] * 3 + [columns(16), ANY],
            out_specs=[seq_block(s) for s in range(seqs) for _ in range(2)],
            scratch_shapes=[
                pltpu.VMEM((width, 3 * cols + EXTRA), bf16),
                pltpu.VMEM((depth, 16, wide), bf16),
                pltpu.VMEM((3 * cols + EXTRA, tile), bf16),
                pltpu.SemaphoreType.DMA((2 * depth,)),
            ],
        ),
        out_shape=shapes * seqs,
        compiler_params=LARGE,
        cost_estimate=takes(11.0),
    )(me, *grads, raw, pack)


def attention_grads(grads, raw, normed, branch, mixed, gain_row, pack, axis, seqs, depth, heads, each_level):
    cols, tokens = grads[0].shape
    width = normed.shape[1]
    shard = width // depth
    count, own_out, piece = branch.shape
    wide = pack.shape[2]
    me = lax.axis_index(axis).reshape(1)
    part = piece // seqs

    def kernel(me, gq, gk, gv, raw, normed_ref, branch_ref, mixed_ref, gain_ref, pack_ref, small_ref, out, turned, branches):
        z = pl.program_id(0)

        @pl.when(z == 0)
        def _():
            for i, g in enumerate((gq, gk, gv)):
                turned[i * cols : (i + 1) * cols, :] = g[...]
            turned[3 * cols :, :] = raw[...].astype(bf16)
            for dev in range(count):
                for s in range(seqs):
                    to = (s * count + dev) * part
                    branches[:, to : to + part] = branch_ref[dev, :, s * part : (s + 1) * part]

        grad = dot(turned[...], normed_ref[...])
        forget = grad[3 * cols :]
        columns = grad[: 3 * cols].T
        out[0, :shard, : 3 * cols] = columns.astype(bf16)
        out[0, :shard, 3 * cols :] = dot_t(mixed_ref[...], branches[...]).astype(bf16)
        by_row = jnp.sum(columns * pack_ref[0, :, : 3 * cols].astype(f32), axis=1, keepdims=True)
        by_row = jnp.broadcast_to(by_row, (shard, 8)).T[:1]
        small = small_ref[0, :, :shard].astype(f32)
        by_row = by_row + jnp.sum(forget[:heads] * small[2 : 2 + heads], axis=0, keepdims=True)
        row = lax.broadcasted_iota(jnp.int32, (16, shard), 0)
        lane = lax.broadcasted_iota(jnp.int32, (16, shard), 1)
        more = jnp.where(row == heads, gain_ref[...], jnp.where(row == heads + 2, by_row / small[:1], 0.0))
        sums = jnp.sum(raw[...], axis=1, keepdims=True)
        for h in range(heads):
            head = me[0] * heads + h
            at = head // each_level * shard + head % each_level - z * shard
            more = more + jnp.where((row == heads + 1) & (lane == at), sums[h : h + 1, :], 0.0)
        out[0, shard : shard + 16, :shard] = jnp.where(row < heads, forget, more).astype(bf16)
        out[0, shard : shard + 16, shard:] = jnp.zeros((16, wide - shard), bf16)
        out[0, shard + 16 :, :] = jnp.zeros((16, wide), bf16)

    def whole(*shape):
        return pl.BlockSpec(shape, lambda z, me: (0,) * len(shape))

    return pl.pallas_call(
        kernel,
        grid_spec=pltpu.PrefetchScalarGridSpec(
            num_scalar_prefetch=1,
            grid=(depth,),
            in_specs=[whole(cols, tokens)] * 3
            + [
                whole(16, tokens),
                pl.BlockSpec((tokens, shard), lambda z, me: (0, z)),
                whole(count, own_out, piece),
                pl.BlockSpec((shard, tokens), lambda z, me: (z, 0)),
                pl.BlockSpec((1, shard), lambda z, me: (0, z)),
                pl.BlockSpec((1, shard, wide), lambda z, me: (z, 0, 0)),
                pl.BlockSpec((1, 16, wide), lambda z, me: (z, shard // 16, 0)),
            ],
            out_specs=pl.BlockSpec((1, shard + 32, wide), lambda z, me: (z, 0, 0)),
            scratch_shapes=[pltpu.VMEM((3 * cols + 16, tokens), bf16), pltpu.VMEM((own_out, tokens), bf16)],
        ),
        out_shape=jax.ShapeDtypeStruct((depth, shard + 32, wide), bf16),
        compiler_params=LARGE,
        cost_estimate=takes(12.0),
    )(me, *grads, raw, normed, branch, mixed, gain_row, pack, pack)


def out_turned(pack, cols, shard):
    depth, rows, wide = pack.shape

    def kernel(pack_ref, out):
        out[...] = pack_ref[0, :, 3 * cols :].T

    return pl.pallas_call(
        kernel,
        grid=(depth,),
        in_specs=[pl.BlockSpec((1, shard, wide), lambda z: (z, 0, 0))],
        out_specs=pl.BlockSpec((cols, shard), lambda z: (0, z)),
        out_shape=jax.ShapeDtypeStruct((cols, depth * shard), bf16),
        compiler_params=SMALL,
        cost_estimate=takes(2),
    )(pack)


def own_kernel(me, gate, up, down, out):
    rows, own = gate.shape[0], down.shape[0]
    out[:rows, :] = gate[...]
    out[rows : 2 * rows, :] = up[...]
    for k in range(down.shape[1] // (128 * pl.num_programs(0))):
        at = (k * pl.num_programs(0) + pl.program_id(0)) * 128
        out[2 * rows + k * own : 2 * rows + (k + 1) * own, :] = down[:, pl.ds(pl.multiple_of(at, 128), 128)]


def own_mlp(w_gate, w_up, w_down, depth, count, me):
    shard, ff = w_gate.shape
    own = w_down.shape[0] // count
    width = w_down.shape[1]
    ff_cols = depth * own
    if own == 128:
        strip = pl.BlockSpec((shard, 128), lambda z, me: (0, z * count + me[0]))
        total = 2 * shard + own * width // ff_cols
        return pl.pallas_call(
            own_kernel,
            grid_spec=pltpu.PrefetchScalarGridSpec(
                num_scalar_prefetch=1,
                grid=(depth,),
                in_specs=[strip, strip, pl.BlockSpec((own, width), lambda z, me: (me[0], 0))],
                out_specs=pl.BlockSpec((total, 128), lambda z, me: (0, z)),
            ),
            out_shape=jax.ShapeDtypeStruct((total, ff_cols), bf16),
            cost_estimate=takes(4.0),
        )(me.reshape(1), w_gate, w_up, w_down)

    def ff_columns(w):
        w = w.reshape(shard, depth, count, own)
        return lax.dynamic_index_in_dim(w, me, 2, keepdims=False).reshape(shard, ff_cols)

    down = lax.dynamic_slice_in_dim(w_down, me * own, own, 0)
    return jnp.concatenate([ff_columns(w_gate), ff_columns(w_up), stack_columns(down, ff_cols)], axis=0)


def contract(a, b, da, db):
    return lax.dot_general(a, b, (((da,), (db,)), ((), ())), preferred_element_type=f32)


def stack_columns(a, width):
    return jnp.concatenate([a[:, i : i + width] for i in range(0, a.shape[1], width)], axis=0)


def to_shards(grad):
    return lax.psum_scatter(grad, "fsdp", scatter_dimension=0, tiled=True)


def local_eight(
    inputs,
    gain_attn,
    w_query,
    w_key,
    w_value,
    w_forget,
    forget_bias,
    w_out,
    gain_mlp,
    w_gate,
    w_up,
    w_down,
    cotangent,
):
    axis = "ctx"
    count, me = lax.axis_size(axis), lax.axis_index(axis)
    depth, level = lax.axis_size("fsdp"), lax.axis_index("fsdp")
    seqs, rows, width = inputs.shape
    tokens = seqs * count * rows
    shard = width // depth
    heads = HEADS // count
    cols = heads * HEAD_DIM
    ff_own = w_down.shape[0] // count
    ff_cols = depth * ff_own
    own_out = width // count
    flat_in, flat_cot = inputs.reshape(seqs * rows, width), cotangent.reshape(seqs * rows, width)

    def token_slots(dev):
        return [(s * rows, rows, (s * count + dev) * rows) for s in range(seqs)]

    x_state = gather_start(flat_in, axis)
    own = own_attention(
        w_query, w_key, w_value, w_forget, forget_bias, w_out, (gain_attn, gain_mlp), heads, me, level
    )
    pack = lax.all_gather(own, "fsdp", axis=0)
    x_far = gather_far(x_state, axis)
    mlp = lax.all_gather(own_mlp(after(w_gate, x_far[3:]), w_up, w_down, depth, count, me), "fsdp", axis=0)
    g_state = gather_start(after(flat_cot, x_far[3:]), axis)
    x_pieces = gather_core_once(x_far, axis)
    pack = after(pack, g_state[1:])
    g_state = gather_far(g_state, axis)
    out_state = gather_start(out_turned(pack, cols, shard), axis)
    gains = pack[:, shard : shard + 2, :shard].astype(f32)
    gain_one, gain_two = gains[:, 0].reshape(width), gains[:, 1].reshape(width)

    x_all, normed, qkv, gate_raw = norm_project(x_pieces, pack, axis, seqs, cols)
    attn, mixed, totals, decay = attend(qkv, gate_raw, seqs, heads)
    mixed, g_state, out_state = lax.optimization_barrier((mixed, g_state, out_state))
    out_state = gather_far(out_state, axis)
    mixed_state = gather_start(mixed, axis)
    g_pieces = gather_core_once(g_state, axis)
    g_all = place(g_pieces, axis, tokens, token_slots)
    out_full = place(gather_core_once(out_state, axis), axis, width, lambda dev: [(0, own_out, dev * own_out)])
    mixed_state = gather_far(after(mixed_state, (g_all, out_full)), axis)
    mixed_pieces = gather_core(mixed_state, axis)
    mixed_all = place(mixed_pieces, axis, width, lambda dev: [(0, cols, dev * cols)])
    normed_two, hidden_own = hidden_norm(x_all, mixed_all, out_full, gain_two, seqs, rows, axis, True)

    sides = [feed_forward(normed_two, g_all, mlp, axis, s, seqs, ff_own) for s in range(seqs)]
    inner = jnp.concatenate([side[0] for side in sides], axis=0)
    gate_up_grads = jnp.concatenate([side[1] for side in sides], axis=0)
    back = Sums([side[2:4] for side in sides], axis)
    grad_down = back.hold(contract(inner, g_all, 0, 0).astype(bf16))
    back.first()
    normed_two = back.hold(normed_two)
    back.send_first()
    result = Sums([after(side[4:6], normed_two) for side in sides], axis)
    grad_gate_up = result.hold(contract(normed_two, gate_up_grads, 0, 0).astype(bf16))
    result.first()
    grad_gate_up, result.moving = back.hold((grad_gate_up, result.moving))
    back.second()
    back.send_second()
    back = back.result()
    grad_down, grad_gate_up = to_shards(grad_down), to_shards(grad_gate_up)

    grad_from_norm, grad_gain_two = norm_pull(hidden_own, gain_two, back)
    grad_hidden = flat_cot.astype(f32) + grad_from_norm
    branch = grad_hidden.astype(bf16)
    grad_mixed = contract(out_full, branch, 0, 1).astype(bf16).reshape(count, cols, seqs * rows)
    branch = after(branch, grad_mixed).T.reshape(count, own_out, seqs * rows)
    grad_mixed = result.hold(grad_mixed)
    grad_mixed = lax.all_to_all(grad_mixed, axis, 0, 0, tiled=True)
    result.send_first()
    grad_mixed, grad_down, branch = lax.optimization_barrier((grad_mixed, grad_down, branch))
    branch = lax.all_to_all(branch, axis, 0, 0, tiled=True)
    down_state = gather_start(grad_down, axis)
    gq, gk, gv, grad_raw = attend_pull(qkv, decay, grad_mixed, attn, totals, gate_raw, seqs, heads)

    down_state, branch, grad_gate_up, grad_raw = result.hold((down_state, branch, grad_gate_up, grad_raw))
    gate_up_state = gather_start(grad_gate_up, axis)
    down_state = gather_far(down_state, axis)
    grads = (gq, gk, gv)
    grad_pack = attention_grads(
        grads, grad_raw, normed, branch, mixed_all, grad_gain_two[None], pack, axis, seqs, depth, heads, HEADS // depth
    )
    grad_raw, down_state, gate_up_state, _ = lax.optimization_barrier((grad_raw, down_state, gate_up_state, grad_pack))
    gate_up_state = gather_far(gate_up_state, axis)
    result.hold(grad_pack)
    result.second()
    grad_raw = result.hold(grad_raw)
    result.send_second()
    down_pieces = gather_core(down_state, axis)
    pairs = project_back(grads, grad_raw, pack, width, axis, seqs)
    grad_pack = to_shards(grad_pack.reshape(-1, 4 * cols))
    pairs, gate_up_state, down_pieces = held(pairs, gate_up_state, down_pieces)
    grad_normed = Sums([pairs[2 * s : 2 * s + 2] for s in range(seqs)], axis)
    grad_normed.first()
    gate_up_state = result.hold(grad_normed.hold(gate_up_state))
    grad_normed.send_first()
    gate_up_pieces = gather_core(gate_up_state, axis)
    grad_down = place_wide(down_pieces, axis)
    grad_gate, grad_up = place_columns(gate_up_pieces, axis, depth, 2)
    grad_pack, _ = grad_normed.hold((grad_pack, (grad_down, grad_gate)))
    grad_normed.second()
    grad_normed.send_second()
    pack_state = gather_start(grad_pack, axis)
    pack_state = grad_normed.hold(pack_state)
    pack_state = gather_far(pack_state, axis)
    grad_in, _ = norm_pull(flat_in.astype(f32), gain_one, grad_normed.result())
    input_grad = (grad_hidden + grad_in).reshape(seqs, rows, width)
    output = (hidden_own + result.result()).astype(bf16).reshape(seqs, rows, width)
    pack_pieces = gather_core(after(pack_state, (input_grad, output)), axis)
    grad_query, grad_key, grad_value, grad_out, grad_forget, grad_gain_one, grad_gain_two, grad_bias = place_heads(
        pack_pieces, axis, shard, cols, heads, forget_bias.shape[0]
    )
    return (
        output,
        input_grad,
        grad_gain_one,
        grad_query,
        grad_key,
        grad_value,
        grad_forget,
        grad_bias,
        grad_out,
        grad_gain_two,
        grad_gate,
        grad_up,
        grad_down,
    )


def local_any(
    inputs,
    gain_attn,
    w_query,
    w_key,
    w_value,
    w_forget,
    forget_bias,
    w_out,
    gain_mlp,
    w_gate,
    w_up,
    w_down,
    cotangent,
):
    axis = "ctx"
    count, me = lax.axis_size(axis), lax.axis_index(axis)
    depth, level = lax.axis_size("fsdp"), lax.axis_index("fsdp")
    seqs, rows, width = inputs.shape
    tokens = seqs * count * rows
    shard = width // depth
    heads = -(-HEADS // count)
    cols = heads * HEAD_DIM
    ff_own = w_down.shape[0] // count
    ff_cols = depth * ff_own
    out_rows, own_out = shard // count, width // count
    flat_in, flat_cot = inputs.reshape(seqs * rows, width), cotangent.reshape(seqs * rows, width)

    def own_columns(w, each_head):
        w = jnp.pad(w, ((0, 0), (0, count * heads * each_head - w.shape[1])))
        return lax.dynamic_slice_in_dim(w, me * heads * each_head, heads * each_head, 1)

    extra = [own_columns(w_forget, 1), gain_attn[:, None], gain_mlp[:, None]]
    extra += [jnp.pad(forget_bias, (0, shard - forget_bias.shape[0]))[:, None]]
    extra += [jnp.zeros((shard, EXTRA - heads - 3), bf16)]
    pack = [own_columns(w, HEAD_DIM) for w in (w_query, w_key, w_value)] + extra
    pack = lax.all_gather(jnp.concatenate(pack, axis=1), "fsdp", axis=0, tiled=True)
    extra = pack[:, 3 * cols :]
    gain_one = extra[:, heads].astype(f32)
    gain_two = extra[:, heads + 1].astype(f32)
    biases = extra[:, heads + 2].reshape(depth, shard)[:, : forget_bias.shape[0]].reshape(-1)
    biases = jnp.pad(biases, (0, count * heads - HEADS))
    bias = lax.dynamic_slice_in_dim(biases, me * heads, heads).astype(f32)
    out_own = lax.all_gather(lax.dynamic_slice_in_dim(w_out, me * out_rows, out_rows, 0), "fsdp", axis=0)
    out_full = lax.all_gather(out_own, axis, axis=1).reshape(width, width)
    mlp = lax.all_gather(own_mlp(w_gate, w_up, w_down, depth, count, me), "fsdp", axis=0)

    x_all = lax.all_gather(inputs, axis, axis=1, tiled=True).reshape(tokens, width)
    x_wide = x_all.astype(f32)
    normed = (x_wide * inverse_rms(x_wide) * gain_one).astype(bf16)
    g_all = lax.all_gather(after(cotangent, normed), axis, axis=1, tiled=True).reshape(tokens, width)
    qkv = contract(pack[:, : 3 * cols], normed, 0, 1).astype(bf16)
    gate_raw = contract(extra, normed, 0, 1)[:heads] + bias[:, None]
    gate_raw = jnp.pad(gate_raw, ((0, -heads % 16), (0, 0)))
    attn, mixed, totals, decay = attend(qkv, gate_raw, seqs, heads)
    mixed_all = lax.all_gather(mixed, axis, axis=0, tiled=True)[:width]
    normed_two, hidden_own = hidden_norm(x_all, mixed_all, out_full, gain_two, seqs, rows, axis, False)

    def summed(part):
        return lax.psum_scatter(part.reshape(count, rows, width), axis, scatter_dimension=0).astype(f32)

    sides, sums = [], []
    for s in range(seqs):
        side = feed_forward(normed_two, g_all, mlp, axis, s, seqs, ff_own)
        sides.append(side[:2])
        sums.append([summed(side[2]), summed(side[3])])
        normed_two = after(normed_two, sums[s])
    back, result = (jnp.concatenate(parts, axis=0) for parts in zip(*sums))
    inner = jnp.concatenate([side[0] for side in sides], axis=0)
    gate_up_grads = jnp.concatenate([side[1] for side in sides], axis=0)
    grad_down = to_shards(contract(inner, g_all, 0, 0).astype(bf16))
    grad_gate_up = to_shards(contract(normed_two, gate_up_grads, 0, 0).astype(bf16))
    output = (hidden_own + result).astype(bf16)

    grad_from_norm, grad_gain_two = norm_pull(hidden_own, gain_two, back)
    grad_hidden = flat_cot.astype(f32) + grad_from_norm
    branch = grad_hidden.astype(bf16)
    grad_mixed = contract(out_full, branch, 1, 1).astype(bf16)
    grad_mixed = jnp.pad(grad_mixed, ((0, count * cols - width), (0, 0)))
    grad_mixed = lax.all_to_all(grad_mixed.reshape(count, cols, seqs * rows), axis, 0, 0, tiled=True)
    branch = lax.all_to_all(branch.T.reshape(count, own_out, seqs * rows), axis, 0, 0, tiled=True)
    branch = branch.reshape(count, own_out, seqs, rows).transpose(1, 2, 0, 3).reshape(own_out, tokens)
    grad_out = contract(branch, mixed_all, 1, 1)
    gq, gk, gv, grad_raw = attend_pull(qkv, decay, grad_mixed, attn, totals, gate_raw, seqs, heads)
    grad_raw = jnp.pad(grad_raw[:heads].astype(bf16), ((0, EXTRA - heads), (0, 0)))
    grads = jnp.concatenate([gq, gk, gv, grad_raw], axis=0)
    grad_normed = contract(grads, pack, 0, 1).astype(bf16).reshape(seqs, count * rows, width)
    grad_normed = jnp.concatenate([summed(part) for part in grad_normed], axis=0)

    grad_pack = contract(grads, normed, 1, 0)
    head_at = me * heads + jnp.arange(heads)
    bias_col = head_at // (HEADS // depth) * shard + head_at % (HEADS // depth)
    bias_sum = jnp.where(head_at < HEADS, jnp.sum(grad_raw[:heads].astype(f32), axis=1), 0.0)
    at_col = jnp.arange(width)[None, :] == bias_col[:, None]
    bias_row = jnp.sum(jnp.where(at_col, bias_sum[:, None], 0.0), axis=0, keepdims=True)
    tail = [grad_pack[3 * cols : 3 * cols + heads], grad_gain_two[None], bias_row]
    tail += [jnp.zeros((EXTRA - heads - 2, width), f32)]
    grad_pack = jnp.concatenate([grad_pack[: 3 * cols]] + tail + [grad_out], axis=0).astype(bf16)
    grad_pack = to_shards(grad_pack.reshape(-1, depth, shard).transpose(1, 0, 2).reshape(-1, shard))
    grad_pack = lax.all_gather(grad_pack, axis)
    out_at = 3 * cols + EXTRA

    def turned(start, size):
        return grad_pack[:, start : start + size].reshape(-1, shard)[:width].T.astype(f32)

    tail = grad_pack[:, 3 * cols : out_at].astype(f32)
    tail_sum = jnp.sum(tail[:, heads : heads + 2], axis=0)
    grad_down = lax.all_gather(grad_down, axis, axis=0, tiled=True).astype(f32)
    grad_gate_up = lax.all_gather(grad_gate_up.reshape(shard, 2, depth, ff_own), axis)
    grad_gate_up = grad_gate_up.transpose(2, 1, 3, 0, 4).reshape((2,) + w_gate.shape).astype(f32)
    grad_in, grad_gain_one = norm_pull(flat_in.astype(f32), gain_one, grad_normed)
    grad_gain_one = lax.psum(grad_gain_one, (axis, "fsdp"))
    return (
        output.reshape(seqs, rows, width),
        (grad_hidden + grad_in).reshape(seqs, rows, width),
        lax.dynamic_slice_in_dim(grad_gain_one, level * shard, shard),
        turned(0, cols),
        turned(cols, cols),
        turned(2 * cols, cols),
        tail[:, :heads].reshape(count * heads, shard)[:HEADS].T,
        tail_sum[1, : forget_bias.shape[0]],
        turned(out_at, own_out),
        tail_sum[0],
        grad_gate_up[0],
        grad_gate_up[1],
        grad_down,
    )


def solution(mesh):
    split, first, rest = P("fsdp", "ctx", None), P("fsdp"), P("fsdp", None)
    return jax.shard_map(
        local_eight if mesh.shape["ctx"] == 8 else local_any,
        mesh=mesh,
        in_specs=(split, first, rest, rest, rest, rest, first, rest, first, rest, rest, rest, split),
        out_specs=(split, split, first, rest, rest, rest, rest, first, rest, first, rest, rest, rest),
        check_vma=False,
    )
```

```python
import jax
import jax.numpy as jnp
from jax import lax
from jax.experimental import pallas as pl
from jax.experimental.pallas import tpu as pltpu
from jax.sharding import PartitionSpec as P

HEADS = 24
HEAD_DIM = 64
BLK = 256
EXTRA = 64
norm_eps = 1e-06
bf16 = jnp.bfloat16
f32 = jnp.float32


def exchange(x, axis, mask):
    return lax.ppermute(x, axis, [(i, i ^ mask) for i in range(lax.axis_size(axis))])


def after(x, done):
    return lax.optimization_barrier((x, done))[0]


def first_half(rows):
    return -(-rows // 32) * 16


def gather_start(x, axis):
    return x, exchange(x, axis, 2), exchange(x, axis, 4)


def gather_far(state, axis):
    x, side, above = state
    half = first_half(x.shape[0])
    return x, side, above, exchange(side[:half], axis, 4), exchange(above[half:], axis, 2)


def gather_core_once(state, axis):
    size = state[0].shape[0]
    half = first_half(size)
    all_rows = jnp.concatenate(state, axis=0)
    other = exchange(all_rows, axis, 1)
    places = ((0, 0, size), (2, 0, size), (4, 0, size), (6, 0, half), (6, half, size - half))
    pieces = [place + (array,) for place, array in zip(places, state)]
    return pieces + [(mask ^ 1, 0, size, other, i * size) for i, mask in enumerate((0, 2, 4, 6))]


def gather_core(state, axis):
    size = state[0].shape[0]
    half = first_half(size)
    places = ((0, 0, size), (2, 0, size), (4, 0, size), (6, 0, half), (6, half, size - half))
    pieces = [place + (array,) for place, array in zip(places, state)]
    return pieces + [(mask ^ 1, start, rows, exchange(a, axis, 1)) for mask, start, rows, a in pieces]


def held(first, second, pieces):
    first, second, arrays = lax.optimization_barrier((first, second, arrays_of(pieces)))
    return first, second, [piece[:3] + (array,) for piece, array in zip(pieces, arrays)]


def arrays_of(pieces):
    return [piece[3] for piece in pieces]


ANY = pl.BlockSpec(memory_space=pl.ANY)
LIMIT = pltpu.CompilerParams(vmem_limit_bytes=48 * 2**20)


def takes(us):
    return pl.CostEstimate(flops=int(us * 1.15e9), bytes_accessed=int(us * 1e5), transcendentals=0)


LARGE = pltpu.CompilerParams(vmem_limit_bytes=60 * 2**20)
SMALL = pltpu.CompilerParams(vmem_limit_bytes=24 * 2**20)


def copy_all(copies, sems):
    started = [pltpu.make_async_copy(source, target, sems.at[i]) for i, (source, target) in enumerate(copies)]
    for copy in started:
        copy.start()
    for copy in started:
        copy.wait()


def rows_at(ref, start, size):
    return ref.at[pl.ds(start if isinstance(start, int) else pl.multiple_of(start, 16), size)]


def slices_of(pieces, me, slots):
    copies = []
    for k, (mask, first, size, _, *at) in enumerate(pieces):
        for start, rows, target in slots(me ^ mask):
            low, high = max(start, first), min(start + rows, first + size)
            if low < high:
                copies.append((k, low - first + sum(at), high - low, target + (low - start)))
    return copies


def place(pieces, axis, total, slots):
    arrays = [p[3] for p in pieces]
    width, dtype = arrays[0].shape[1], arrays[0].dtype
    me = lax.axis_index(axis).reshape(1)

    def kernel(me, *refs):
        out, sems = refs[-2:]
        copies = slices_of(pieces, me[0], slots)
        copy_all([(refs[k].at[pl.ds(s, size)], rows_at(out, t, size)) for k, s, size, t in copies], sems)

    return pl.pallas_call(
        kernel,
        in_specs=[pl.BlockSpec(memory_space=pltpu.SMEM)] + [ANY] * len(arrays),
        out_specs=pl.BlockSpec(memory_space=pltpu.VMEM),
        out_shape=jax.ShapeDtypeStruct((total, width), dtype),
        scratch_shapes=[pltpu.SemaphoreType.DMA((len(slices_of(pieces, 0, slots)),))],
        compiler_params=LIMIT,
        cost_estimate=takes(5.0),
    )(me, *arrays)


def add_first(parts):
    rows, width = parts[0][0].shape[1:]

    def kernel(*refs):
        for h in range(2):
            refs[4 + h][...] = (refs[2 * h][...].astype(f32) + refs[2 * h + 1][...].astype(f32)).astype(bf16)

    blocks = [pl.BlockSpec((1, rows, width), at) for at in (lambda g: (2 * g + 1, 0, 0), lambda g: (g + 2, 0, 0))]
    return pl.pallas_call(
        kernel,
        grid=(2,),
        in_specs=[blocks[0]] * 2 + [blocks[1]] * 2,
        out_specs=[pl.BlockSpec((1, rows, width), lambda g: (g, 0, 0))] * 2,
        out_shape=[jax.ShapeDtypeStruct((2, rows, width), bf16)] * 2,
        compiler_params=LARGE,
        cost_estimate=takes(3),
    )(*parts[0], *parts[1])


def add_second(parts):
    rows, width = parts[0][0].shape[1:]
    part = rows // 2

    def kernel(*refs):
        for h in range(2):
            keep, core, moved = (ref[0].astype(f32) for ref in refs[3 * h : 3 * h + 3])
            refs[6 + h][...] = (keep + core + moved).astype(bf16)

    def block(at):
        return pl.BlockSpec((1, part, width), lambda g: (at, g, 0))

    return pl.pallas_call(
        kernel,
        grid=(rows // part,),
        in_specs=[block(2), block(2), block(1), block(1), block(1), block(1)],
        out_specs=[pl.BlockSpec((part, width), lambda g: (g, 0))] * 2,
        out_shape=[jax.ShapeDtypeStruct((rows, width), bf16)] * 2,
        compiler_params=LARGE,
        cost_estimate=takes(3),
    )(*parts[0], *parts[1])


class Sums:
    def __init__(self, pairs, axis):
        self.axis = axis
        self.parts = [[keep] for keep, _ in pairs]
        self.moving = [exchange(send, axis, 1) for _, send in pairs]

    def hold(self, others):
        self.moving, others = lax.optimization_barrier((self.moving, others))
        return others

    def arrived(self):
        for part, moved in zip(self.parts, self.moving):
            part.append(moved)

    def first(self):
        self.arrived()
        self.moving = list(add_first(self.parts))

    def send_first(self):
        self.moving = [exchange(m, self.axis, (2, 4)[h % 2]) for h, m in enumerate(self.moving)]

    def second(self):
        self.arrived()
        self.moving = list(add_second(self.parts))

    def send_second(self):
        self.moving = [exchange(m, self.axis, (4, 2)[h % 2]) for h, m in enumerate(self.moving)]

    def result(self):
        sums = [sum(p[0].astype(f32) for p in part) for part in self.parts]
        return jnp.concatenate([s + m.astype(f32) for s, m in zip(sums, self.moving)], axis=0)


def each(count, body, carry):
    if count <= 3:
        return body(pl.ds(0, count * BLK), carry) if count else carry
    return lax.fori_loop(0, count, lambda j, carry: body(span(j), carry), carry)


def span(j):
    return pl.ds(j * BLK if isinstance(j, int) else pl.multiple_of(j * BLK, BLK), BLK)


def dot(a, b):
    return jnp.dot(a, b, preferred_element_type=f32)


def dot_t(a, b):
    return lax.dot_general(a, b, (((1,), (1,)), ((), ())), preferred_element_type=f32)


def running_sum(rows, backward):
    length = rows.shape[1]
    lane = lax.broadcasted_iota(jnp.int32, rows.shape, 1)
    step = 1
    while step < length:
        moved = pltpu.roll(rows, length - step if backward else step, 1)
        inside = lane < length - step if backward else lane >= step
        rows = rows + jnp.where(inside, moved, 0.0)
        step *= 2
    return rows


def log_sigmoid(x):
    return jnp.minimum(x, 0.0) - jnp.log1p(jnp.exp(-jnp.abs(x)))


def head_rows(h, part=0):
    return slice(part + h * HEAD_DIM, part + (h + 1) * HEAD_DIM)


def attend(qkv, gate_raw, seqs, heads):
    length, cols = qkv.shape[1] // seqs, heads * HEAD_DIM
    lines = gate_raw.shape[0]

    def kernel(qkv_ref, raw_ref, attn_ref, mixed_ref, total_ref, decay_ref, k_rows, decay_cols):
        decay = running_sum(log_sigmoid(raw_ref[...]), False)
        decay_ref[...] = decay
        decay_cols[...] = decay.T
        total_ref[...] = jnp.ones_like(total_ref)
        for h in range(heads):
            k_rows[h] = qkv_ref[head_rows(h, cols), :].T

        for i in range(length // BLK):
            for h in range(heads):
                at = span(i)
                query = qkv_ref[head_rows(h), at] * 0.125
                decay_q = decay_ref[h : h + 1, at]

                def visit(keys, carry, last=False):
                    summed, total = carry
                    offset = decay_q - decay_cols[keys, h : h + 1]
                    if last:
                        offset = -jnp.abs(offset)
                    terms = jnp.exp(dot(k_rows[h, keys, :], query) + offset)
                    total = total + jnp.sum(terms, axis=0, keepdims=True)
                    return summed + dot(qkv_ref[head_rows(h, 2 * cols), keys], terms.astype(bf16)), total

                start = (jnp.zeros((HEAD_DIM, BLK), f32), jnp.zeros((1, BLK), f32))
                summed, total = visit(at, each(i, visit, start), True)
                attn = summed / total
                attn_ref[head_rows(h), at] = attn
                mixed_ref[head_rows(h), at] = attn.astype(bf16)
                total_ref[h : h + 1, at] = total

    def block(rows):
        return pl.BlockSpec((rows, length), lambda s: (0, s))

    tokens = seqs * length
    return pl.pallas_call(
        kernel,
        grid=(seqs,),
        in_specs=[block(3 * cols), block(lines)],
        out_specs=[block(cols), block(cols), block(lines), block(lines)],
        out_shape=[
            jax.ShapeDtypeStruct((cols, tokens), f32),
            jax.ShapeDtypeStruct((cols, tokens), bf16),
            jax.ShapeDtypeStruct((lines, tokens), f32),
            jax.ShapeDtypeStruct((lines, tokens), f32),
        ],
        scratch_shapes=[pltpu.VMEM((heads, length, HEAD_DIM), bf16), pltpu.VMEM((length, lines), f32)],
        compiler_params=SMALL,
        cost_estimate=takes(9.0),
    )(qkv, gate_raw)


def attend_pull(qkv, decay, grad_mixed, attn, totals, gate_raw, seqs, heads):
    length, cols = qkv.shape[1] // seqs, heads * HEAD_DIM
    lines = gate_raw.shape[0]
    pieces = grad_mixed.shape[0]
    piece = length // pieces
    deep = HEAD_DIM + 16

    def kernel(
        qkv_ref, decay_ref, gm_ref, attn_ref, total_ref, raw_ref, gq_ref, gk_ref, gv_ref, graw_ref,
        k_rows, v_rows, decay_cols, q_more, k_more, gs_all, delta_all, gk_sum, gv_sum, gd_all,
    ):
        decay_cols[...] = decay_ref[...].T
        gd_all[...] = jnp.zeros_like(gd_all)
        gk_sum[...] = jnp.zeros_like(gk_sum)
        gv_sum[...] = jnp.zeros_like(gv_sum)
        more = (lax.broadcasted_iota(jnp.int32, (16, length), 0) == 0).astype(bf16)
        for h in range(heads):
            k_rows[h] = qkv_ref[head_rows(h, cols), :].T
            v_rows[h] = qkv_ref[head_rows(h, 2 * cols), :].T
            k_more[h, :HEAD_DIM, :] = qkv_ref[head_rows(h, cols), :]
            k_more[h, HEAD_DIM:, :] = more
            q_more[h, :HEAD_DIM, :] = qkv_ref[head_rows(h), :] * 0.125
            q_more[h, HEAD_DIM:, :] = more
            for p in range(pieces):
                at = slice(p * piece, (p + 1) * piece)
                grad = gm_ref[p, head_rows(h), :].astype(f32)
                total = total_ref[h : h + 1, at]
                gs_all[head_rows(h), at] = (grad / total).astype(bf16)
                delta_all[h : h + 1, at] = jnp.sum(grad * attn_ref[head_rows(h), at], axis=0, keepdims=True) / total

        key_first = lax.broadcasted_iota(jnp.int32, (BLK, BLK), 0) <= lax.broadcasted_iota(
            jnp.int32, (BLK, BLK), 1
        )
        ones = (lax.broadcasted_iota(jnp.int32, (16, BLK), 0) == 0).astype(bf16)

        for i in range(length // BLK):
            for h in range(heads):
                at = span(i)
                query = q_more[h, :HEAD_DIM, at]
                decay_q = decay_ref[h : h + 1, at]
                gs = gs_all[head_rows(h), at]
                delta = delta_all[h : h + 1, at]

                def terms_of(keys, last):
                    offset = decay_q - decay_cols[keys, h : h + 1]
                    if last:
                        offset = -jnp.abs(offset)
                    terms = jnp.exp(dot(k_rows[h, keys, :], query) + offset)
                    grads = (terms * (dot(v_rows[h, keys, :], gs) - delta)).astype(bf16)
                    gv_sum[head_rows(h), keys] += dot_t(gs, terms.astype(bf16))
                    return grads

                def visit(keys, carry):
                    grads = terms_of(keys, False)
                    gk_sum[h, :, keys] += dot_t(q_more[h, :, at], grads)
                    return carry + dot(k_more[h, :, keys], grads)

                gq = each(i, visit, jnp.zeros((deep, BLK), f32))
                grads = terms_of(at, True)
                gk_sum[h, :HEAD_DIM, at] += dot_t(query, grads)
                gq_own = gq[:HEAD_DIM] + dot(k_more[h, :HEAD_DIM, at], grads)
                signed = jnp.where(key_first, grads, -grads)
                gk_sum[h, HEAD_DIM:, at] += dot_t(ones, signed)
                gd_all[h : h + 1, at] = (gq[HEAD_DIM:] + dot(ones, signed))[:1]
                gq_ref[head_rows(h), at] = (gq_own * 0.125).astype(bf16)

        for h in range(heads):
            gk_ref[head_rows(h), :] = gk_sum[h, :HEAD_DIM, :].astype(bf16)
            gd_all[h : h + 1, :] = gd_all[h : h + 1, :] - gk_sum[h, HEAD_DIM : HEAD_DIM + 1, :]
        gv_ref[...] = gv_sum[...].astype(bf16)
        grad_log = running_sum(gd_all[...], True)
        graw_ref[...] = (grad_log * jax.nn.sigmoid(-raw_ref[...])).astype(bf16).astype(f32)

    def block(rows):
        return pl.BlockSpec((rows, length), lambda s: (0, s))

    tokens = seqs * length
    shape = jax.ShapeDtypeStruct((cols, tokens), bf16)
    return pl.pallas_call(
        kernel,
        grid=(seqs,),
        in_specs=[
            block(3 * cols),
            block(lines),
            pl.BlockSpec((pieces, cols, piece), lambda s: (0, 0, s)),
            block(cols),
            block(lines),
            block(lines),
        ],
        out_specs=[block(cols), block(cols), block(cols), block(lines)],
        out_shape=[shape, shape, shape, jax.ShapeDtypeStruct((lines, tokens), f32)],
        scratch_shapes=[
            pltpu.VMEM((heads, length, HEAD_DIM), bf16),
            pltpu.VMEM((heads, length, HEAD_DIM), bf16),
            pltpu.VMEM((length, lines), f32),
            pltpu.VMEM((heads, deep, length), bf16),
            pltpu.VMEM((heads, deep, length), bf16),
            pltpu.VMEM((cols, length), bf16),
            pltpu.VMEM((lines, length), f32),
            pltpu.VMEM((heads, deep, length), f32),
            pltpu.VMEM((cols, length), f32),
            pltpu.VMEM((lines, length), f32),
        ],
        compiler_params=LARGE,
        cost_estimate=takes(19.0),
    )(qkv, decay, grad_mixed, attn, totals, gate_raw)


def inverse_rms(rows):
    return lax.rsqrt(jnp.mean(rows * rows, axis=-1, keepdims=True) + norm_eps)


def norm_pull(rows, gain, grad):
    scale = inverse_rms(rows)
    weighted = grad * gain
    inner = jnp.mean(rows * weighted, axis=-1, keepdims=True)
    return scale * weighted - rows * (scale * scale * scale * inner), jnp.sum(grad * rows * scale, axis=0)


def place_columns(pieces, axis, parts, both):
    arrays = [p[3] for p in pieces]
    rows, width = arrays[0].shape
    count = 8
    me = lax.axis_index(axis).reshape(1)

    def slots(dev):
        return [(0, rows, dev * rows)]

    def kernel(me, *refs):
        outs, (held, sems) = refs[len(arrays) : -2], refs[-2:]

        @pl.when(pl.program_id(0) == 0)
        def _():
            copies = slices_of(pieces, me[0], slots)
            copy_all([(refs[k].at[pl.ds(s, size)], rows_at(held, t, size)) for k, s, size, t in copies], sems)

        for b, out in enumerate(outs):
            at = pl.multiple_of((b * parts + pl.program_id(0)) * 128, 128)
            for dev in range(count):
                out[:, dev * 128 : (dev + 1) * 128] = held[dev * rows : (dev + 1) * rows, pl.ds(at, 128)].astype(f32)

    return pl.pallas_call(
        kernel,
        grid_spec=pltpu.PrefetchScalarGridSpec(
            num_scalar_prefetch=1,
            grid=(parts,),
            in_specs=[ANY] * len(arrays),
            out_specs=[pl.BlockSpec((rows, count * 128), lambda p, me: (0, p))] * both,
            scratch_shapes=[pltpu.VMEM((count * rows, width), bf16), pltpu.SemaphoreType.DMA((len(arrays),))],
        ),
        out_shape=[jax.ShapeDtypeStruct((rows, parts * count * 128), f32)] * both,
        compiler_params=LIMIT,
        cost_estimate=takes(7.0),
    )(me, *arrays)


def place_wide(pieces, axis):
    arrays = [p[3] for p in pieces]
    rows, width = arrays[0].shape
    count = 8
    me = lax.axis_index(axis).reshape(1)

    def kernel(me, *refs):
        out, held, sems = refs[-3:]

        @pl.when(pl.program_id(0) == 0)
        def _():
            copies = slices_of(pieces, me[0], lambda dev: [(0, rows, dev * rows)])
            copy_all([(refs[k].at[pl.ds(s, size)], rows_at(held, t, size)) for k, s, size, t in copies], sems)

        out[...] = held[pl.ds(pl.multiple_of(pl.program_id(0) * rows, rows), rows), :].astype(f32)

    return pl.pallas_call(
        kernel,
        grid_spec=pltpu.PrefetchScalarGridSpec(
            num_scalar_prefetch=1,
            grid=(count,),
            in_specs=[ANY] * len(arrays),
            out_specs=pl.BlockSpec((rows, width), lambda p, me: (p, 0)),
            scratch_shapes=[pltpu.VMEM((count * rows, width), bf16), pltpu.SemaphoreType.DMA((len(arrays),))],
        ),
        out_shape=jax.ShapeDtypeStruct((count * rows, width), f32),
        compiler_params=LIMIT,
        cost_estimate=takes(6.0),
    )(me, *arrays)


def place_heads(pieces, axis, shard, cols, heads, biases):
    arrays = arrays_of(pieces)
    rows, wide = arrays[0].shape
    count, parts = 8, wide // cols
    me = lax.axis_index(axis).reshape(1)

    def slots(dev):
        return [(0, rows, dev * rows)]

    def kernel(me, *refs):
        forget, gain_one, gain_two, bias, held, turned, sems = refs[-7:]
        refs, outs = refs[: len(arrays)], refs[len(arrays) : -7]

        @pl.when(pl.program_id(0) == 0)
        def _():
            copies = slices_of(pieces, me[0], slots)
            copy_all([(refs[k].at[pl.ds(s, size)], rows_at(held, t, size)) for k, s, size, t in copies], sems)
            tails = [held[dev * rows + shard : dev * rows + shard + 16, :shard].astype(f32) for dev in range(count)]
            for dev in range(count):
                turned[dev * heads : (dev + 1) * heads, :] = tails[dev][:heads]
            forget[...] = turned[...].T
            total = sum(tails)
            gain_two[...] = total[heads]
            bias[...] = total[heads + 1, :biases]
            gain_one[...] = total[heads + 2]

        strip = outs[0].shape[0]
        for dev in range(count):
            block = held[pl.ds(pl.multiple_of(dev * rows + pl.program_id(0) * strip, 16), strip), :].astype(f32)
            for part, out in enumerate(outs):
                out[:, dev * cols : (dev + 1) * cols] = block[:, part * cols : (part + 1) * cols]

    steps = 4
    return pl.pallas_call(
        kernel,
        grid_spec=pltpu.PrefetchScalarGridSpec(
            num_scalar_prefetch=1,
            grid=(steps,),
            in_specs=[ANY] * len(arrays),
            out_specs=[pl.BlockSpec((shard // steps, count * cols), lambda g, me: (g, 0))] * parts
            + [
                pl.BlockSpec((shard, count * heads), lambda g, me: (0, 0)),
                pl.BlockSpec((shard,), lambda g, me: (0,)),
                pl.BlockSpec((shard,), lambda g, me: (0,)),
                pl.BlockSpec((biases,), lambda g, me: (0,)),
            ],
            scratch_shapes=[
                pltpu.VMEM((count * rows, wide), bf16),
                pltpu.VMEM((count * heads, shard), f32),
                pltpu.SemaphoreType.DMA((len(arrays),)),
            ],
        ),
        out_shape=[jax.ShapeDtypeStruct((shard, count * cols), f32)] * parts
        + [jax.ShapeDtypeStruct(s, f32) for s in ((shard, count * heads), (shard,), (shard,), (biases,))],
        compiler_params=LIMIT,
        cost_estimate=takes(6.0),
    )(me, *arrays)


def own_attention(w_query, w_key, w_value, w_forget, forget_bias, w_out, gains, heads, me, level):
    shard = w_query.shape[0]
    cols = heads * HEAD_DIM
    each_level = forget_bias.shape[0]

    def kernel(at, wq, wk, wv, wo, wf, gain_one, gain_two, bias, out):
        for odd in range(2):

            @pl.when(at[0] % 2 == odd)
            def _():
                for i, w in enumerate((wq, wk, wv, wo)):
                    out[:shard, i * cols : (i + 1) * cols] = w[:, odd * cols : (odd + 1) * cols]

        row = lax.broadcasted_iota(jnp.int32, (16, shard), 0)
        gain_one, gain_two = (jnp.broadcast_to(g[...].astype(f32)[None], (16, shard)) for g in (gain_one, gain_two))
        rows = jnp.where(row == 0, gain_one, jnp.where(row == 1, gain_two, 0.0))
        head = lax.broadcasted_iota(jnp.int32, (16, HEADS), 1)
        slot = lax.broadcasted_iota(jnp.int32, (16, HEADS), 0)
        chosen = ((head == at[0] * heads + slot - 2) & (slot >= 2) & (slot < heads + 2)).astype(bf16)
        out[shard:, :shard] = (rows + dot(chosen, wf[...])).astype(bf16)
        row = lax.broadcasted_iota(jnp.int32, (16, each_level), 0)
        lane = lax.broadcasted_iota(jnp.int32, (16, each_level), 1)
        mine = (at[1] * each_level + lane == at[0] * heads + row) & (row < heads)
        column = jnp.sum(jnp.where(mine, bias[...].astype(f32), 0.0), axis=1, keepdims=True)
        out[shard:, shard:] = jnp.broadcast_to(column, (16, 4 * cols - shard)).astype(bf16)

    pair = pl.BlockSpec((shard, 2 * cols), lambda i, at: (0, at[0] // 2))
    line = pl.BlockSpec((shard,), lambda i, at: (0,))

    def whole(*shape):
        return pl.BlockSpec(shape, lambda i, at: (0, 0))

    return pl.pallas_call(
        kernel,
        grid_spec=pltpu.PrefetchScalarGridSpec(
            num_scalar_prefetch=1,
            grid=(1,),
            in_specs=[pair] * 4 + [whole(HEADS, shard), line, line, whole(1, each_level)],
            out_specs=whole(shard + 16, 4 * cols),
        ),
        out_shape=jax.ShapeDtypeStruct((shard + 16, 4 * cols), bf16),
        compiler_params=LARGE,
        cost_estimate=takes(3.0),
    )(
        jnp.stack([me, level]), w_query, w_key, w_value, w_out, w_forget.T, *gains, forget_bias.reshape(1, -1)
    )


def norm_project(pieces, pack, axis, seqs, cols):
    arrays = [p[3] for p in pieces]
    rows, width = arrays[0].shape[0] // seqs, arrays[0].shape[1]
    count, depth, wide = 8, pack.shape[0], pack.shape[2]
    shard = width // depth
    tokens = seqs * count * rows
    tile, heads = 2 * rows, cols // HEAD_DIM
    me = lax.axis_index(axis).reshape(1)

    def slots(dev):
        return [(s * rows, rows, (s * count + dev) * rows) for s in range(seqs)]

    number = len(slices_of(pieces, 0, slots))

    def kernel(me, pack_ref, *refs):
        x_out, out, qkv_out, raw_out, held, weights, turned, small, gain, sems = refs[-10:]
        step = pl.program_id(0)

        @pl.when(step == 0)
        def _():
            copies = []
            for z in range(depth):
                copies.append((pack_ref.at[z, pl.ds(0, shard)], rows_at(weights, z * shard, shard)))
                copies.append((pack_ref.at[z, pl.ds(pack.shape[1] - 16, 16)], small.at[z]))
            for k, s, size, t in slices_of(pieces, me[0], slots):
                copies.append((refs[k].at[pl.ds(s, size)], rows_at(held, t, size)))
            copy_all(copies, sems)
            turned[: 3 * cols, :] = weights[:, : 3 * cols].T
            row = lax.broadcasted_iota(jnp.int32, (16, shard), 0)
            for z in range(depth):
                at = slice(z * shard, (z + 1) * shard)
                rows = small[z, :, :shard].astype(f32)
                gain[:, at] = rows
                moved = jnp.concatenate([rows[2:], rows[:2]], axis=0)
                turned[3 * cols :, at] = jnp.where(row < heads, moved, 0.0).astype(bf16)

        bias = sum(small[z, :, shard:].astype(f32) for z in range(depth))[:, :1]
        block = held[pl.ds(pl.multiple_of(step * tile, tile), tile), :]
        x_out[...] = block
        x = block.astype(f32)
        normed = (x * inverse_rms(x) * gain[:1, :]).astype(bf16)
        out[...] = normed
        projected = dot_t(turned[...], normed)
        qkv_out[...] = projected[: 3 * cols].astype(bf16)
        raw_out[...] = projected[3 * cols :] + bias

    spec = pl.BlockSpec((tile, width), lambda p, me: (p, 0))
    shape = jax.ShapeDtypeStruct((tokens, width), bf16)
    return pl.pallas_call(
        kernel,
        grid_spec=pltpu.PrefetchScalarGridSpec(
            num_scalar_prefetch=1,
            grid=(tokens // tile,),
            in_specs=[ANY] * (1 + len(arrays)),
            out_specs=[
                spec,
                spec,
                pl.BlockSpec((3 * cols, tile), lambda p, me: (0, p)),
                pl.BlockSpec((16, tile), lambda p, me: (0, p)),
            ],
            scratch_shapes=[
                pltpu.VMEM((tokens, width), bf16),
                pltpu.VMEM((width, wide), bf16),
                pltpu.VMEM((3 * cols + 16, width), bf16),
                pltpu.VMEM((depth, 16, wide), bf16),
                pltpu.VMEM((16, width), f32),
                pltpu.SemaphoreType.DMA((number + 2 * depth,)),
            ],
        ),
        out_shape=[
            shape,
            shape,
            jax.ShapeDtypeStruct((3 * cols, tokens), bf16),
            jax.ShapeDtypeStruct((16, tokens), f32),
        ],
        compiler_params=LIMIT,
        cost_estimate=takes(12.0),
    )(me, pack, *arrays)


def hidden_norm(x_all, mixed_all, w_out, gain, seqs, rows, axis, turned):
    tokens, width = x_all.shape
    tile = 4 * rows
    tiles = tokens // seqs // tile
    me = lax.axis_index(axis).reshape(1)

    def kernel(me, x_ref, mixed_ref, w_ref, gain_ref, out_ref, own_ref, hidden_ref):
        parts = [slice(2 * i * rows, 2 * (i + 1) * rows) for i in range(2)]
        for at in parts:
            hidden_ref[at, :] = x_ref[at, :].astype(f32) + (dot_t if turned else dot)(mixed_ref[:, at].T, w_ref[...])
        for at in parts:
            hidden = hidden_ref[at, :]
            out_ref[at, :] = (hidden * inverse_rms(hidden) * gain_ref[...]).astype(bf16)

        @pl.when(pl.program_id(1) == me[0] // 4)
        def _():
            own_ref[...] = hidden_ref[pl.ds(pl.multiple_of(me[0] % 4 * rows, rows), rows), :]

    return pl.pallas_call(
        kernel,
        grid_spec=pltpu.PrefetchScalarGridSpec(
            num_scalar_prefetch=1,
            grid=(seqs, tiles),
            in_specs=[
                pl.BlockSpec((tile, width), lambda s, t, me: (s * tiles + t, 0)),
                pl.BlockSpec((width, tile), lambda s, t, me: (0, s * tiles + t)),
                pl.BlockSpec((width, width), lambda s, t, me: (0, 0)),
                pl.BlockSpec((1, width), lambda s, t, me: (0, 0)),
            ],
            out_specs=[
                pl.BlockSpec((tile, width), lambda s, t, me: (s * tiles + t, 0)),
                pl.BlockSpec((rows, width), lambda s, t, me: (s, 0)),
            ],
            scratch_shapes=[pltpu.VMEM((tile, width), f32)],
        ),
        out_shape=[jax.ShapeDtypeStruct((tokens, width), bf16), jax.ShapeDtypeStruct((seqs * rows, width), f32)],
        compiler_params=LARGE,
        cost_estimate=takes(17.0),
    )(me, x_all, mixed_all, w_out, gain.reshape(1, width))


def split_pair(value, keep_ref, send_ref, me):
    rows = value.shape[0] // 4
    blocks = [value[i * rows : (i + 1) * rows] for i in range(4)]
    core, side = me % 2 == 0, me // 2 % 2 == 0
    for t in range(2):
        first, second = (jnp.where(side, blocks[2 * t + c], blocks[2 - 2 * t + c]) for c in range(2))
        keep_ref[t] = jnp.where(core, first, second).astype(bf16)
        send_ref[t] = jnp.where(core, second, first).astype(bf16)


def pair_specs(paired, tile, tiles, width):
    if paired:
        block = pl.BlockSpec((2, tile // 4, width), lambda t, me: (t, 0, 0))
        shape = jax.ShapeDtypeStruct((2 * tiles, tile // 4, width), bf16)
        return (lambda t, me: me[0] // 4 ^ t), [block] * 2, [shape] * 2
    block = pl.BlockSpec((tile, width), lambda t, me: (t, 0))
    return (lambda t, me: t), [block], [jax.ShapeDtypeStruct((tiles * tile, width), bf16)]


def feed_forward(normed, cot, mlp, axis, first, number, seqs, own):
    tokens, width = normed.shape
    depth, packed, ff_cols = mlp.shape
    shard = width // depth
    paired = lax.axis_size(axis) == 8
    tile = 512
    tiles = tokens // seqs // tile
    at, specs, shapes = pair_specs(paired, tile, tiles, width)
    blocks = width // ff_cols
    me = lax.axis_index(axis).reshape(1)

    def kernel(me, normed_ref, cot_ref, mlp_ref, inner_ref, grads_ref, *refs):
        outs, (gate_up, down, sems) = refs[:-3], refs[-3:]

        @pl.when((pl.program_id(0) == 0) & (pl.program_id(1) == 0))
        def _():
            copies = []
            for z in range(depth):
                for part in range(2):
                    copies.append(
                        (
                            mlp_ref.at[z, pl.ds(part * shard, shard)],
                            gate_up.at[pl.ds(z * shard, shard), pl.ds(part * ff_cols, ff_cols)],
                        )
                    )
                for k in range(blocks):
                    copies.append(
                        (
                            mlp_ref.at[z, pl.ds(2 * shard + k * own, own)],
                            down.at[pl.ds(z * own, own), pl.ds(k * ff_cols, ff_cols)],
                        )
                    )
            copy_all(copies, sems)

        both = dot(normed_ref[...], gate_up[...])
        grad_inner = dot_t(cot_ref[...], down[...])
        gate, up = both[:, :ff_cols], both[:, ff_cols:]
        sig = jax.nn.sigmoid(gate)
        silu = gate * sig
        inner = (silu * up).astype(bf16)
        inner_ref[...] = inner
        grads_ref[:, :ff_cols] = (grad_inner * up * sig * (1.0 + gate * (1.0 - sig))).astype(bf16)
        grads_ref[:, ff_cols:] = (grad_inner * silu).astype(bf16)
        back = dot_t(grads_ref[...], gate_up[...])
        result = dot(inner, down[...])
        each_seq = len(outs) // number
        for q in range(number):

            @pl.when(pl.program_id(0) == q)
            def _():
                own_outs = outs[q * each_seq : (q + 1) * each_seq]
                if paired:
                    split_pair(back, own_outs[0], own_outs[1], me[0])
                    split_pair(result, own_outs[2], own_outs[3], me[0])
                else:
                    own_outs[0][...] = back.astype(bf16)
                    own_outs[1][...] = result.astype(bf16)

    rows = pl.BlockSpec((tile, width), lambda q, t, me: ((first + q) * tiles + at(t, me), 0))
    length = tokens // seqs

    def own_rows(cols):
        return pl.BlockSpec((tile, cols), lambda q, t, me: (q * tiles + at(t, me), 0))

    def for_seq(spec, s):
        def index(q, t, me):
            return spec.index_map(jnp.where(q == s, t, jnp.where(q < s, 0, tiles - 1)), me)

        return pl.BlockSpec(spec.block_shape, index)

    return pl.pallas_call(
        kernel,
        grid_spec=pltpu.PrefetchScalarGridSpec(
            num_scalar_prefetch=1,
            grid=(number, tiles),
            in_specs=[rows, rows, ANY],
            out_specs=[own_rows(ff_cols), own_rows(2 * ff_cols)]
            + [for_seq(spec, s) for s in range(number) for spec in specs * 2],
            scratch_shapes=[
                pltpu.VMEM((width, 2 * ff_cols), bf16),
                pltpu.VMEM((ff_cols, width), bf16),
                pltpu.SemaphoreType.DMA((depth * (2 + blocks),)),
            ],
        ),
        out_shape=[
            jax.ShapeDtypeStruct((number * length, ff_cols), bf16),
            jax.ShapeDtypeStruct((number * length, 2 * ff_cols), bf16),
        ]
        + shapes * 2 * number,
        compiler_params=LARGE,
        cost_estimate=takes(17 * number),
    )(me, normed, cot, mlp)


def project_back(grads, raw, pack, width, axis, seqs):
    cols, tokens = grads[0].shape
    depth, wide = pack.shape[0], pack.shape[2]
    shard, heads = width // depth, cols // HEAD_DIM
    tile = 512
    tiles = tokens // seqs // tile
    at, specs, shapes = pair_specs(True, tile, tiles, width)
    me = lax.axis_index(axis).reshape(1)

    def kernel(me, gq, gk, gv, raw, pack_ref, *refs):
        outs, (weights, small, turned, sems) = refs[:-4], refs[-4:]

        @pl.when((pl.program_id(0) == 0) & (pl.program_id(1) == 0))
        def _():
            copies = []
            for z in range(depth):
                copies.append((pack_ref.at[z, pl.ds(0, shard), pl.ds(0, 5 * 128)], rows_at(weights, z * shard, shard)))
                copies.append((pack_ref.at[z, pl.ds(shard, 16)], small.at[z]))
            copy_all(copies, sems)
            for z in range(depth):
                forget = jnp.concatenate(
                    [small[z, 2 : 2 + heads, :shard].astype(f32), jnp.zeros((EXTRA - heads, shard), f32)], axis=0
                )
                weights[z * shard : (z + 1) * shard, 3 * cols :] = forget.T.astype(bf16)

        for i, part in enumerate((gq, gk, gv)):
            turned[i * cols : (i + 1) * cols, :] = part[...]
        turned[3 * cols : 3 * cols + 16, :] = raw[...].astype(bf16)
        turned[3 * cols + 16 :, :] = jnp.zeros((EXTRA - 16, tile), bf16)
        back = dot_t(turned[...].T, weights[...])
        for s in range(seqs):

            @pl.when(pl.program_id(0) == s)
            def _():
                split_pair(back, outs[2 * s], outs[2 * s + 1], me[0])

    def seq_block(s):
        return pl.BlockSpec(
            (2, tile // 4, width), lambda q, t, me: (jnp.where(q == s, t, jnp.where(q < s, 0, tiles - 1)), 0, 0)
        )

    def columns(rows):
        return pl.BlockSpec((rows, tile), lambda s, t, me: (0, s * tiles + at(t, me)))

    return pl.pallas_call(
        kernel,
        grid_spec=pltpu.PrefetchScalarGridSpec(
            num_scalar_prefetch=1,
            grid=(seqs, tiles),
            in_specs=[columns(cols)] * 3 + [columns(16), ANY],
            out_specs=[seq_block(s) for s in range(seqs) for _ in range(2)],
            scratch_shapes=[
                pltpu.VMEM((width, 3 * cols + EXTRA), bf16),
                pltpu.VMEM((depth, 16, wide), bf16),
                pltpu.VMEM((3 * cols + EXTRA, tile), bf16),
                pltpu.SemaphoreType.DMA((2 * depth,)),
            ],
        ),
        out_shape=shapes * seqs,
        compiler_params=LARGE,
        cost_estimate=takes(11.0),
    )(me, *grads, raw, pack)


def attention_grads(grads, raw, normed, branch, mixed, gain_row, pack, axis, seqs, depth, heads, each_level):
    cols, tokens = grads[0].shape
    width = normed.shape[1]
    shard = width // depth
    count, own_out, piece = branch.shape
    wide = pack.shape[2]
    me = lax.axis_index(axis).reshape(1)
    part = piece // seqs

    def kernel(me, gq, gk, gv, raw, normed_ref, branch_ref, mixed_ref, gain_ref, pack_ref, small_ref, out, turned, branches):
        z = pl.program_id(0)

        @pl.when(z == 0)
        def _():
            for i, g in enumerate((gq, gk, gv)):
                turned[i * cols : (i + 1) * cols, :] = g[...]
            turned[3 * cols :, :] = raw[...].astype(bf16)
            for dev in range(count):
                for s in range(seqs):
                    to = (s * count + dev) * part
                    branches[:, to : to + part] = branch_ref[dev, :, s * part : (s + 1) * part]

        grad = dot(turned[...], normed_ref[...])
        forget = grad[3 * cols :]
        columns = grad[: 3 * cols].T
        out[0, :shard, : 3 * cols] = columns.astype(bf16)
        out[0, :shard, 3 * cols :] = dot_t(mixed_ref[...], branches[...]).astype(bf16)
        by_row = jnp.sum(columns * pack_ref[0, :, : 3 * cols].astype(f32), axis=1, keepdims=True)
        by_row = jnp.broadcast_to(by_row, (shard, 8)).T[:1]
        small = small_ref[0, :, :shard].astype(f32)
        by_row = by_row + jnp.sum(forget[:heads] * small[2 : 2 + heads], axis=0, keepdims=True)
        row = lax.broadcasted_iota(jnp.int32, (16, shard), 0)
        lane = lax.broadcasted_iota(jnp.int32, (16, shard), 1)
        more = jnp.where(row == heads, gain_ref[...], jnp.where(row == heads + 2, by_row / small[:1], 0.0))
        sums = jnp.sum(raw[...], axis=1, keepdims=True)
        for h in range(heads):
            head = me[0] * heads + h
            at = head // each_level * shard + head % each_level - z * shard
            more = more + jnp.where((row == heads + 1) & (lane == at), sums[h : h + 1, :], 0.0)
        out[0, shard : shard + 16, :shard] = jnp.where(row < heads, forget, more).astype(bf16)
        out[0, shard : shard + 16, shard:] = jnp.zeros((16, wide - shard), bf16)
        out[0, shard + 16 :, :] = jnp.zeros((16, wide), bf16)

    def whole(*shape):
        return pl.BlockSpec(shape, lambda z, me: (0,) * len(shape))

    return pl.pallas_call(
        kernel,
        grid_spec=pltpu.PrefetchScalarGridSpec(
            num_scalar_prefetch=1,
            grid=(depth,),
            in_specs=[whole(cols, tokens)] * 3
            + [
                whole(16, tokens),
                pl.BlockSpec((tokens, shard), lambda z, me: (0, z)),
                whole(count, own_out, piece),
                pl.BlockSpec((shard, tokens), lambda z, me: (z, 0)),
                pl.BlockSpec((1, shard), lambda z, me: (0, z)),
                pl.BlockSpec((1, shard, wide), lambda z, me: (z, 0, 0)),
                pl.BlockSpec((1, 16, wide), lambda z, me: (z, shard // 16, 0)),
            ],
            out_specs=pl.BlockSpec((1, shard + 32, wide), lambda z, me: (z, 0, 0)),
            scratch_shapes=[pltpu.VMEM((3 * cols + 16, tokens), bf16), pltpu.VMEM((own_out, tokens), bf16)],
        ),
        out_shape=jax.ShapeDtypeStruct((depth, shard + 32, wide), bf16),
        compiler_params=LARGE,
        cost_estimate=takes(12.0),
    )(me, *grads, raw, normed, branch, mixed, gain_row, pack, pack)


def out_turned(pack, cols, shard):
    depth, rows, wide = pack.shape

    def kernel(pack_ref, out):
        out[...] = pack_ref[0, :, 3 * cols :].T

    return pl.pallas_call(
        kernel,
        grid=(depth,),
        in_specs=[pl.BlockSpec((1, shard, wide), lambda z: (z, 0, 0))],
        out_specs=pl.BlockSpec((cols, shard), lambda z: (0, z)),
        out_shape=jax.ShapeDtypeStruct((cols, depth * shard), bf16),
        compiler_params=SMALL,
        cost_estimate=takes(2),
    )(pack)


def own_kernel(me, gate, up, down, out):
    rows, own = gate.shape[0], down.shape[0]
    out[:rows, :] = gate[...]
    out[rows : 2 * rows, :] = up[...]
    for k in range(down.shape[1] // (128 * pl.num_programs(0))):
        at = (k * pl.num_programs(0) + pl.program_id(0)) * 128
        out[2 * rows + k * own : 2 * rows + (k + 1) * own, :] = down[:, pl.ds(pl.multiple_of(at, 128), 128)]


def own_mlp(w_gate, w_up, w_down, depth, count, me):
    shard, ff = w_gate.shape
    own = w_down.shape[0] // count
    width = w_down.shape[1]
    ff_cols = depth * own
    if own == 128:
        strip = pl.BlockSpec((shard, 128), lambda z, me: (0, z * count + me[0]))
        total = 2 * shard + own * width // ff_cols
        return pl.pallas_call(
            own_kernel,
            grid_spec=pltpu.PrefetchScalarGridSpec(
                num_scalar_prefetch=1,
                grid=(depth,),
                in_specs=[strip, strip, pl.BlockSpec((own, width), lambda z, me: (me[0], 0))],
                out_specs=pl.BlockSpec((total, 128), lambda z, me: (0, z)),
            ),
            out_shape=jax.ShapeDtypeStruct((total, ff_cols), bf16),
            cost_estimate=takes(4.0),
        )(me.reshape(1), w_gate, w_up, w_down)

    def ff_columns(w):
        w = w.reshape(shard, depth, count, own)
        return lax.dynamic_index_in_dim(w, me, 2, keepdims=False).reshape(shard, ff_cols)

    down = lax.dynamic_slice_in_dim(w_down, me * own, own, 0)
    return jnp.concatenate([ff_columns(w_gate), ff_columns(w_up), stack_columns(down, ff_cols)], axis=0)


def contract(a, b, da, db):
    return lax.dot_general(a, b, (((da,), (db,)), ((), ())), preferred_element_type=f32)


def stack_columns(a, width):
    return jnp.concatenate([a[:, i : i + width] for i in range(0, a.shape[1], width)], axis=0)


def to_shards(grad):
    return lax.psum_scatter(grad, "fsdp", scatter_dimension=0, tiled=True)


def local_eight(
    inputs,
    gain_attn,
    w_query,
    w_key,
    w_value,
    w_forget,
    forget_bias,
    w_out,
    gain_mlp,
    w_gate,
    w_up,
    w_down,
    cotangent,
):
    axis = "ctx"
    count, me = lax.axis_size(axis), lax.axis_index(axis)
    depth, level = lax.axis_size("fsdp"), lax.axis_index("fsdp")
    seqs, rows, width = inputs.shape
    tokens = seqs * count * rows
    shard = width // depth
    heads = HEADS // count
    cols = heads * HEAD_DIM
    ff_own = w_down.shape[0] // count
    ff_cols = depth * ff_own
    own_out = width // count
    flat_in, flat_cot = inputs.reshape(seqs * rows, width), cotangent.reshape(seqs * rows, width)

    def token_slots(dev):
        return [(s * rows, rows, (s * count + dev) * rows) for s in range(seqs)]

    x_state = gather_start(flat_in, axis)
    own = own_attention(
        w_query, w_key, w_value, w_forget, forget_bias, w_out, (gain_attn, gain_mlp), heads, me, level
    )
    pack = lax.all_gather(own, "fsdp", axis=0)
    x_far = gather_far(x_state, axis)
    mlp = lax.all_gather(own_mlp(after(w_gate, x_far[3:]), w_up, w_down, depth, count, me), "fsdp", axis=0)
    g_state = gather_start(after(flat_cot, x_far[3:]), axis)
    x_pieces = gather_core_once(x_far, axis)
    pack = after(pack, g_state[1:])
    g_state = gather_far(g_state, axis)
    out_state = gather_start(out_turned(pack, cols, shard), axis)
    gains = pack[:, shard : shard + 2, :shard].astype(f32)
    gain_one, gain_two = gains[:, 0].reshape(width), gains[:, 1].reshape(width)

    x_all, normed, qkv, gate_raw = norm_project(x_pieces, pack, axis, seqs, cols)
    attn, mixed, totals, decay = attend(qkv, gate_raw, seqs, heads)
    mixed, g_state, out_state = lax.optimization_barrier((mixed, g_state, out_state))
    out_state = gather_far(out_state, axis)
    mixed_state = gather_start(mixed, axis)
    g_pieces = gather_core_once(g_state, axis)
    g_all = place(g_pieces, axis, tokens, token_slots)
    out_full = place(gather_core_once(out_state, axis), axis, width, lambda dev: [(0, own_out, dev * own_out)])
    mixed_state = gather_far(after(mixed_state, (g_all, out_full)), axis)
    mixed_pieces = gather_core(mixed_state, axis)
    mixed_all = place(mixed_pieces, axis, width, lambda dev: [(0, cols, dev * cols)])
    normed_two, hidden_own = hidden_norm(x_all, mixed_all, out_full, gain_two, seqs, rows, axis, True)

    inner, gate_up_grads, *sides = feed_forward(normed_two, g_all, mlp, axis, 0, seqs, seqs, ff_own)
    sides = [sides[4 * s : 4 * s + 4] for s in range(seqs)]
    back = Sums([side[:2] for side in sides], axis)
    grad_down = back.hold(contract(inner, g_all, 0, 0).astype(bf16))
    back.first()
    normed_two = back.hold(normed_two)
    back.send_first()
    result = Sums([after(side[2:], normed_two) for side in sides], axis)
    grad_gate_up = result.hold(contract(normed_two, gate_up_grads, 0, 0).astype(bf16))
    result.first()
    grad_gate_up, result.moving = back.hold((grad_gate_up, result.moving))
    back.second()
    back.send_second()
    back = back.result()
    grad_down, grad_gate_up = to_shards(grad_down), to_shards(grad_gate_up)

    grad_from_norm, grad_gain_two = norm_pull(hidden_own, gain_two, back)
    grad_hidden = flat_cot.astype(f32) + grad_from_norm
    branch = grad_hidden.astype(bf16)
    grad_mixed = contract(out_full, branch, 0, 1).astype(bf16).reshape(count, cols, seqs * rows)
    branch = after(branch, grad_mixed).T.reshape(count, own_out, seqs * rows)
    grad_mixed = result.hold(grad_mixed)
    grad_mixed = lax.all_to_all(grad_mixed, axis, 0, 0, tiled=True)
    result.send_first()
    grad_mixed, grad_down, branch = lax.optimization_barrier((grad_mixed, grad_down, branch))
    branch = lax.all_to_all(branch, axis, 0, 0, tiled=True)
    down_state = gather_start(grad_down, axis)
    gq, gk, gv, grad_raw = attend_pull(qkv, decay, grad_mixed, attn, totals, gate_raw, seqs, heads)

    down_state, branch, grad_gate_up, grad_raw = result.hold((down_state, branch, grad_gate_up, grad_raw))
    gate_up_state = gather_start(grad_gate_up, axis)
    down_state = gather_far(down_state, axis)
    grads = (gq, gk, gv)
    grad_pack = attention_grads(
        grads, grad_raw, normed, branch, mixed_all, grad_gain_two[None], pack, axis, seqs, depth, heads, HEADS // depth
    )
    grad_raw, down_state, gate_up_state, _ = lax.optimization_barrier((grad_raw, down_state, gate_up_state, grad_pack))
    gate_up_state = gather_far(gate_up_state, axis)
    result.hold(grad_pack)
    result.second()
    grad_raw = result.hold(grad_raw)
    result.send_second()
    down_pieces = gather_core(down_state, axis)
    pairs = project_back(grads, grad_raw, pack, width, axis, seqs)
    grad_pack = to_shards(grad_pack.reshape(-1, 4 * cols))
    pairs, gate_up_state, down_pieces = held(pairs, gate_up_state, down_pieces)
    grad_normed = Sums([pairs[2 * s : 2 * s + 2] for s in range(seqs)], axis)
    grad_normed.first()
    gate_up_state = result.hold(grad_normed.hold(gate_up_state))
    grad_normed.send_first()
    gate_up_pieces = gather_core(gate_up_state, axis)
    grad_down = place_wide(down_pieces, axis)
    grad_gate, grad_up = place_columns(gate_up_pieces, axis, depth, 2)
    grad_pack, _ = grad_normed.hold((grad_pack, (grad_down, grad_gate)))
    grad_normed.second()
    grad_normed.send_second()
    pack_state = gather_start(grad_pack, axis)
    pack_state = grad_normed.hold(pack_state)
    pack_state = gather_far(pack_state, axis)
    grad_in, _ = norm_pull(flat_in.astype(f32), gain_one, grad_normed.result())
    input_grad = (grad_hidden + grad_in).reshape(seqs, rows, width)
    output = (hidden_own + result.result()).astype(bf16).reshape(seqs, rows, width)
    pack_pieces = gather_core(after(pack_state, (input_grad, output)), axis)
    grad_query, grad_key, grad_value, grad_out, grad_forget, grad_gain_one, grad_gain_two, grad_bias = place_heads(
        pack_pieces, axis, shard, cols, heads, forget_bias.shape[0]
    )
    return (
        output,
        input_grad,
        grad_gain_one,
        grad_query,
        grad_key,
        grad_value,
        grad_forget,
        grad_bias,
        grad_out,
        grad_gain_two,
        grad_gate,
        grad_up,
        grad_down,
    )


def local_any(
    inputs,
    gain_attn,
    w_query,
    w_key,
    w_value,
    w_forget,
    forget_bias,
    w_out,
    gain_mlp,
    w_gate,
    w_up,
    w_down,
    cotangent,
):
    axis = "ctx"
    count, me = lax.axis_size(axis), lax.axis_index(axis)
    depth, level = lax.axis_size("fsdp"), lax.axis_index("fsdp")
    seqs, rows, width = inputs.shape
    tokens = seqs * count * rows
    shard = width // depth
    heads = -(-HEADS // count)
    cols = heads * HEAD_DIM
    ff_own = w_down.shape[0] // count
    ff_cols = depth * ff_own
    out_rows, own_out = shard // count, width // count
    flat_in, flat_cot = inputs.reshape(seqs * rows, width), cotangent.reshape(seqs * rows, width)

    def own_columns(w, each_head):
        w = jnp.pad(w, ((0, 0), (0, count * heads * each_head - w.shape[1])))
        return lax.dynamic_slice_in_dim(w, me * heads * each_head, heads * each_head, 1)

    extra = [own_columns(w_forget, 1), gain_attn[:, None], gain_mlp[:, None]]
    extra += [jnp.pad(forget_bias, (0, shard - forget_bias.shape[0]))[:, None]]
    extra += [jnp.zeros((shard, EXTRA - heads - 3), bf16)]
    pack = [own_columns(w, HEAD_DIM) for w in (w_query, w_key, w_value)] + extra
    pack = lax.all_gather(jnp.concatenate(pack, axis=1), "fsdp", axis=0, tiled=True)
    extra = pack[:, 3 * cols :]
    gain_one = extra[:, heads].astype(f32)
    gain_two = extra[:, heads + 1].astype(f32)
    biases = extra[:, heads + 2].reshape(depth, shard)[:, : forget_bias.shape[0]].reshape(-1)
    biases = jnp.pad(biases, (0, count * heads - HEADS))
    bias = lax.dynamic_slice_in_dim(biases, me * heads, heads).astype(f32)
    out_own = lax.all_gather(lax.dynamic_slice_in_dim(w_out, me * out_rows, out_rows, 0), "fsdp", axis=0)
    out_full = lax.all_gather(out_own, axis, axis=1).reshape(width, width)
    mlp = lax.all_gather(own_mlp(w_gate, w_up, w_down, depth, count, me), "fsdp", axis=0)

    x_all = lax.all_gather(inputs, axis, axis=1, tiled=True).reshape(tokens, width)
    x_wide = x_all.astype(f32)
    normed = (x_wide * inverse_rms(x_wide) * gain_one).astype(bf16)
    g_all = lax.all_gather(after(cotangent, normed), axis, axis=1, tiled=True).reshape(tokens, width)
    qkv = contract(pack[:, : 3 * cols], normed, 0, 1).astype(bf16)
    gate_raw = contract(extra, normed, 0, 1)[:heads] + bias[:, None]
    gate_raw = jnp.pad(gate_raw, ((0, -heads % 16), (0, 0)))
    attn, mixed, totals, decay = attend(qkv, gate_raw, seqs, heads)
    mixed_all = lax.all_gather(mixed, axis, axis=0, tiled=True)[:width]
    normed_two, hidden_own = hidden_norm(x_all, mixed_all, out_full, gain_two, seqs, rows, axis, False)

    def summed(part):
        return lax.psum_scatter(part.reshape(count, rows, width), axis, scatter_dimension=0).astype(f32)

    sides, sums = [], []
    for s in range(seqs):
        side = feed_forward(normed_two, g_all, mlp, axis, s, 1, seqs, ff_own)
        sides.append(side[:2])
        sums.append([summed(side[2]), summed(side[3])])
        normed_two = after(normed_two, sums[s])
    back, result = (jnp.concatenate(parts, axis=0) for parts in zip(*sums))
    inner = jnp.concatenate([side[0] for side in sides], axis=0)
    gate_up_grads = jnp.concatenate([side[1] for side in sides], axis=0)
    grad_down = to_shards(contract(inner, g_all, 0, 0).astype(bf16))
    grad_gate_up = to_shards(contract(normed_two, gate_up_grads, 0, 0).astype(bf16))
    output = (hidden_own + result).astype(bf16)

    grad_from_norm, grad_gain_two = norm_pull(hidden_own, gain_two, back)
    grad_hidden = flat_cot.astype(f32) + grad_from_norm
    branch = grad_hidden.astype(bf16)
    grad_mixed = contract(out_full, branch, 1, 1).astype(bf16)
    grad_mixed = jnp.pad(grad_mixed, ((0, count * cols - width), (0, 0)))
    grad_mixed = lax.all_to_all(grad_mixed.reshape(count, cols, seqs * rows), axis, 0, 0, tiled=True)
    branch = lax.all_to_all(branch.T.reshape(count, own_out, seqs * rows), axis, 0, 0, tiled=True)
    branch = branch.reshape(count, own_out, seqs, rows).transpose(1, 2, 0, 3).reshape(own_out, tokens)
    grad_out = contract(branch, mixed_all, 1, 1)
    gq, gk, gv, grad_raw = attend_pull(qkv, decay, grad_mixed, attn, totals, gate_raw, seqs, heads)
    grad_raw = jnp.pad(grad_raw[:heads].astype(bf16), ((0, EXTRA - heads), (0, 0)))
    grads = jnp.concatenate([gq, gk, gv, grad_raw], axis=0)
    grad_normed = contract(grads, pack, 0, 1).astype(bf16).reshape(seqs, count * rows, width)
    grad_normed = jnp.concatenate([summed(part) for part in grad_normed], axis=0)

    grad_pack = contract(grads, normed, 1, 0)
    head_at = me * heads + jnp.arange(heads)
    bias_col = head_at // (HEADS // depth) * shard + head_at % (HEADS // depth)
    bias_sum = jnp.where(head_at < HEADS, jnp.sum(grad_raw[:heads].astype(f32), axis=1), 0.0)
    at_col = jnp.arange(width)[None, :] == bias_col[:, None]
    bias_row = jnp.sum(jnp.where(at_col, bias_sum[:, None], 0.0), axis=0, keepdims=True)
    tail = [grad_pack[3 * cols : 3 * cols + heads], grad_gain_two[None], bias_row]
    tail += [jnp.zeros((EXTRA - heads - 2, width), f32)]
    grad_pack = jnp.concatenate([grad_pack[: 3 * cols]] + tail + [grad_out], axis=0).astype(bf16)
    grad_pack = to_shards(grad_pack.reshape(-1, depth, shard).transpose(1, 0, 2).reshape(-1, shard))
    grad_pack = lax.all_gather(grad_pack, axis)
    out_at = 3 * cols + EXTRA

    def turned(start, size):
        return grad_pack[:, start : start + size].reshape(-1, shard)[:width].T.astype(f32)

    tail = grad_pack[:, 3 * cols : out_at].astype(f32)
    tail_sum = jnp.sum(tail[:, heads : heads + 2], axis=0)
    grad_down = lax.all_gather(grad_down, axis, axis=0, tiled=True).astype(f32)
    grad_gate_up = lax.all_gather(grad_gate_up.reshape(shard, 2, depth, ff_own), axis)
    grad_gate_up = grad_gate_up.transpose(2, 1, 3, 0, 4).reshape((2,) + w_gate.shape).astype(f32)
    grad_in, grad_gain_one = norm_pull(flat_in.astype(f32), gain_one, grad_normed)
    grad_gain_one = lax.psum(grad_gain_one, (axis, "fsdp"))
    return (
        output.reshape(seqs, rows, width),
        (grad_hidden + grad_in).reshape(seqs, rows, width),
        lax.dynamic_slice_in_dim(grad_gain_one, level * shard, shard),
        turned(0, cols),
        turned(cols, cols),
        turned(2 * cols, cols),
        tail[:, :heads].reshape(count * heads, shard)[:HEADS].T,
        tail_sum[1, : forget_bias.shape[0]],
        turned(out_at, own_out),
        tail_sum[0],
        grad_gate_up[0],
        grad_gate_up[1],
        grad_down,
    )


def solution(mesh):
    split, first, rest = P("fsdp", "ctx", None), P("fsdp"), P("fsdp", None)
    return jax.shard_map(
        local_eight if mesh.shape["ctx"] == 8 else local_any,
        mesh=mesh,
        in_specs=(split, first, rest, rest, rest, rest, first, rest, first, rest, rest, rest, split),
        out_specs=(split, split, first, rest, rest, rest, rest, first, rest, first, rest, rest, rest),
        check_vma=False,
    )
```

```python
import jax
import jax.numpy as jnp
from jax import lax
from jax.experimental import pallas as pl
from jax.experimental.pallas import tpu as pltpu
from jax.sharding import PartitionSpec as P

HEADS = 24
HEAD_DIM = 64
BLK = 256
EXTRA = 64
norm_eps = 1e-06
bf16 = jnp.bfloat16
f32 = jnp.float32


def exchange(x, axis, mask):
    return lax.ppermute(x, axis, [(i, i ^ mask) for i in range(lax.axis_size(axis))])


def after(x, done):
    return lax.optimization_barrier((x, done))[0]


def first_half(rows):
    return -(-rows // 32) * 16


def gather_start(x, axis):
    return x, exchange(x, axis, 2), exchange(x, axis, 4)


def gather_far(state, axis):
    x, side, above = state
    half = first_half(x.shape[0])
    return x, side, above, exchange(side[:half], axis, 4), exchange(above[half:], axis, 2)


def gather_core_once(state, axis):
    size = state[0].shape[0]
    half = first_half(size)
    all_rows = jnp.concatenate(state, axis=0)
    other = exchange(all_rows, axis, 1)
    places = ((0, 0, size), (2, 0, size), (4, 0, size), (6, 0, half), (6, half, size - half))
    pieces = [place + (array,) for place, array in zip(places, state)]
    return pieces + [(mask ^ 1, 0, size, other, i * size) for i, mask in enumerate((0, 2, 4, 6))]


def gather_core(state, axis):
    size = state[0].shape[0]
    half = first_half(size)
    places = ((0, 0, size), (2, 0, size), (4, 0, size), (6, 0, half), (6, half, size - half))
    pieces = [place + (array,) for place, array in zip(places, state)]
    return pieces + [(mask ^ 1, start, rows, exchange(a, axis, 1)) for mask, start, rows, a in pieces]


def held(first, second, pieces):
    first, second, arrays = lax.optimization_barrier((first, second, arrays_of(pieces)))
    return first, second, [piece[:3] + (array,) for piece, array in zip(pieces, arrays)]


def arrays_of(pieces):
    return [piece[3] for piece in pieces]


ANY = pl.BlockSpec(memory_space=pl.ANY)
LIMIT = pltpu.CompilerParams(vmem_limit_bytes=48 * 2**20)


def takes(us):
    return pl.CostEstimate(flops=int(us * 1.15e9), bytes_accessed=int(us * 1e5), transcendentals=0)


LARGE = pltpu.CompilerParams(vmem_limit_bytes=60 * 2**20)
SMALL = pltpu.CompilerParams(vmem_limit_bytes=24 * 2**20)


def copy_all(copies, sems):
    started = [pltpu.make_async_copy(source, target, sems.at[i]) for i, (source, target) in enumerate(copies)]
    for copy in started:
        copy.start()
    for copy in started:
        copy.wait()


def rows_at(ref, start, size):
    return ref.at[pl.ds(start if isinstance(start, int) else pl.multiple_of(start, 16), size)]


def slices_of(pieces, me, slots):
    copies = []
    for k, (mask, first, size, _, *at) in enumerate(pieces):
        for start, rows, target in slots(me ^ mask):
            low, high = max(start, first), min(start + rows, first + size)
            if low < high:
                copies.append((k, low - first + sum(at), high - low, target + (low - start)))
    return copies


def place(pieces, axis, total, slots):
    arrays = [p[3] for p in pieces]
    width, dtype = arrays[0].shape[1], arrays[0].dtype
    me = lax.axis_index(axis).reshape(1)

    def kernel(me, *refs):
        out, sems = refs[-2:]
        copies = slices_of(pieces, me[0], slots)
        copy_all([(refs[k].at[pl.ds(s, size)], rows_at(out, t, size)) for k, s, size, t in copies], sems)

    return pl.pallas_call(
        kernel,
        in_specs=[pl.BlockSpec(memory_space=pltpu.SMEM)] + [ANY] * len(arrays),
        out_specs=pl.BlockSpec(memory_space=pltpu.VMEM),
        out_shape=jax.ShapeDtypeStruct((total, width), dtype),
        scratch_shapes=[pltpu.SemaphoreType.DMA((len(slices_of(pieces, 0, slots)),))],
        compiler_params=LIMIT,
        cost_estimate=takes(5.0),
    )(me, *arrays)


def add_first(parts):
    rows, width = parts[0][0].shape[1:]

    def kernel(*refs):
        for h in range(2):
            refs[4 + h][...] = (refs[2 * h][...].astype(f32) + refs[2 * h + 1][...].astype(f32)).astype(bf16)

    blocks = [pl.BlockSpec((1, rows, width), at) for at in (lambda g: (2 * g + 1, 0, 0), lambda g: (g + 2, 0, 0))]
    return pl.pallas_call(
        kernel,
        grid=(2,),
        in_specs=[blocks[0]] * 2 + [blocks[1]] * 2,
        out_specs=[pl.BlockSpec((1, rows, width), lambda g: (g, 0, 0))] * 2,
        out_shape=[jax.ShapeDtypeStruct((2, rows, width), bf16)] * 2,
        compiler_params=LARGE,
        cost_estimate=takes(3),
    )(*parts[0], *parts[1])


def add_second(parts):
    rows, width = parts[0][0].shape[1:]
    part = rows // 2

    def kernel(*refs):
        for h in range(2):
            keep, core, moved = (ref[0].astype(f32) for ref in refs[3 * h : 3 * h + 3])
            refs[6 + h][...] = (keep + core + moved).astype(bf16)

    def block(at):
        return pl.BlockSpec((1, part, width), lambda g: (at, g, 0))

    return pl.pallas_call(
        kernel,
        grid=(rows // part,),
        in_specs=[block(2), block(2), block(1), block(1), block(1), block(1)],
        out_specs=[pl.BlockSpec((part, width), lambda g: (g, 0))] * 2,
        out_shape=[jax.ShapeDtypeStruct((rows, width), bf16)] * 2,
        compiler_params=LARGE,
        cost_estimate=takes(3),
    )(*parts[0], *parts[1])


class Sums:
    def __init__(self, pairs, axis):
        self.axis = axis
        self.parts = [[keep] for keep, _ in pairs]
        self.moving = [exchange(send, axis, 1) for _, send in pairs]

    def hold(self, others):
        self.moving, others = lax.optimization_barrier((self.moving, others))
        return others

    def arrived(self):
        for part, moved in zip(self.parts, self.moving):
            part.append(moved)

    def first(self):
        self.arrived()
        self.moving = list(add_first(self.parts))

    def send_first(self):
        self.moving = [exchange(m, self.axis, (2, 4)[h % 2]) for h, m in enumerate(self.moving)]

    def second(self):
        self.arrived()
        self.moving = list(add_second(self.parts))

    def send_second(self):
        self.moving = [exchange(m, self.axis, (4, 2)[h % 2]) for h, m in enumerate(self.moving)]

    def result(self):
        sums = [sum(p[0].astype(f32) for p in part) for part in self.parts]
        return jnp.concatenate([s + m.astype(f32) for s, m in zip(sums, self.moving)], axis=0)


def each(count, body, carry):
    if count <= 3:
        return body(pl.ds(0, count * BLK), carry) if count else carry
    return lax.fori_loop(0, count, lambda j, carry: body(span(j), carry), carry)


def span(j):
    return pl.ds(j * BLK if isinstance(j, int) else pl.multiple_of(j * BLK, BLK), BLK)


def dot(a, b):
    return jnp.dot(a, b, preferred_element_type=f32)


def dot_t(a, b):
    return lax.dot_general(a, b, (((1,), (1,)), ((), ())), preferred_element_type=f32)


def running_sum(rows, backward):
    length = rows.shape[1]
    lane = lax.broadcasted_iota(jnp.int32, rows.shape, 1)
    step = 1
    while step < length:
        moved = pltpu.roll(rows, length - step if backward else step, 1)
        inside = lane < length - step if backward else lane >= step
        rows = rows + jnp.where(inside, moved, 0.0)
        step *= 2
    return rows


def log_sigmoid(x):
    return jnp.minimum(x, 0.0) - jnp.log1p(jnp.exp(-jnp.abs(x)))


def head_rows(h, part=0):
    return slice(part + h * HEAD_DIM, part + (h + 1) * HEAD_DIM)


def attend(qkv, gate_raw, seqs, heads):
    length, cols = qkv.shape[1] // seqs, heads * HEAD_DIM
    lines = gate_raw.shape[0]

    def kernel(qkv_ref, raw_ref, attn_ref, mixed_ref, total_ref, decay_ref, k_rows, decay_cols):
        decay = running_sum(log_sigmoid(raw_ref[...]), False)
        decay_ref[...] = decay
        decay_cols[...] = decay.T
        total_ref[...] = jnp.ones_like(total_ref)
        for h in range(heads):
            k_rows[h] = qkv_ref[head_rows(h, cols), :].T

        for i in range(length // BLK):
            for h in range(heads):
                at = span(i)
                query = qkv_ref[head_rows(h), at] * 0.125
                decay_q = decay_ref[h : h + 1, at]

                def visit(keys, carry, last=False):
                    summed, total = carry
                    offset = decay_q - decay_cols[keys, h : h + 1]
                    if last:
                        offset = -jnp.abs(offset)
                    terms = jnp.exp(dot(k_rows[h, keys, :], query) + offset)
                    total = total + jnp.sum(terms, axis=0, keepdims=True)
                    return summed + dot(qkv_ref[head_rows(h, 2 * cols), keys], terms.astype(bf16)), total

                start = (jnp.zeros((HEAD_DIM, BLK), f32), jnp.zeros((1, BLK), f32))
                summed, total = visit(at, each(i, visit, start), True)
                attn = summed / total
                attn_ref[head_rows(h), at] = attn
                mixed_ref[head_rows(h), at] = attn.astype(bf16)
                total_ref[h : h + 1, at] = total

    def block(rows):
        return pl.BlockSpec((rows, length), lambda s: (0, s))

    tokens = seqs * length
    return pl.pallas_call(
        kernel,
        grid=(seqs,),
        in_specs=[block(3 * cols), block(lines)],
        out_specs=[block(cols), block(cols), block(lines), block(lines)],
        out_shape=[
            jax.ShapeDtypeStruct((cols, tokens), f32),
            jax.ShapeDtypeStruct((cols, tokens), bf16),
            jax.ShapeDtypeStruct((lines, tokens), f32),
            jax.ShapeDtypeStruct((lines, tokens), f32),
        ],
        scratch_shapes=[pltpu.VMEM((heads, length, HEAD_DIM), bf16), pltpu.VMEM((length, lines), f32)],
        compiler_params=SMALL,
        cost_estimate=takes(9.0),
    )(qkv, gate_raw)


def attend_pull(qkv, decay, grad_mixed, attn, totals, gate_raw, seqs, heads):
    length, cols = qkv.shape[1] // seqs, heads * HEAD_DIM
    lines = gate_raw.shape[0]
    pieces = grad_mixed.shape[0]
    piece = length // pieces
    deep = HEAD_DIM + 16

    def kernel(
        qkv_ref, decay_ref, gm_ref, attn_ref, total_ref, raw_ref, gq_ref, gk_ref, gv_ref, graw_ref,
        k_rows, v_rows, decay_cols, q_more, k_more, gs_all, delta_all, gk_sum, gv_sum, gd_all,
    ):
        decay_cols[...] = decay_ref[...].T
        gd_all[...] = jnp.zeros_like(gd_all)
        gk_sum[...] = jnp.zeros_like(gk_sum)
        gv_sum[...] = jnp.zeros_like(gv_sum)
        more = (lax.broadcasted_iota(jnp.int32, (16, length), 0) == 0).astype(bf16)
        for h in range(heads):
            k_rows[h] = qkv_ref[head_rows(h, cols), :].T
            v_rows[h] = qkv_ref[head_rows(h, 2 * cols), :].T
            k_more[h, :HEAD_DIM, :] = qkv_ref[head_rows(h, cols), :]
            k_more[h, HEAD_DIM:, :] = more
            q_more[h, :HEAD_DIM, :] = qkv_ref[head_rows(h), :] * 0.125
            q_more[h, HEAD_DIM:, :] = more
            for p in range(pieces):
                at = slice(p * piece, (p + 1) * piece)
                grad = gm_ref[p, head_rows(h), :].astype(f32)
                total = total_ref[h : h + 1, at]
                gs_all[head_rows(h), at] = (grad / total).astype(bf16)
                delta_all[h : h + 1, at] = jnp.sum(grad * attn_ref[head_rows(h), at], axis=0, keepdims=True) / total

        key_first = lax.broadcasted_iota(jnp.int32, (BLK, BLK), 0) <= lax.broadcasted_iota(
            jnp.int32, (BLK, BLK), 1
        )
        ones = (lax.broadcasted_iota(jnp.int32, (16, BLK), 0) == 0).astype(bf16)

        for i in range(length // BLK):
            for h in range(heads):
                at = span(i)
                query = q_more[h, :HEAD_DIM, at]
                decay_q = decay_ref[h : h + 1, at]
                gs = gs_all[head_rows(h), at]
                delta = delta_all[h : h + 1, at]

                def terms_of(keys, last):
                    offset = decay_q - decay_cols[keys, h : h + 1]
                    if last:
                        offset = -jnp.abs(offset)
                    terms = jnp.exp(dot(k_rows[h, keys, :], query) + offset)
                    grads = (terms * (dot(v_rows[h, keys, :], gs) - delta)).astype(bf16)
                    gv_sum[head_rows(h), keys] += dot_t(gs, terms.astype(bf16))
                    return grads

                def visit(keys, carry):
                    grads = terms_of(keys, False)
                    gk_sum[h, :, keys] += dot_t(q_more[h, :, at], grads)
                    return carry + dot(k_more[h, :, keys], grads)

                gq = each(i, visit, jnp.zeros((deep, BLK), f32))
                grads = terms_of(at, True)
                gk_sum[h, :HEAD_DIM, at] += dot_t(query, grads)
                gq_own = gq[:HEAD_DIM] + dot(k_more[h, :HEAD_DIM, at], grads)
                signed = jnp.where(key_first, grads, -grads)
                gk_sum[h, HEAD_DIM:, at] += dot_t(ones, signed)
                gd_all[h : h + 1, at] = (gq[HEAD_DIM:] + dot(ones, signed))[:1]
                gq_ref[head_rows(h), at] = (gq_own * 0.125).astype(bf16)

        for h in range(heads):
            gk_ref[head_rows(h), :] = gk_sum[h, :HEAD_DIM, :].astype(bf16)
            gd_all[h : h + 1, :] = gd_all[h : h + 1, :] - gk_sum[h, HEAD_DIM : HEAD_DIM + 1, :]
        gv_ref[...] = gv_sum[...].astype(bf16)
        grad_log = running_sum(gd_all[...], True)
        graw_ref[...] = (grad_log * jax.nn.sigmoid(-raw_ref[...])).astype(bf16).astype(f32)

    def block(rows):
        return pl.BlockSpec((rows, length), lambda s: (0, s))

    tokens = seqs * length
    shape = jax.ShapeDtypeStruct((cols, tokens), bf16)
    return pl.pallas_call(
        kernel,
        grid=(seqs,),
        in_specs=[
            block(3 * cols),
            block(lines),
            pl.BlockSpec((pieces, cols, piece), lambda s: (0, 0, s)),
            block(cols),
            block(lines),
            block(lines),
        ],
        out_specs=[block(cols), block(cols), block(cols), block(lines)],
        out_shape=[shape, shape, shape, jax.ShapeDtypeStruct((lines, tokens), f32)],
        scratch_shapes=[
            pltpu.VMEM((heads, length, HEAD_DIM), bf16),
            pltpu.VMEM((heads, length, HEAD_DIM), bf16),
            pltpu.VMEM((length, lines), f32),
            pltpu.VMEM((heads, deep, length), bf16),
            pltpu.VMEM((heads, deep, length), bf16),
            pltpu.VMEM((cols, length), bf16),
            pltpu.VMEM((lines, length), f32),
            pltpu.VMEM((heads, deep, length), f32),
            pltpu.VMEM((cols, length), f32),
            pltpu.VMEM((lines, length), f32),
        ],
        compiler_params=LARGE,
        cost_estimate=takes(19.0),
    )(qkv, decay, grad_mixed, attn, totals, gate_raw)


def inverse_rms(rows):
    return lax.rsqrt(jnp.mean(rows * rows, axis=-1, keepdims=True) + norm_eps)


def norm_pull(rows, gain, grad):
    scale = inverse_rms(rows)
    weighted = grad * gain
    inner = jnp.mean(rows * weighted, axis=-1, keepdims=True)
    return scale * weighted - rows * (scale * scale * scale * inner), jnp.sum(grad * rows * scale, axis=0)


def place_columns(pieces, axis, parts, both):
    arrays = [p[3] for p in pieces]
    rows, width = arrays[0].shape
    count = 8
    me = lax.axis_index(axis).reshape(1)

    def slots(dev):
        return [(0, rows, dev * rows)]

    def kernel(me, *refs):
        outs, (held, sems) = refs[len(arrays) : -2], refs[-2:]

        @pl.when(pl.program_id(0) == 0)
        def _():
            copies = slices_of(pieces, me[0], slots)
            copy_all([(refs[k].at[pl.ds(s, size)], rows_at(held, t, size)) for k, s, size, t in copies], sems)

        for b, out in enumerate(outs):
            at = pl.multiple_of((b * parts + pl.program_id(0)) * 128, 128)
            for dev in range(count):
                out[:, dev * 128 : (dev + 1) * 128] = held[dev * rows : (dev + 1) * rows, pl.ds(at, 128)].astype(f32)

    return pl.pallas_call(
        kernel,
        grid_spec=pltpu.PrefetchScalarGridSpec(
            num_scalar_prefetch=1,
            grid=(parts,),
            in_specs=[ANY] * len(arrays),
            out_specs=[pl.BlockSpec((rows, count * 128), lambda p, me: (0, p))] * both,
            scratch_shapes=[pltpu.VMEM((count * rows, width), bf16), pltpu.SemaphoreType.DMA((len(arrays),))],
        ),
        out_shape=[jax.ShapeDtypeStruct((rows, parts * count * 128), f32)] * both,
        compiler_params=LIMIT,
        cost_estimate=takes(7.0),
    )(me, *arrays)


def place_wide(pieces, axis):
    arrays = [p[3] for p in pieces]
    rows, width = arrays[0].shape
    count = 8
    me = lax.axis_index(axis).reshape(1)

    def kernel(me, *refs):
        out, held, sems = refs[-3:]

        @pl.when(pl.program_id(0) == 0)
        def _():
            copies = slices_of(pieces, me[0], lambda dev: [(0, rows, dev * rows)])
            copy_all([(refs[k].at[pl.ds(s, size)], rows_at(held, t, size)) for k, s, size, t in copies], sems)

        out[...] = held[pl.ds(pl.multiple_of(pl.program_id(0) * rows, rows), rows), :].astype(f32)

    return pl.pallas_call(
        kernel,
        grid_spec=pltpu.PrefetchScalarGridSpec(
            num_scalar_prefetch=1,
            grid=(count,),
            in_specs=[ANY] * len(arrays),
            out_specs=pl.BlockSpec((rows, width), lambda p, me: (p, 0)),
            scratch_shapes=[pltpu.VMEM((count * rows, width), bf16), pltpu.SemaphoreType.DMA((len(arrays),))],
        ),
        out_shape=jax.ShapeDtypeStruct((count * rows, width), f32),
        compiler_params=LIMIT,
        cost_estimate=takes(6.0),
    )(me, *arrays)


def place_heads(pieces, axis, shard, cols, heads, biases):
    arrays = arrays_of(pieces)
    rows, wide = arrays[0].shape
    count, parts = 8, wide // cols
    me = lax.axis_index(axis).reshape(1)

    def slots(dev):
        return [(0, rows, dev * rows)]

    def kernel(me, *refs):
        forget, gain_one, gain_two, bias, held, turned, sems = refs[-7:]
        refs, outs = refs[: len(arrays)], refs[len(arrays) : -7]

        @pl.when(pl.program_id(0) == 0)
        def _():
            copies = slices_of(pieces, me[0], slots)
            copy_all([(refs[k].at[pl.ds(s, size)], rows_at(held, t, size)) for k, s, size, t in copies], sems)
            tails = [held[dev * rows + shard : dev * rows + shard + 16, :shard].astype(f32) for dev in range(count)]
            for dev in range(count):
                turned[dev * heads : (dev + 1) * heads, :] = tails[dev][:heads]
            forget[...] = turned[...].T
            total = sum(tails)
            gain_two[...] = total[heads]
            bias[...] = total[heads + 1, :biases]
            gain_one[...] = total[heads + 2]

        strip = outs[0].shape[0]
        for dev in range(count):
            block = held[pl.ds(pl.multiple_of(dev * rows + pl.program_id(0) * strip, 16), strip), :].astype(f32)
            for part, out in enumerate(outs):
                out[:, dev * cols : (dev + 1) * cols] = block[:, part * cols : (part + 1) * cols]

    steps = 4
    return pl.pallas_call(
        kernel,
        grid_spec=pltpu.PrefetchScalarGridSpec(
            num_scalar_prefetch=1,
            grid=(steps,),
            in_specs=[ANY] * len(arrays),
            out_specs=[pl.BlockSpec((shard // steps, count * cols), lambda g, me: (g, 0))] * parts
            + [
                pl.BlockSpec((shard, count * heads), lambda g, me: (0, 0)),
                pl.BlockSpec((shard,), lambda g, me: (0,)),
                pl.BlockSpec((shard,), lambda g, me: (0,)),
                pl.BlockSpec((biases,), lambda g, me: (0,)),
            ],
            scratch_shapes=[
                pltpu.VMEM((count * rows, wide), bf16),
                pltpu.VMEM((count * heads, shard), f32),
                pltpu.SemaphoreType.DMA((len(arrays),)),
            ],
        ),
        out_shape=[jax.ShapeDtypeStruct((shard, count * cols), f32)] * parts
        + [jax.ShapeDtypeStruct(s, f32) for s in ((shard, count * heads), (shard,), (shard,), (biases,))],
        compiler_params=LIMIT,
        cost_estimate=takes(6.0),
    )(me, *arrays)


def own_attention(w_query, w_key, w_value, w_forget, forget_bias, w_out, gains, heads, me, level):
    shard = w_query.shape[0]
    cols = heads * HEAD_DIM
    each_level = forget_bias.shape[0]

    def kernel(at, wq, wk, wv, wo, wf, gain_one, gain_two, bias, out):
        for odd in range(2):

            @pl.when(at[0] % 2 == odd)
            def _():
                for i, w in enumerate((wq, wk, wv, wo)):
                    out[:shard, i * cols : (i + 1) * cols] = w[:, odd * cols : (odd + 1) * cols]

        row = lax.broadcasted_iota(jnp.int32, (16, shard), 0)
        gain_one, gain_two = (jnp.broadcast_to(g[...].astype(f32)[None], (16, shard)) for g in (gain_one, gain_two))
        rows = jnp.where(row == 0, gain_one, jnp.where(row == 1, gain_two, 0.0))
        head = lax.broadcasted_iota(jnp.int32, (16, HEADS), 1)
        slot = lax.broadcasted_iota(jnp.int32, (16, HEADS), 0)
        chosen = ((head == at[0] * heads + slot - 2) & (slot >= 2) & (slot < heads + 2)).astype(bf16)
        out[shard:, :shard] = (rows + dot(chosen, wf[...])).astype(bf16)
        row = lax.broadcasted_iota(jnp.int32, (16, each_level), 0)
        lane = lax.broadcasted_iota(jnp.int32, (16, each_level), 1)
        mine = (at[1] * each_level + lane == at[0] * heads + row) & (row < heads)
        column = jnp.sum(jnp.where(mine, bias[...].astype(f32), 0.0), axis=1, keepdims=True)
        out[shard:, shard:] = jnp.broadcast_to(column, (16, 4 * cols - shard)).astype(bf16)

    pair = pl.BlockSpec((shard, 2 * cols), lambda i, at: (0, at[0] // 2))
    line = pl.BlockSpec((shard,), lambda i, at: (0,))

    def whole(*shape):
        return pl.BlockSpec(shape, lambda i, at: (0, 0))

    return pl.pallas_call(
        kernel,
        grid_spec=pltpu.PrefetchScalarGridSpec(
            num_scalar_prefetch=1,
            grid=(1,),
            in_specs=[pair] * 4 + [whole(HEADS, shard), line, line, whole(1, each_level)],
            out_specs=whole(shard + 16, 4 * cols),
        ),
        out_shape=jax.ShapeDtypeStruct((shard + 16, 4 * cols), bf16),
        compiler_params=LARGE,
        cost_estimate=takes(3.0),
    )(
        jnp.stack([me, level]), w_query, w_key, w_value, w_out, w_forget.T, *gains, forget_bias.reshape(1, -1)
    )


def norm_project(pieces, pack, axis, seqs, cols):
    arrays = [p[3] for p in pieces]
    rows, width = arrays[0].shape[0] // seqs, arrays[0].shape[1]
    count, depth, wide = 8, pack.shape[0], pack.shape[2]
    shard = width // depth
    tokens = seqs * count * rows
    tile, heads = 2 * rows, cols // HEAD_DIM
    me = lax.axis_index(axis).reshape(1)

    def slots(dev):
        return [(s * rows, rows, (s * count + dev) * rows) for s in range(seqs)]

    number = len(slices_of(pieces, 0, slots))

    def kernel(me, pack_ref, *refs):
        x_out, out, qkv_out, raw_out, held, weights, turned, small, gain, sems = refs[-10:]
        step = pl.program_id(0)

        @pl.when(step == 0)
        def _():
            copies = []
            for z in range(depth):
                copies.append((pack_ref.at[z, pl.ds(0, shard)], rows_at(weights, z * shard, shard)))
                copies.append((pack_ref.at[z, pl.ds(pack.shape[1] - 16, 16)], small.at[z]))
            for k, s, size, t in slices_of(pieces, me[0], slots):
                copies.append((refs[k].at[pl.ds(s, size)], rows_at(held, t, size)))
            copy_all(copies, sems)
            turned[: 3 * cols, :] = weights[:, : 3 * cols].T
            row = lax.broadcasted_iota(jnp.int32, (16, shard), 0)
            for z in range(depth):
                at = slice(z * shard, (z + 1) * shard)
                rows = small[z, :, :shard].astype(f32)
                gain[:, at] = rows
                moved = jnp.concatenate([rows[2:], rows[:2]], axis=0)
                turned[3 * cols :, at] = jnp.where(row < heads, moved, 0.0).astype(bf16)

        bias = sum(small[z, :, shard:].astype(f32) for z in range(depth))[:, :1]
        block = held[pl.ds(pl.multiple_of(step * tile, tile), tile), :]
        x_out[...] = block
        x = block.astype(f32)
        normed = (x * inverse_rms(x) * gain[:1, :]).astype(bf16)
        out[...] = normed
        projected = dot_t(turned[...], normed)
        qkv_out[...] = projected[: 3 * cols].astype(bf16)
        raw_out[...] = projected[3 * cols :] + bias

    spec = pl.BlockSpec((tile, width), lambda p, me: (p, 0))
    shape = jax.ShapeDtypeStruct((tokens, width), bf16)
    return pl.pallas_call(
        kernel,
        grid_spec=pltpu.PrefetchScalarGridSpec(
            num_scalar_prefetch=1,
            grid=(tokens // tile,),
            in_specs=[ANY] * (1 + len(arrays)),
            out_specs=[
                spec,
                spec,
                pl.BlockSpec((3 * cols, tile), lambda p, me: (0, p)),
                pl.BlockSpec((16, tile), lambda p, me: (0, p)),
            ],
            scratch_shapes=[
                pltpu.VMEM((tokens, width), bf16),
                pltpu.VMEM((width, wide), bf16),
                pltpu.VMEM((3 * cols + 16, width), bf16),
                pltpu.VMEM((depth, 16, wide), bf16),
                pltpu.VMEM((16, width), f32),
                pltpu.SemaphoreType.DMA((number + 2 * depth,)),
            ],
        ),
        out_shape=[
            shape,
            shape,
            jax.ShapeDtypeStruct((3 * cols, tokens), bf16),
            jax.ShapeDtypeStruct((16, tokens), f32),
        ],
        compiler_params=LIMIT,
        cost_estimate=takes(12.0),
    )(me, pack, *arrays)


def hidden_norm(x_all, mixed_all, w_out, gain, seqs, rows, axis, turned):
    tokens, width = x_all.shape
    tile = 4 * rows
    tiles = tokens // seqs // tile
    me = lax.axis_index(axis).reshape(1)

    def kernel(me, x_ref, mixed_ref, w_ref, gain_ref, out_ref, own_ref, hidden_ref):
        parts = [slice(2 * i * rows, 2 * (i + 1) * rows) for i in range(2)]
        for at in parts:
            hidden_ref[at, :] = x_ref[at, :].astype(f32) + (dot_t if turned else dot)(mixed_ref[:, at].T, w_ref[...])
        for at in parts:
            hidden = hidden_ref[at, :]
            out_ref[at, :] = (hidden * inverse_rms(hidden) * gain_ref[...]).astype(bf16)

        @pl.when(pl.program_id(1) == me[0] // 4)
        def _():
            own_ref[...] = hidden_ref[pl.ds(pl.multiple_of(me[0] % 4 * rows, rows), rows), :]

    return pl.pallas_call(
        kernel,
        grid_spec=pltpu.PrefetchScalarGridSpec(
            num_scalar_prefetch=1,
            grid=(seqs, tiles),
            in_specs=[
                pl.BlockSpec((tile, width), lambda s, t, me: (s * tiles + t, 0)),
                pl.BlockSpec((width, tile), lambda s, t, me: (0, s * tiles + t)),
                pl.BlockSpec((width, width), lambda s, t, me: (0, 0)),
                pl.BlockSpec((1, width), lambda s, t, me: (0, 0)),
            ],
            out_specs=[
                pl.BlockSpec((tile, width), lambda s, t, me: (s * tiles + t, 0)),
                pl.BlockSpec((rows, width), lambda s, t, me: (s, 0)),
            ],
            scratch_shapes=[pltpu.VMEM((tile, width), f32)],
        ),
        out_shape=[jax.ShapeDtypeStruct((tokens, width), bf16), jax.ShapeDtypeStruct((seqs * rows, width), f32)],
        compiler_params=LARGE,
        cost_estimate=takes(17.0),
    )(me, x_all, mixed_all, w_out, gain.reshape(1, width))


def split_pair(value, keep_ref, send_ref, me):
    rows = value.shape[0] // 4
    blocks = [value[i * rows : (i + 1) * rows] for i in range(4)]
    core, side = me % 2 == 0, me // 2 % 2 == 0
    for t in range(2):
        first, second = (jnp.where(side, blocks[2 * t + c], blocks[2 - 2 * t + c]) for c in range(2))
        keep_ref[t] = jnp.where(core, first, second).astype(bf16)
        send_ref[t] = jnp.where(core, second, first).astype(bf16)


def pair_specs(paired, tile, tiles, width):
    if paired:
        block = pl.BlockSpec((2, tile // 4, width), lambda t, me: (t, 0, 0))
        shape = jax.ShapeDtypeStruct((2 * tiles, tile // 4, width), bf16)
        return (lambda t, me: me[0] // 4 ^ t), [block] * 2, [shape] * 2
    block = pl.BlockSpec((tile, width), lambda t, me: (t, 0))
    return (lambda t, me: t), [block], [jax.ShapeDtypeStruct((tiles * tile, width), bf16)]


def feed_forward(normed, cot, mlp, axis, first, number, seqs, own):
    tokens, width = normed.shape
    depth, packed, ff_cols = mlp.shape
    shard = width // depth
    paired = lax.axis_size(axis) == 8
    tile = 512
    tiles = tokens // seqs // tile
    at, specs, shapes = pair_specs(paired, tile, tiles, width)
    blocks = width // ff_cols
    me = lax.axis_index(axis).reshape(1)

    def kernel(me, normed_ref, cot_ref, mlp_ref, inner_ref, grads_ref, *refs):
        outs, (gate_up, down, sems) = refs[:-3], refs[-3:]

        @pl.when((pl.program_id(0) == 0) & (pl.program_id(1) == 0))
        def _():
            copies = []
            for z in range(depth):
                for part in range(2):
                    copies.append(
                        (
                            mlp_ref.at[z, pl.ds(part * shard, shard)],
                            gate_up.at[pl.ds(z * shard, shard), pl.ds(part * ff_cols, ff_cols)],
                        )
                    )
                for k in range(blocks):
                    copies.append(
                        (
                            mlp_ref.at[z, pl.ds(2 * shard + k * own, own)],
                            down.at[pl.ds(z * own, own), pl.ds(k * ff_cols, ff_cols)],
                        )
                    )
            copy_all(copies, sems)

        both = dot(normed_ref[...], gate_up[...])
        grad_inner = dot_t(cot_ref[...], down[...])
        gate, up = both[:, :ff_cols], both[:, ff_cols:]
        sig = jax.nn.sigmoid(gate)
        silu = gate * sig
        inner = (silu * up).astype(bf16)
        inner_ref[...] = inner
        grads_ref[:, :ff_cols] = (grad_inner * up * sig * (1.0 + gate * (1.0 - sig))).astype(bf16)
        grads_ref[:, ff_cols:] = (grad_inner * silu).astype(bf16)
        back = dot_t(grads_ref[...], gate_up[...])
        result = dot(inner, down[...])
        each_seq = len(outs) // number
        for q in range(number):

            @pl.when(pl.program_id(0) == q)
            def _():
                own_outs = outs[q * each_seq : (q + 1) * each_seq]
                if paired:
                    split_pair(back, own_outs[0], own_outs[1], me[0])
                    split_pair(result, own_outs[2], own_outs[3], me[0])
                else:
                    own_outs[0][...] = back.astype(bf16)
                    own_outs[1][...] = result.astype(bf16)

    rows = pl.BlockSpec((tile, width), lambda q, t, me: ((first + q) * tiles + at(t, me), 0))
    length = tokens // seqs

    def own_rows(cols):
        return pl.BlockSpec((tile, cols), lambda q, t, me: (q * tiles + at(t, me), 0))

    def for_seq(spec, s):
        def index(q, t, me):
            return spec.index_map(jnp.where(q == s, t, jnp.where(q < s, 0, tiles - 1)), me)

        return pl.BlockSpec(spec.block_shape, index)

    return pl.pallas_call(
        kernel,
        grid_spec=pltpu.PrefetchScalarGridSpec(
            num_scalar_prefetch=1,
            grid=(number, tiles),
            in_specs=[rows, rows, ANY],
            out_specs=[own_rows(ff_cols), own_rows(2 * ff_cols)]
            + [for_seq(spec, s) for s in range(number) for spec in specs * 2],
            scratch_shapes=[
                pltpu.VMEM((width, 2 * ff_cols), bf16),
                pltpu.VMEM((ff_cols, width), bf16),
                pltpu.SemaphoreType.DMA((depth * (2 + blocks),)),
            ],
        ),
        out_shape=[
            jax.ShapeDtypeStruct((number * length, ff_cols), bf16),
            jax.ShapeDtypeStruct((number * length, 2 * ff_cols), bf16),
        ]
        + shapes * 2 * number,
        compiler_params=LARGE,
        cost_estimate=takes(17 * number),
    )(me, normed, cot, mlp)


def project_back(grads, raw, pack, width, axis, seqs):
    cols, tokens = grads[0].shape
    depth, wide = pack.shape[0], pack.shape[2]
    shard, heads = width // depth, cols // HEAD_DIM
    tile = 512
    tiles = tokens // seqs // tile
    at, specs, shapes = pair_specs(True, tile, tiles, width)
    me = lax.axis_index(axis).reshape(1)

    def kernel(me, gq, gk, gv, raw, pack_ref, *refs):
        outs, (weights, small, turned, sems) = refs[:-4], refs[-4:]

        @pl.when((pl.program_id(0) == 0) & (pl.program_id(1) == 0))
        def _():
            copies = []
            for z in range(depth):
                copies.append((pack_ref.at[z, pl.ds(0, shard), pl.ds(0, 5 * 128)], rows_at(weights, z * shard, shard)))
                copies.append((pack_ref.at[z, pl.ds(shard, 16)], small.at[z]))
            copy_all(copies, sems)
            for z in range(depth):
                forget = jnp.concatenate(
                    [small[z, 2 : 2 + heads, :shard].astype(f32), jnp.zeros((EXTRA - heads, shard), f32)], axis=0
                )
                weights[z * shard : (z + 1) * shard, 3 * cols :] = forget.T.astype(bf16)

        for i, part in enumerate((gq, gk, gv)):
            turned[i * cols : (i + 1) * cols, :] = part[...]
        turned[3 * cols : 3 * cols + 16, :] = raw[...].astype(bf16)
        turned[3 * cols + 16 :, :] = jnp.zeros((EXTRA - 16, tile), bf16)
        back = dot_t(turned[...].T, weights[...])
        for s in range(seqs):

            @pl.when(pl.program_id(0) == s)
            def _():
                split_pair(back, outs[2 * s], outs[2 * s + 1], me[0])

    def seq_block(s):
        return pl.BlockSpec(
            (2, tile // 4, width), lambda q, t, me: (jnp.where(q == s, t, jnp.where(q < s, 0, tiles - 1)), 0, 0)
        )

    def columns(rows):
        return pl.BlockSpec((rows, tile), lambda s, t, me: (0, s * tiles + at(t, me)))

    return pl.pallas_call(
        kernel,
        grid_spec=pltpu.PrefetchScalarGridSpec(
            num_scalar_prefetch=1,
            grid=(seqs, tiles),
            in_specs=[columns(cols)] * 3 + [columns(16), ANY],
            out_specs=[seq_block(s) for s in range(seqs) for _ in range(2)],
            scratch_shapes=[
                pltpu.VMEM((width, 3 * cols + EXTRA), bf16),
                pltpu.VMEM((depth, 16, wide), bf16),
                pltpu.VMEM((3 * cols + EXTRA, tile), bf16),
                pltpu.SemaphoreType.DMA((2 * depth,)),
            ],
        ),
        out_shape=shapes * seqs,
        compiler_params=LARGE,
        cost_estimate=takes(11.0),
    )(me, *grads, raw, pack)


def attention_grads(grads, raw, normed, branch, mixed, gain_row, pack, axis, seqs, depth, heads, each_level):
    cols, tokens = grads[0].shape
    width = normed.shape[1]
    shard = width // depth
    count, own_out, piece = branch.shape
    wide = pack.shape[2]
    me = lax.axis_index(axis).reshape(1)
    part = piece // seqs

    def kernel(me, gq, gk, gv, raw, normed_ref, branch_ref, mixed_ref, gain_ref, pack_ref, small_ref, out, turned, branches):
        z = pl.program_id(0)

        @pl.when(z == 0)
        def _():
            for i, g in enumerate((gq, gk, gv)):
                turned[i * cols : (i + 1) * cols, :] = g[...]
            turned[3 * cols :, :] = raw[...].astype(bf16)
            for dev in range(count):
                for s in range(seqs):
                    to = (s * count + dev) * part
                    branches[:, to : to + part] = branch_ref[dev, :, s * part : (s + 1) * part]

        grad = dot(turned[...], normed_ref[...])
        forget = grad[3 * cols :]
        columns = grad[: 3 * cols].T
        out[0, :shard, : 3 * cols] = columns.astype(bf16)
        out[0, :shard, 3 * cols :] = dot_t(mixed_ref[...], branches[...]).astype(bf16)
        by_row = jnp.sum(columns * pack_ref[0, :, : 3 * cols].astype(f32), axis=1, keepdims=True)
        by_row = jnp.broadcast_to(by_row, (shard, 8)).T[:1]
        small = small_ref[0, :, :shard].astype(f32)
        by_row = by_row + jnp.sum(forget[:heads] * small[2 : 2 + heads], axis=0, keepdims=True)
        row = lax.broadcasted_iota(jnp.int32, (16, shard), 0)
        lane = lax.broadcasted_iota(jnp.int32, (16, shard), 1)
        more = jnp.where(row == heads, gain_ref[...], jnp.where(row == heads + 2, by_row / small[:1], 0.0))
        sums = jnp.sum(raw[...], axis=1, keepdims=True)
        for h in range(heads):
            head = me[0] * heads + h
            at = head // each_level * shard + head % each_level - z * shard
            more = more + jnp.where((row == heads + 1) & (lane == at), sums[h : h + 1, :], 0.0)
        out[0, shard : shard + 16, :shard] = jnp.where(row < heads, forget, more).astype(bf16)
        out[0, shard : shard + 16, shard:] = jnp.zeros((16, wide - shard), bf16)
        out[0, shard + 16 :, :] = jnp.zeros((16, wide), bf16)

    def whole(*shape):
        return pl.BlockSpec(shape, lambda z, me: (0,) * len(shape))

    return pl.pallas_call(
        kernel,
        grid_spec=pltpu.PrefetchScalarGridSpec(
            num_scalar_prefetch=1,
            grid=(depth,),
            in_specs=[whole(cols, tokens)] * 3
            + [
                whole(16, tokens),
                pl.BlockSpec((tokens, shard), lambda z, me: (0, z)),
                whole(count, own_out, piece),
                pl.BlockSpec((shard, tokens), lambda z, me: (z, 0)),
                pl.BlockSpec((1, shard), lambda z, me: (0, z)),
                pl.BlockSpec((1, shard, wide), lambda z, me: (z, 0, 0)),
                pl.BlockSpec((1, 16, wide), lambda z, me: (z, shard // 16, 0)),
            ],
            out_specs=pl.BlockSpec((1, shard + 32, wide), lambda z, me: (z, 0, 0)),
            scratch_shapes=[pltpu.VMEM((3 * cols + 16, tokens), bf16), pltpu.VMEM((own_out, tokens), bf16)],
        ),
        out_shape=jax.ShapeDtypeStruct((depth, shard + 32, wide), bf16),
        compiler_params=LARGE,
        cost_estimate=takes(12.0),
    )(me, *grads, raw, normed, branch, mixed, gain_row, pack, pack)


def out_turned(pack, cols, shard):
    depth, rows, wide = pack.shape

    def kernel(pack_ref, out):
        out[...] = pack_ref[0, :, 3 * cols :].T

    return pl.pallas_call(
        kernel,
        grid=(depth,),
        in_specs=[pl.BlockSpec((1, shard, wide), lambda z: (z, 0, 0))],
        out_specs=pl.BlockSpec((cols, shard), lambda z: (0, z)),
        out_shape=jax.ShapeDtypeStruct((cols, depth * shard), bf16),
        compiler_params=SMALL,
        cost_estimate=takes(2),
    )(pack)


def own_kernel(me, gate, up, down, out):
    rows, own = gate.shape[0], down.shape[0]
    out[:rows, :] = gate[...]
    out[rows : 2 * rows, :] = up[...]
    for k in range(down.shape[1] // (128 * pl.num_programs(0))):
        at = (k * pl.num_programs(0) + pl.program_id(0)) * 128
        out[2 * rows + k * own : 2 * rows + (k + 1) * own, :] = down[:, pl.ds(pl.multiple_of(at, 128), 128)]


def own_mlp(w_gate, w_up, w_down, depth, count, me):
    shard, ff = w_gate.shape
    own = w_down.shape[0] // count
    width = w_down.shape[1]
    ff_cols = depth * own
    if own == 128:
        strip = pl.BlockSpec((shard, 128), lambda z, me: (0, z * count + me[0]))
        total = 2 * shard + own * width // ff_cols
        return pl.pallas_call(
            own_kernel,
            grid_spec=pltpu.PrefetchScalarGridSpec(
                num_scalar_prefetch=1,
                grid=(depth,),
                in_specs=[strip, strip, pl.BlockSpec((own, width), lambda z, me: (me[0], 0))],
                out_specs=pl.BlockSpec((total, 128), lambda z, me: (0, z)),
            ),
            out_shape=jax.ShapeDtypeStruct((total, ff_cols), bf16),
            cost_estimate=takes(4.0),
        )(me.reshape(1), w_gate, w_up, w_down)

    def ff_columns(w):
        w = w.reshape(shard, depth, count, own)
        return lax.dynamic_index_in_dim(w, me, 2, keepdims=False).reshape(shard, ff_cols)

    down = lax.dynamic_slice_in_dim(w_down, me * own, own, 0)
    return jnp.concatenate([ff_columns(w_gate), ff_columns(w_up), stack_columns(down, ff_cols)], axis=0)


def contract(a, b, da, db):
    return lax.dot_general(a, b, (((da,), (db,)), ((), ())), preferred_element_type=f32)


def stack_columns(a, width):
    return jnp.concatenate([a[:, i : i + width] for i in range(0, a.shape[1], width)], axis=0)


def to_shards(grad):
    return lax.psum_scatter(grad, "fsdp", scatter_dimension=0, tiled=True)


def local_eight(
    inputs,
    gain_attn,
    w_query,
    w_key,
    w_value,
    w_forget,
    forget_bias,
    w_out,
    gain_mlp,
    w_gate,
    w_up,
    w_down,
    cotangent,
):
    axis = "ctx"
    count, me = lax.axis_size(axis), lax.axis_index(axis)
    depth, level = lax.axis_size("fsdp"), lax.axis_index("fsdp")
    seqs, rows, width = inputs.shape
    tokens = seqs * count * rows
    shard = width // depth
    heads = HEADS // count
    cols = heads * HEAD_DIM
    ff_own = w_down.shape[0] // count
    ff_cols = depth * ff_own
    own_out = width // count
    flat_in, flat_cot = inputs.reshape(seqs * rows, width), cotangent.reshape(seqs * rows, width)

    def token_slots(dev):
        return [(s * rows, rows, (s * count + dev) * rows) for s in range(seqs)]

    x_state = gather_start(flat_in, axis)
    own = own_attention(
        w_query, w_key, w_value, w_forget, forget_bias, w_out, (gain_attn, gain_mlp), heads, me, level
    )
    pack = lax.all_gather(own, "fsdp", axis=0)
    x_far = gather_far(x_state, axis)
    mlp = lax.all_gather(own_mlp(after(w_gate, x_far[3:]), w_up, w_down, depth, count, me), "fsdp", axis=0)
    g_state = gather_start(after(flat_cot, x_far[3:]), axis)
    x_pieces = gather_core_once(x_far, axis)
    pack = after(pack, g_state[1:])
    g_state = gather_far(g_state, axis)
    out_state = gather_start(out_turned(pack, cols, shard), axis)
    gains = pack[:, shard : shard + 2, :shard].astype(f32)
    gain_one, gain_two = gains[:, 0].reshape(width), gains[:, 1].reshape(width)

    x_all, normed, qkv, gate_raw = norm_project(x_pieces, pack, axis, seqs, cols)
    attn, mixed, totals, decay = attend(qkv, gate_raw, seqs, heads)
    mixed, g_state, out_state = lax.optimization_barrier((mixed, g_state, out_state))
    out_state = gather_far(out_state, axis)
    mixed_state = gather_start(mixed, axis)
    g_pieces = gather_core_once(g_state, axis)
    g_all = place(g_pieces, axis, tokens, token_slots)
    out_full = place(gather_core_once(out_state, axis), axis, width, lambda dev: [(0, own_out, dev * own_out)])
    mixed_state = gather_far(after(mixed_state, (g_all, out_full)), axis)
    mixed_pieces = gather_core(mixed_state, axis)
    mixed_all = place(mixed_pieces, axis, width, lambda dev: [(0, cols, dev * cols)])
    normed_two, hidden_own = hidden_norm(x_all, mixed_all, out_full, gain_two, seqs, rows, axis, True)

    inner, gate_up_grads, *sides = feed_forward(normed_two, g_all, mlp, axis, 0, seqs, seqs, ff_own)
    sides = [sides[4 * s : 4 * s + 4] for s in range(seqs)]
    back = Sums([side[:2] for side in sides], axis)
    grad_down = back.hold(contract(inner, g_all, 0, 0).astype(bf16))
    back.first()
    normed_two = back.hold(normed_two)
    back.send_first()
    result = Sums([after(side[2:], normed_two) for side in sides], axis)
    grad_gate_up = result.hold(contract(normed_two, gate_up_grads, 0, 0).astype(bf16))
    result.first()
    grad_gate_up, result.moving = back.hold((grad_gate_up, result.moving))
    back.second()
    result.moving = back.hold(result.moving)
    back.send_second()
    result.send_first()
    back = back.result()
    grad_down, grad_gate_up = to_shards(grad_down), to_shards(grad_gate_up)

    grad_from_norm, grad_gain_two = norm_pull(hidden_own, gain_two, back)
    grad_hidden = flat_cot.astype(f32) + grad_from_norm
    branch = grad_hidden.astype(bf16)
    grad_mixed = contract(out_full, branch, 0, 1).astype(bf16).reshape(count, cols, seqs * rows)
    branch = after(branch, grad_mixed).T.reshape(count, own_out, seqs * rows)
    grad_mixed = lax.all_to_all(grad_mixed, axis, 0, 0, tiled=True)
    grad_mixed, grad_down, branch = result.hold((grad_mixed, grad_down, branch))
    result.second()
    grad_mixed = result.hold(grad_mixed)
    result.send_second()
    branch = lax.all_to_all(branch, axis, 0, 0, tiled=True)
    down_state = gather_start(grad_down, axis)
    gq, gk, gv, grad_raw = attend_pull(qkv, decay, grad_mixed, attn, totals, gate_raw, seqs, heads)

    down_state, branch, grad_gate_up, grad_raw = result.hold((down_state, branch, grad_gate_up, grad_raw))
    gate_up_state = gather_start(grad_gate_up, axis)
    down_state = gather_far(down_state, axis)
    grads = (gq, gk, gv)
    grad_pack = attention_grads(
        grads, grad_raw, normed, branch, mixed_all, grad_gain_two[None], pack, axis, seqs, depth, heads, HEADS // depth
    )
    grad_raw, down_state, gate_up_state, _ = lax.optimization_barrier((grad_raw, down_state, gate_up_state, grad_pack))
    gate_up_state = gather_far(gate_up_state, axis)
    down_pieces = gather_core(down_state, axis)
    pairs = project_back(grads, grad_raw, pack, width, axis, seqs)
    grad_pack = to_shards(grad_pack.reshape(-1, 4 * cols))
    pairs, gate_up_state, down_pieces = held(pairs, gate_up_state, down_pieces)
    grad_normed = Sums([pairs[2 * s : 2 * s + 2] for s in range(seqs)], axis)
    grad_normed.first()
    gate_up_state = result.hold(grad_normed.hold(gate_up_state))
    grad_normed.send_first()
    gate_up_pieces = gather_core(gate_up_state, axis)
    grad_down = place_wide(down_pieces, axis)
    grad_gate, grad_up = place_columns(gate_up_pieces, axis, depth, 2)
    grad_pack, _ = grad_normed.hold((grad_pack, (grad_down, grad_gate)))
    grad_normed.second()
    grad_normed.send_second()
    pack_state = gather_start(grad_pack, axis)
    pack_state = grad_normed.hold(pack_state)
    pack_state = gather_far(pack_state, axis)
    grad_in, _ = norm_pull(flat_in.astype(f32), gain_one, grad_normed.result())
    input_grad = (grad_hidden + grad_in).reshape(seqs, rows, width)
    output = (hidden_own + result.result()).astype(bf16).reshape(seqs, rows, width)
    pack_pieces = gather_core(after(pack_state, (input_grad, output)), axis)
    grad_query, grad_key, grad_value, grad_out, grad_forget, grad_gain_one, grad_gain_two, grad_bias = place_heads(
        pack_pieces, axis, shard, cols, heads, forget_bias.shape[0]
    )
    return (
        output,
        input_grad,
        grad_gain_one,
        grad_query,
        grad_key,
        grad_value,
        grad_forget,
        grad_bias,
        grad_out,
        grad_gain_two,
        grad_gate,
        grad_up,
        grad_down,
    )


def local_any(
    inputs,
    gain_attn,
    w_query,
    w_key,
    w_value,
    w_forget,
    forget_bias,
    w_out,
    gain_mlp,
    w_gate,
    w_up,
    w_down,
    cotangent,
):
    axis = "ctx"
    count, me = lax.axis_size(axis), lax.axis_index(axis)
    depth, level = lax.axis_size("fsdp"), lax.axis_index("fsdp")
    seqs, rows, width = inputs.shape
    tokens = seqs * count * rows
    shard = width // depth
    heads = -(-HEADS // count)
    cols = heads * HEAD_DIM
    ff_own = w_down.shape[0] // count
    ff_cols = depth * ff_own
    out_rows, own_out = shard // count, width // count
    flat_in, flat_cot = inputs.reshape(seqs * rows, width), cotangent.reshape(seqs * rows, width)

    def own_columns(w, each_head):
        w = jnp.pad(w, ((0, 0), (0, count * heads * each_head - w.shape[1])))
        return lax.dynamic_slice_in_dim(w, me * heads * each_head, heads * each_head, 1)

    extra = [own_columns(w_forget, 1), gain_attn[:, None], gain_mlp[:, None]]
    extra += [jnp.pad(forget_bias, (0, shard - forget_bias.shape[0]))[:, None]]
    extra += [jnp.zeros((shard, EXTRA - heads - 3), bf16)]
    pack = [own_columns(w, HEAD_DIM) for w in (w_query, w_key, w_value)] + extra
    pack = lax.all_gather(jnp.concatenate(pack, axis=1), "fsdp", axis=0, tiled=True)
    extra = pack[:, 3 * cols :]
    gain_one = extra[:, heads].astype(f32)
    gain_two = extra[:, heads + 1].astype(f32)
    biases = extra[:, heads + 2].reshape(depth, shard)[:, : forget_bias.shape[0]].reshape(-1)
    biases = jnp.pad(biases, (0, count * heads - HEADS))
    bias = lax.dynamic_slice_in_dim(biases, me * heads, heads).astype(f32)
    out_own = lax.all_gather(lax.dynamic_slice_in_dim(w_out, me * out_rows, out_rows, 0), "fsdp", axis=0)
    out_full = lax.all_gather(out_own, axis, axis=1).reshape(width, width)
    mlp = lax.all_gather(own_mlp(w_gate, w_up, w_down, depth, count, me), "fsdp", axis=0)

    x_all = lax.all_gather(inputs, axis, axis=1, tiled=True).reshape(tokens, width)
    x_wide = x_all.astype(f32)
    normed = (x_wide * inverse_rms(x_wide) * gain_one).astype(bf16)
    g_all = lax.all_gather(after(cotangent, normed), axis, axis=1, tiled=True).reshape(tokens, width)
    qkv = contract(pack[:, : 3 * cols], normed, 0, 1).astype(bf16)
    gate_raw = contract(extra, normed, 0, 1)[:heads] + bias[:, None]
    gate_raw = jnp.pad(gate_raw, ((0, -heads % 16), (0, 0)))
    attn, mixed, totals, decay = attend(qkv, gate_raw, seqs, heads)
    mixed_all = lax.all_gather(mixed, axis, axis=0, tiled=True)[:width]
    normed_two, hidden_own = hidden_norm(x_all, mixed_all, out_full, gain_two, seqs, rows, axis, False)

    def summed(part):
        return lax.psum_scatter(part.reshape(count, rows, width), axis, scatter_dimension=0).astype(f32)

    sides, sums = [], []
    for s in range(seqs):
        side = feed_forward(normed_two, g_all, mlp, axis, s, 1, seqs, ff_own)
        sides.append(side[:2])
        sums.append([summed(side[2]), summed(side[3])])
        normed_two = after(normed_two, sums[s])
    back, result = (jnp.concatenate(parts, axis=0) for parts in zip(*sums))
    inner = jnp.concatenate([side[0] for side in sides], axis=0)
    gate_up_grads = jnp.concatenate([side[1] for side in sides], axis=0)
    grad_down = to_shards(contract(inner, g_all, 0, 0).astype(bf16))
    grad_gate_up = to_shards(contract(normed_two, gate_up_grads, 0, 0).astype(bf16))
    output = (hidden_own + result).astype(bf16)

    grad_from_norm, grad_gain_two = norm_pull(hidden_own, gain_two, back)
    grad_hidden = flat_cot.astype(f32) + grad_from_norm
    branch = grad_hidden.astype(bf16)
    grad_mixed = contract(out_full, branch, 1, 1).astype(bf16)
    grad_mixed = jnp.pad(grad_mixed, ((0, count * cols - width), (0, 0)))
    grad_mixed = lax.all_to_all(grad_mixed.reshape(count, cols, seqs * rows), axis, 0, 0, tiled=True)
    branch = lax.all_to_all(branch.T.reshape(count, own_out, seqs * rows), axis, 0, 0, tiled=True)
    branch = branch.reshape(count, own_out, seqs, rows).transpose(1, 2, 0, 3).reshape(own_out, tokens)
    grad_out = contract(branch, mixed_all, 1, 1)
    gq, gk, gv, grad_raw = attend_pull(qkv, decay, grad_mixed, attn, totals, gate_raw, seqs, heads)
    grad_raw = jnp.pad(grad_raw[:heads].astype(bf16), ((0, EXTRA - heads), (0, 0)))
    grads = jnp.concatenate([gq, gk, gv, grad_raw], axis=0)
    grad_normed = contract(grads, pack, 0, 1).astype(bf16).reshape(seqs, count * rows, width)
    grad_normed = jnp.concatenate([summed(part) for part in grad_normed], axis=0)

    grad_pack = contract(grads, normed, 1, 0)
    head_at = me * heads + jnp.arange(heads)
    bias_col = head_at // (HEADS // depth) * shard + head_at % (HEADS // depth)
    bias_sum = jnp.where(head_at < HEADS, jnp.sum(grad_raw[:heads].astype(f32), axis=1), 0.0)
    at_col = jnp.arange(width)[None, :] == bias_col[:, None]
    bias_row = jnp.sum(jnp.where(at_col, bias_sum[:, None], 0.0), axis=0, keepdims=True)
    tail = [grad_pack[3 * cols : 3 * cols + heads], grad_gain_two[None], bias_row]
    tail += [jnp.zeros((EXTRA - heads - 2, width), f32)]
    grad_pack = jnp.concatenate([grad_pack[: 3 * cols]] + tail + [grad_out], axis=0).astype(bf16)
    grad_pack = to_shards(grad_pack.reshape(-1, depth, shard).transpose(1, 0, 2).reshape(-1, shard))
    grad_pack = lax.all_gather(grad_pack, axis)
    out_at = 3 * cols + EXTRA

    def turned(start, size):
        return grad_pack[:, start : start + size].reshape(-1, shard)[:width].T.astype(f32)

    tail = grad_pack[:, 3 * cols : out_at].astype(f32)
    tail_sum = jnp.sum(tail[:, heads : heads + 2], axis=0)
    grad_down = lax.all_gather(grad_down, axis, axis=0, tiled=True).astype(f32)
    grad_gate_up = lax.all_gather(grad_gate_up.reshape(shard, 2, depth, ff_own), axis)
    grad_gate_up = grad_gate_up.transpose(2, 1, 3, 0, 4).reshape((2,) + w_gate.shape).astype(f32)
    grad_in, grad_gain_one = norm_pull(flat_in.astype(f32), gain_one, grad_normed)
    grad_gain_one = lax.psum(grad_gain_one, (axis, "fsdp"))
    return (
        output.reshape(seqs, rows, width),
        (grad_hidden + grad_in).reshape(seqs, rows, width),
        lax.dynamic_slice_in_dim(grad_gain_one, level * shard, shard),
        turned(0, cols),
        turned(cols, cols),
        turned(2 * cols, cols),
        tail[:, :heads].reshape(count * heads, shard)[:HEADS].T,
        tail_sum[1, : forget_bias.shape[0]],
        turned(out_at, own_out),
        tail_sum[0],
        grad_gate_up[0],
        grad_gate_up[1],
        grad_down,
    )


def solution(mesh):
    split, first, rest = P("fsdp", "ctx", None), P("fsdp"), P("fsdp", None)
    return jax.shard_map(
        local_eight if mesh.shape["ctx"] == 8 else local_any,
        mesh=mesh,
        in_specs=(split, first, rest, rest, rest, rest, first, rest, first, rest, rest, rest, split),
        out_specs=(split, split, first, rest, rest, rest, rest, first, rest, first, rest, rest, rest),
        check_vma=False,
    )
```
